32 devices in a mesh: batch: 8 (over z, x), tower: 4 (over y, core).
Axes of the slice: x: 2, y: 2, z: 4, core: 2. Of those that a mesh axis runs over, the one named last changes fastest.
Arguments:
- convmaps: bfloat16 [4096, 2, 169, 256], P(('batch', 'tower')), may hold values from -8 to 8
- group: int32 [4096], P(('batch', 'tower')), may hold values from 0 to 1
- alpha1: bfloat16 [2, 2, 256], replicated, may hold values from 0.19921875 to 1
- weight: bfloat16 [9216, 8192], P('batch', 'tower'), may hold values from -0.0625 to 0.0625
- bias: bfloat16 [8192], P('tower'), may hold values from -3 to 3
- alpha2: bfloat16 [2, 8192], P(None, 'tower'), may hold values from 0.19921875 to 1
- cotangent: bfloat16 [4096, 8192], P('batch', 'tower'), may hold values from -6 to 6
Outputs:
- activations: bfloat16 [4096, 8192], P('batch', 'tower')
- input_grad: bfloat16 [4096, 2, 169, 256], P(('batch', 'tower'))
- weight_grad: float32 [9216, 8192], P('batch', 'tower')
- bias_grad: float32 [8192], P('tower')
- alpha1_grad: float32 [2, 2, 256], replicated
- alpha2_grad: float32 [2, 8192], P(None, 'tower')
The draws below stay inside these ranges and needn't reach their ends.
Inputs may be any that keep to these rules, and one draw needn't show every extreme that they name: `group`: 0 marks an image of a 227 input with a full 6 x 6 pool, 1 an image of a 195 input whose pool is 5 x 5 padded.
All inputs are finite; a program needn't handle non-finite values.
Results may differ from the reference program's by a relative error of at most 0.0055.
Values may be sent and summed in bfloat16 or wider, within the bound.
No kernel may reach another device: no remote copies, remote signals or barrier semaphores. Data moves between devices by JAX's collectives and lax.ppermute only.
A program may use at most 320 MiB of HBM per device.

```python
import jax
import jax.numpy as jnp
from jax import lax

CH = 256
FC = 4096
MAP = 169
FEAT = 9216
IMAGES = 4096
N_BATCH = 8


def plant(result, own_key, low, high):
    longest = result.shape.index(max(result.shape))
    spots = []
    for shift in (0, 1):
        where = [jax.random.randint(jax.random.fold_in(own_key, axis), (), 0, length) for axis, length in enumerate(result.shape)]
        where[longest] = (where[longest] + shift) % result.shape[longest]
        spots.append(tuple(where))
    return result.at[spots[0]].set(low).at[spots[1]].set(high)


def block_levels(own_key, dims, cuts, low, top_value):
    def one(dim, blocks):
        heights = jax.random.uniform(jax.random.fold_in(jax.random.fold_in(own_key, 6), dim), (blocks,), jnp.float32, low / len(cuts), top_value / len(cuts))
        return jnp.repeat(jnp.exp(heights), dims[dim] // blocks).reshape((-1,) + (1,) * (len(dims) - dim - 1))

    factor_of = one(*cuts[0])
    for cut in cuts[1:]:
        factor_of = factor_of * one(*cut)
    return factor_of


def normal_values(own_key, extent, deviation, reach, pieces=(), kind=jnp.bfloat16):
    array = jax.random.normal(own_key, extent, jnp.float32) * deviation
    if len(pieces) > 0:
        array = block_levels(own_key, extent, pieces, -0.22, 0.18) * array
    return jnp.clip(array, min=-reach, max=reach).astype(kind)


def setup_inputs(seed: int = 0) -> dict:
    streams_of = jax.random.split(jax.random.key(seed), 8)
    return {
        "convmaps": normal_values(streams_of[0], (IMAGES, 2, MAP, CH), 2.0, 8.0, ((0, 32),)),
        "group": plant(jax.random.randint(streams_of[1], (IMAGES,), 0, 2), jax.random.fold_in(streams_of[1], 1), 0, 1).astype(jnp.int32),
        "alpha1": jnp.clip(jax.random.uniform(streams_of[2], (2, 2, CH), jnp.float32, 0.19921875, 1.0), 0.19921875, 1.0).astype(jnp.bfloat16),
        "weight": normal_values(streams_of[3], (FEAT, 2 * FC), FEAT ** -0.5, 0.0625, ((0, 8), (1, 4))),
        "bias": normal_values(streams_of[4], (2 * FC,), 0.5, 3.0, ((0, 4),)),
        "alpha2": jnp.clip(0.19921875 + 0.80078125 * jax.random.uniform(streams_of[5], (2, 2 * FC), jnp.float32) ** block_levels(streams_of[5], (2, 2 * FC), ((1, 4),), -0.2, 0.2), 0.19921875, 1.0).astype(jnp.bfloat16),
        "cotangent": normal_values(streams_of[6], (IMAGES, 2 * FC), 1.0, 6.0, ((0, 8), (1, 4))),
    }


@jax.custom_vjp
def low(v):
    return lax.optimization_barrier(v.astype(jnp.bfloat16)).astype(jnp.float32)

@jax.custom_vjp
def low_back(v):
    return v

def low_keep(v):
    return (low(v), None)

def low_pass(kept, grad):
    return (grad,)

def back_keep(v):
    return (v, None)

def back_low(kept, grad):
    return (low(grad),)
low.defvjp(low_keep, low_pass)
low_back.defvjp(back_keep, back_low)

def pool_table(dtype):
    pooled_pos = jnp.arange(36)[:, None]
    map_pos = jnp.arange(169)[None, :]
    prow = pooled_pos // 6
    pcol = pooled_pos % 6
    qrow = map_pos // 13
    qcol = map_pos % 13
    inside = (qrow >= 2 * prow) & (qrow <= 2 * prow + 2) & (qcol >= 2 * pcol) & (qcol <= 2 * pcol + 2)
    return jnp.where(inside, 1.0, 0.0).astype(dtype)

def keep_mask(group):
    place = jnp.arange(36)
    small = (place // 6 < 5) & (place % 6 < 5)
    return jnp.where((group == 0)[:, None] | small[None, :], 1.0, 0.0).astype(jnp.float32)

def forward(maps, keep, first, weight, bias, second):
    highest = lax.Precision.HIGHEST
    count = maps.shape[0]
    table = pool_table(jnp.float32)
    pooled = jnp.einsum('pq,nsqc->snpc', table, maps, precision=highest) * (1.0 / 9.0) * keep[None, :, :, None]
    mixed = low(jnp.einsum('asc,snpc->anpc', first, pooled, precision=highest)).reshape(2, count, FEAT)
    pre = jnp.einsum('snf,fsk->snk', mixed, weight.reshape(FEAT, 2, FC), precision=highest)
    pre = low_back(pre + bias.reshape(2, FC)[:, None, :])
    act = low(jax.nn.gelu(pre))
    out = jnp.einsum('sak,snk->nak', second.reshape(2, 2, FC), act, precision=highest)
    return out.reshape(count, 2 * FC)

def reference(convmaps, group, alpha1, weight, bias, alpha2, cotangent):
    per = IMAGES // N_BATCH
    maps = convmaps.reshape(N_BATCH, per, 2, MAP, CH)
    groups = group.reshape(N_BATCH, per)
    cots = cotangent.reshape(N_BATCH, per, 2 * FC)
    first = alpha1.astype(jnp.float32)
    wfull = weight.astype(jnp.float32)
    bfull = bias.astype(jnp.float32)
    second = alpha2.astype(jnp.float32)

    def step(carry, items):
        block_maps, block_group, block_cot = items
        keep = keep_mask(block_group)

        def local(mm, a1, ww, bb, a2):
            return forward(mm, keep, a1, ww, bb, a2)
        out, pull = jax.vjp(local, block_maps.astype(jnp.float32), first, wfull, bfull, second)
        grads = pull(block_cot.astype(jnp.float32))
        carry = tuple((c + g for c, g in zip(carry, grads[1:])))
        return (carry, (out.astype(jnp.bfloat16), grads[0].astype(jnp.bfloat16)))
    start = (jnp.zeros((2, 2, CH), jnp.float32), jnp.zeros((FEAT, 2 * FC), jnp.float32), jnp.zeros((2 * FC,), jnp.float32), jnp.zeros((2, 2 * FC), jnp.float32))
    sums, (outs, dmaps) = lax.scan(step, start, (maps, groups, cots))
    activations = outs.reshape(IMAGES, 2 * FC)
    input_grad = dmaps.reshape(IMAGES, 2, MAP, CH)
    return (activations, input_grad, sums[1], sums[2], sums[0], sums[3])
```

```python
import functools

import jax
import jax.numpy as jnp
from jax import lax
from jax.experimental import pallas as pl
from jax.experimental.pallas import tpu as pltpu
from jax.sharding import PartitionSpec as P

F32 = jnp.float32
BF16 = jnp.bfloat16
POOLED = 36
PITCH = 48
LANES = 128
VMEM_LIMIT = 56 * 1024 * 1024
CHUNKS = 4


def params():
    return pltpu.CompilerParams(vmem_limit_bytes=VMEM_LIMIT)


def flipped(value, axis, bit):
    pairs = [(source, source ^ bit) for source in range(lax.axis_size(axis))]
    return lax.ppermute(value, axis, pairs)


def x_swap(value):
    return flipped(value, "batch", 1)


def y_swap(value):
    return flipped(value, "tower", 2)


def c_swap(value):
    return flipped(value, "tower", 1)


def line(value, kind):
    steps = {
        "near": ((0, 1), (1, 0), (2, 3), (3, 2)),
        "middle": ((1, 2), (2, 1)),
        "outward": ((1, 0), (2, 3)),
        "inward": ((0, 1), (3, 2)),
    }[kind]
    pairs = [(2 * a + x, 2 * b + x) for a, b in steps for x in range(2)]
    return lax.ppermute(value, "batch", pairs)


def slab_groups():
    size = lax.axis_size("batch")
    return [list(range(x, size, 2)) for x in range(2)]


def is_line():
    return lax.axis_size("batch") == 8


def line_order(z):
    rows = jnp.array([[0, 1, 2, 3], [1, 0, 2, 3], [2, 3, 1, 0], [3, 2, 1, 0]])
    return rows[z]


def gather_rows(block):
    if not is_line():
        return [(lax.all_gather(block, "batch", axis=0, tiled=True, axis_index_groups=slab_groups()),)]
    near = line(block, "near")
    inner = line(block, "middle")
    passed = line(inner, "outward")
    outer = line(near, "middle")
    last = line(outer, "outward")
    return [(block,), (near,), (inner, passed), (outer, last)]


def scatter_rows(total):
    if not is_line():
        return lax.psum_scatter(total, "batch", scatter_dimension=0, tiled=True, axis_index_groups=slab_groups())
    own, near, inner, outer = jnp.split(total, 4, axis=0)
    from_end = line(outer.astype(BF16), "inward").astype(F32)
    crossed = line((outer + from_end).astype(BF16), "middle").astype(F32)
    from_end2 = line(inner.astype(BF16), "inward").astype(F32)
    mine = line((inner + from_end2).astype(BF16), "middle").astype(F32)
    last = line((near + crossed).astype(BF16), "near").astype(F32)
    return own + mine + last


def sum_slabs(value):
    if not is_line():
        return lax.psum(value, "batch", axis_index_groups=slab_groups())
    value = value + flipped(value, "batch", 2)
    return value + flipped(value, "batch", 4)


def sum_all(value):
    if not is_line():
        return lax.psum(value, ("batch", "tower"))
    value = value + c_swap(value)
    value = value + y_swap(value)
    value = value + x_swap(value)
    return sum_slabs(value)


def pool_table(order):
    map_pos = jnp.arange(169)[None, :]
    prow = (order // 6)[:, None]
    pcol = (order % 6)[:, None]
    qrow = map_pos // 13
    qcol = map_pos % 13
    inside = (
        (qrow >= 2 * prow) & (qrow <= 2 * prow + 2) & (qcol >= 2 * pcol) & (qcol <= 2 * pcol + 2)
    )
    small = (prow < 5) & (pcol < 5)
    table = jnp.stack([inside, inside & small]).astype(BF16)
    return jnp.pad(table, ((0, 0), (0, PITCH - POOLED), (0, 0)))


def pool_kernel(group, table, first, maps, own_out, other_out, pooled_out, own, other, pool0, pool1):
    count = maps.shape[0]
    base = pl.program_id(0) * count
    ch = maps.shape[3]

    def image(n, carry):
        window = table[group[base + n]]
        p0 = jnp.dot(window, maps[n, 0], preferred_element_type=F32) * (1.0 / 9.0)
        p1 = jnp.dot(window, maps[n, 1], preferred_element_type=F32) * (1.0 / 9.0)
        rows = pl.ds(pl.multiple_of(n * PITCH, PITCH), PITCH)
        mixed0 = first[0:1, :] * p0 + first[1:2, :] * p1
        mixed1 = first[2:3, :] * p0 + first[3:4, :] * p1
        for hold, value in ((pool0, p0), (pool1, p1), (own, mixed0), (other, mixed1)):
            for h in range(ch // LANES):
                hold[h, rows, :] = value[:, h * LANES : (h + 1) * LANES]
        return carry

    lax.fori_loop(0, count, image, 0, unroll=2)
    for p in range(POOLED):
        rows = pl.ds(p, count, stride=PITCH)
        for h in range(ch // LANES):
            lanes = slice(p * ch + h * LANES, p * ch + (h + 1) * LANES)
            own_out[:, lanes] = own[h, rows, :].astype(BF16)
            other_out[:, lanes] = other[h, rows, :].astype(BF16)
            pooled_out[0, :, lanes] = pool0[h, rows, :]
            pooled_out[1, :, lanes] = pool1[h, rows, :]


def pool(convmaps, group, table, first):
    count, _, places, ch = convmaps.shape
    nb = 16
    feats = POOLED * ch
    return pl.pallas_call(
        pool_kernel,
        grid_spec=pltpu.PrefetchScalarGridSpec(
            num_scalar_prefetch=1,
            grid=(count // nb,),
            in_specs=[
                pl.BlockSpec((2, PITCH, places), lambda i, g: (0, 0, 0)),
                pl.BlockSpec((4, ch), lambda i, g: (0, 0)),
                pl.BlockSpec((nb, 2, places, ch), lambda i, g: (i, 0, 0, 0)),
            ],
            out_specs=[
                pl.BlockSpec((nb, feats), lambda i, g: (i, 0)),
                pl.BlockSpec((nb, feats), lambda i, g: (i, 0)),
                pl.BlockSpec((2, nb, feats), lambda i, g: (0, i, 0)),
            ],
            scratch_shapes=[pltpu.VMEM((ch // LANES, nb * PITCH, LANES), F32)] * 4,
        ),
        out_shape=[
            jax.ShapeDtypeStruct((count, feats), BF16),
            jax.ShapeDtypeStruct((count, feats), BF16),
            jax.ShapeDtypeStruct((2, count, feats), F32),
        ],
        compiler_params=params(),
        cost_estimate=pl.CostEstimate(
            flops=2 * count * 2 * PITCH * places * ch, bytes_accessed=count * ch * 600, transcendentals=0
        ),
        name="pool",
    )(group, table, first, convmaps)


def first_grad_kernel(pooled, *refs):
    pieces = (len(refs) - 1) // 2
    out = refs[-1]
    ch = out.shape[2]

    @pl.when(pl.program_id(0) == 0)
    def _():
        out[...] = jnp.zeros_like(out)

    for a in range(2):
        sums = [0.0, 0.0]
        start = 0
        for ref in refs[a * pieces : (a + 1) * pieces]:
            for p in range(ref.shape[1] // ch):
                grad = ref[:, p * ch : (p + 1) * ch].astype(F32)
                lanes = slice(start + p * ch, start + (p + 1) * ch)
                for s in range(2):
                    sums[s] = sums[s] + grad * pooled[s, :, lanes]
            start += ref.shape[1]
        for s in range(2):
            out[2 * a + s] += sums[s]


def first_grad(pooled, own, other):
    count, feats = pooled.shape[1:]
    ch = feats // POOLED
    nb = 16
    specs = [pl.BlockSpec((nb, piece.shape[1]), lambda i: (i, 0)) for piece in own + other]
    sums = pl.pallas_call(
        first_grad_kernel,
        grid=(count // nb,),
        in_specs=[pl.BlockSpec((2, nb, feats), lambda i: (0, i, 0))] + specs,
        out_specs=pl.BlockSpec((4, nb, ch), lambda i: (0, 0, 0)),
        out_shape=jax.ShapeDtypeStruct((4, nb, ch), F32),
        compiler_params=params(),
        cost_estimate=pl.CostEstimate(
            flops=8 * count * feats, bytes_accessed=count * feats * 14, transcendentals=0
        ),
        name="first_grad",
    )(pooled, *own, *other)
    return jnp.sum(sums, axis=1)


def unpool_kernel(group, table, first, *refs):
    pieces = (len(refs) - 3) // 2
    out, own, other = refs[-3:]
    count = out.shape[0]
    base = pl.program_id(0) * count
    ch = out.shape[3]
    places = out.shape[2]

    @pl.when(pl.program_id(0) == 0)
    def _():
        own[...] = jnp.zeros_like(own)
        other[...] = jnp.zeros_like(other)

    for hold, parts in ((own, refs[:pieces]), (other, refs[pieces : 2 * pieces])):
        start = 0
        for ref in parts:
            for p in range(ref.shape[1] // ch):
                for h in range(ch // LANES):
                    lanes = slice(p * ch + h * LANES, p * ch + (h + 1) * LANES)
                    hold[h, pl.ds(start + p, count, stride=PITCH), :] = ref[:, lanes].astype(F32)
            start += ref.shape[1] // ch

    def image(n, carry):
        window = table[group[base + n]]
        rows = pl.ds(pl.multiple_of(n * PITCH, PITCH), PITCH)
        g0, g1 = (
            jnp.concatenate([hold[h, rows, :] for h in range(ch // LANES)], axis=1) for hold in (own, other)
        )
        for s in range(2):
            grad = (first[s : s + 1, :] * g0 + first[2 + s : 3 + s, :] * g1) * (1.0 / 9.0)
            high = grad.astype(BF16)
            low = (grad - high.astype(F32)).astype(BF16)
            both = jnp.concatenate([high, low], axis=0)
            spread = jnp.dot(window, both, preferred_element_type=F32)
            out[n, s] = spread[:places].astype(BF16)
        return carry

    lax.fori_loop(0, count, image, 0, unroll=2)


def unpool(own, other, group, table, first, places):
    count = own[0].shape[0]
    ch = first.shape[1]
    nb = 16
    specs = [pl.BlockSpec((nb, piece.shape[1]), lambda i, g: (i, 0)) for piece in own + other]
    spread = jnp.swapaxes(table, 1, 2)
    spread = jnp.pad(jnp.concatenate([spread, spread], axis=2), ((0, 0), (0, 176 - places), (0, 0)))
    return pl.pallas_call(
        unpool_kernel,
        grid_spec=pltpu.PrefetchScalarGridSpec(
            num_scalar_prefetch=1,
            grid=(count // nb,),
            in_specs=[
                pl.BlockSpec(spread.shape, lambda i, g: (0, 0, 0)),
                pl.BlockSpec((4, ch), lambda i, g: (0, 0)),
            ]
            + specs,
            out_specs=pl.BlockSpec((nb, 2, places, ch), lambda i, g: (i, 0, 0, 0)),
            scratch_shapes=[pltpu.VMEM((ch // LANES, nb * PITCH, LANES), F32)] * 2,
        ),
        out_shape=jax.ShapeDtypeStruct((count, 2, places, ch), BF16),
        compiler_params=params(),
        cost_estimate=pl.CostEstimate(
            flops=2 * count * 2 * 2 * PITCH * places * ch, bytes_accessed=count * ch * 700, transcendentals=0
        ),
        name="unpool",
    )(group, spread, first, *own, *other)


def tile_of(rows):
    return next(t for t in (1152, 768, 576, 512, 384, 256, 128) if rows % t == 0)


def forward_kernel(layout, tile, feats, vectors, cot_own, cot_other, *refs):
    terms = sum(layout)
    pieces = refs[:terms]
    act_out, dpre_out, sums_out, total, weight = refs[terms:]
    step = pl.program_id(0)
    per = pl.num_programs(0) // len(layout)
    at = 0
    for s, many in enumerate(layout):
        group = pieces[at : at + many]
        at += many

        @pl.when(step // per == s)
        def _(group=group):
            value = group[0][...]
            for extra in group[1:]:
                value = value + extra[...]
            weight[...] = value

    @pl.when(step == 0)
    def _():
        total[...] = jnp.zeros_like(total)

    total[...] += jnp.dot(feats[...], weight[...], preferred_element_type=F32)

    @pl.when(step == pl.num_programs(0) - 1)
    def _():
        bias, own_coef, other_coef = (vectors[i : i + 1, :] for i in range(3))
        c = 0.7978845608028654
        block = 64

        def rows_of(i, sums):
            rows = pl.ds(pl.multiple_of(i * block, block), block)
            x = total[rows, :] + bias
            x2 = x * x
            t = jnp.tanh(c * (x + 0.044715 * (x2 * x)))
            half = 0.5 * (1.0 + t)
            act = (x * half).astype(BF16)
            slope = half + (0.5 * c) * x * (1.0 - t * t) * (1.0 + (3.0 * 0.044715) * x2)
            k0 = cot_own[rows, :].astype(F32)
            k1 = cot_other[rows, :].astype(F32)
            dpre = ((own_coef * k0 + other_coef * k1) * slope).astype(BF16)
            act_out[rows, :] = act
            dpre_out[rows, :] = dpre
            actf = act.astype(F32)

            def fold(v):
                return jnp.sum(v.reshape(block // 8, 8, v.shape[1]), axis=0)

            return (
                sums[0] + fold(dpre.astype(F32)),
                sums[1] + fold(k0 * actf),
                sums[2] + fold(k1 * actf),
            )

        zero = jnp.zeros((8, total.shape[1]), F32)
        sums = lax.fori_loop(0, total.shape[0] // block, rows_of, (zero, zero, zero))
        for i in range(3):
            sums_out[i] = sums[i]


def forward(feats, pieces, vectors, cot_own, cot_other):
    rows, depth = feats.shape
    units = cot_own.shape[1]
    tile = tile_of(pieces[0][0].shape[0])
    per = pieces[0][0].shape[0] // tile
    steps = per * len(pieces)
    specs, terms = [], []
    for s, piece in enumerate(pieces):
        for term in piece:
            terms.append(term)
            specs.append(
                pl.BlockSpec((tile, units), lambda k, s=s: (jnp.clip(k - s * per, 0, per - 1), 0))
            )
    whole = pl.BlockSpec((rows, units), lambda k: (0, 0))
    return pl.pallas_call(
        functools.partial(forward_kernel, [len(p) for p in pieces], tile),
        grid=(steps,),
        in_specs=[
            pl.BlockSpec((rows, tile), lambda k: (0, k)),
            pl.BlockSpec((8, units), lambda k: (0, 0)),
            whole,
            whole,
        ]
        + specs,
        out_specs=[whole, whole, pl.BlockSpec((3, 8, units), lambda k: (0, 0, 0))],
        out_shape=[
            jax.ShapeDtypeStruct((rows, units), BF16),
            jax.ShapeDtypeStruct((rows, units), BF16),
            jax.ShapeDtypeStruct((3, 8, units), F32),
        ],
        scratch_shapes=[pltpu.VMEM((rows, units), F32), pltpu.VMEM((tile, units), BF16)],
        compiler_params=params(),
        cost_estimate=pl.CostEstimate(
            flops=2 * rows * depth * units, bytes_accessed=rows * depth * 2, transcendentals=rows * units
        ),
        name="forward",
    )(feats, vectors, cot_own, cot_other, *terms)


def back_kernel(layout, *refs):
    grads = refs[: len(layout)]
    keep_out, send_out, grad, weight = refs[-4:]
    units = grads[0].shape[1]
    at = len(layout)
    for j, many in enumerate(layout):
        value = refs[at][...]
        for extra in refs[at + 1 : at + many]:
            value = value + extra[...]
        weight[:, j * units : (j + 1) * units] = value
        at += many

    @pl.when(pl.program_id(0) == 0)
    def _():
        for j, ref in enumerate(grads):
            grad[:, j * units : (j + 1) * units] = ref[...]

    half = keep_out.shape[0]
    block = 256
    contract = (((1,), (1,)), ((), ()))

    def rows_of(i, carry):
        rows = pl.ds(pl.multiple_of(i * block, block), block)
        lower = pl.ds(pl.multiple_of(half + i * block, block), block)
        keep_out[rows, :] = lax.dot_general(grad[rows, :], weight[...], contract, preferred_element_type=F32)
        send_out[rows, :] = lax.dot_general(
            grad[lower, :], weight[...], contract, preferred_element_type=F32
        ).astype(BF16)
        return carry

    lax.fori_loop(0, half // block, rows_of, 0)


def back(grads, piece):
    rows, units = grads[0].shape
    depth = piece[0][0].shape[0]
    tile = tile_of(depth) if depth < 1152 else 384
    specs = [pl.BlockSpec((rows, units), lambda k: (0, 0)) for _ in grads]
    terms = [term for chunk in piece for term in chunk]
    specs += [pl.BlockSpec((tile, units), lambda k: (k, 0)) for _ in terms]
    half = pl.BlockSpec((rows // 2, tile), lambda k: (0, k))
    total = units * len(grads)
    return pl.pallas_call(
        functools.partial(back_kernel, [len(c) for c in piece]),
        grid=(depth // tile,),
        in_specs=specs,
        out_specs=[half, half],
        out_shape=[
            jax.ShapeDtypeStruct((rows // 2, depth), F32),
            jax.ShapeDtypeStruct((rows // 2, depth), BF16),
        ],
        scratch_shapes=[pltpu.VMEM((rows, total), BF16), pltpu.VMEM((tile, total), BF16)],
        compiler_params=params(),
        cost_estimate=pl.CostEstimate(
            flops=2 * rows * depth * total, bytes_accessed=rows * depth * 4, transcendentals=0
        ),
        name="back",
    )(*grads, *terms)


def either(flag, value, axis):
    return jnp.where(flag, jnp.flip(value, axis), value)


def shards(convmaps, group, alpha1, weight, bias, alpha2, cotangent):
    count, _, places, channels = convmaps.shape
    batch_id = lax.axis_index("batch")
    tower_id = lax.axis_index("tower")
    x = batch_id % 2
    z = batch_id // 2
    y = tower_id // 2
    core = tower_id % 2
    depth, width = weight.shape
    units = width // 2
    n = units // CHUNKS
    images = 8 * count
    mine, theirs = x * units, (1 - x) * units

    own_cols = lax.dynamic_slice_in_dim(weight, mine, units, 1)
    other_cols = lax.dynamic_slice_in_dim(weight, theirs, units, 1)
    chunks = []
    for j in range(CHUNKS):
        cols = slice(j * n, (j + 1) * n)
        a, b = own_cols[:, cols], x_swap(other_cols[:, cols])
        slab = jnp.where(x == 0, jnp.concatenate([a, b]), jnp.concatenate([b, a]))
        chunks.append(gather_rows(slab))

    cot = cotangent.reshape(2, 2, count, width)
    cot = either(core == 1, either(y == 1, cot, 0), 1).swapaxes(0, 1)
    cot_mine = lax.dynamic_slice_in_dim(cot, mine, units, 3)
    cot_theirs = lax.dynamic_slice_in_dim(cot, theirs, units, 3)
    cot_own = jnp.stack([cot_mine, x_swap(cot_theirs)], axis=1)
    cot_other = jnp.flip(y_swap(cot_own), 2).reshape(images, units)
    cot_own = cot_own.reshape(images, units)
    second = lax.dynamic_slice_in_dim(alpha2, mine, units, 1)
    own_coef = lax.dynamic_index_in_dim(second, y, 0, keepdims=True).astype(F32)
    cross = lax.dynamic_index_in_dim(second, 1 - y, 0, keepdims=True)
    cross_back = y_swap(cross).astype(F32)
    cross = cross.astype(F32)
    own_bias = lax.dynamic_slice_in_dim(bias, mine, units, 0)[None, :].astype(F32)
    vectors = jnp.concatenate([own_bias, own_coef, cross_back, jnp.zeros((5, units), F32)])

    order = jnp.arange(POOLED)
    if is_line():
        order = order.reshape(4, -1)[line_order(z)].reshape(-1)
    table = pool_table(order)
    first = alpha1.astype(F32)
    first = either(y == 1, first, 0).reshape(4, channels)
    kept, sent, pooled = pool(convmaps, group, table, first)
    arrived = y_swap(sent)
    blocks = [kept, arrived, x_swap(kept), x_swap(arrived)]
    blocks += [c_swap(block) for block in blocks]
    feats = jnp.concatenate(blocks)

    acts, grads, sums, stitched, crossed, owned = [], [], [], [], [], []
    weight_grad = jnp.zeros((depth, width), F32)
    for j in range(CHUNKS):
        cols = slice(j * n, (j + 1) * n)
        act, dpre, sums_j = forward(feats, chunks[j], vectors[:, cols], cot_own[:, cols], cot_other[:, cols])
        grads.append(dpre)
        sums.append(jnp.sum(sums_j, axis=1))
        total = lax.dot_general(feats, dpre, (((0,), (0,)), ((), ())), preferred_element_type=F32)
        slab = scatter_rows(total)
        stay = lax.dynamic_slice_in_dim(slab, x * depth, depth, 0)
        leave = lax.dynamic_slice_in_dim(slab, (1 - x) * depth, depth, 0)
        came = x_swap(leave.astype(BF16)).astype(F32)
        weight_grad = lax.dynamic_update_slice(weight_grad, stay, (0, mine + j * n))
        weight_grad = lax.dynamic_update_slice(weight_grad, came, (0, theirs + j * n))
        other_act = jnp.flip(y_swap(act).reshape(4, 2, count, n), 1).reshape(images, n)
        mix = (own_coef[:, cols] * act.astype(F32) + cross[:, cols] * other_act.astype(F32)).astype(BF16)
        mix = mix.reshape(2, 2, 2, count, n)
        stitched.append(mix[:, 0])
        crossed.append(x_swap(mix[:, 1]))

    left = jnp.concatenate(stitched, axis=3)
    right = jnp.concatenate(crossed, axis=3)
    rows = jnp.where(x == 0, jnp.concatenate([left, right], 3), jnp.concatenate([right, left], 3))
    rows = either(y == 1, either(core == 1, rows, 0), 1).swapaxes(0, 1)
    activations = rows.reshape(4 * count, width)

    sums = sum_slabs(jnp.concatenate(sums, axis=1))
    far = x_swap(sums)
    sums = jnp.where(x == 0, jnp.concatenate([sums, far], 1), jnp.concatenate([far, sums], 1))
    bias_grad = sums[0]
    other_second = y_swap(sums[2])
    alpha2_grad = either(y == 1, jnp.stack([sums[1], other_second]), 0)

    own_parts, other_parts = [], []
    for s in range(len(chunks[0])):
        keep, send = back(grads, [chunk[s] for chunk in chunks])
        part = keep + c_swap(send).astype(F32)
        keep, send = part[: 2 * count], part[2 * count :]
        part = keep + x_swap(send.astype(BF16)).astype(F32)
        own_parts.append(part[:count])
        other_parts.append(y_swap(part[count:].astype(BF16)))
    partial = first_grad(pooled, own_parts, other_parts)
    partial = either(y == 1, partial.reshape(2, 2, channels), 0)
    alpha1_grad = sum_all(partial)
    input_grad = unpool(own_parts, other_parts, group, table, first, places)
    return (activations, input_grad, weight_grad, bias_grad, alpha1_grad, alpha2_grad)


def solution(mesh):
    in_specs = (
        P(("batch", "tower"), None, None, None),
        P(("batch", "tower")),
        P(),
        P("batch", "tower"),
        P("tower"),
        P(None, "tower"),
        P("batch", "tower"),
    )
    out_specs = (
        P("batch", "tower"),
        P(("batch", "tower"), None, None, None),
        P("batch", "tower"),
        P("tower"),
        P(),
        P(None, "tower"),
    )
    return jax.shard_map(shards, mesh=mesh, in_specs=in_specs, out_specs=out_specs, check_vma=False)
```

```python
import functools

import jax
import jax.numpy as jnp
from jax import lax
from jax.experimental import pallas as pl
from jax.experimental.pallas import tpu as pltpu
from jax.sharding import PartitionSpec as P

F32 = jnp.float32
BF16 = jnp.bfloat16
POOLED = 36
PITCH = 48
LANES = 128
VMEM_LIMIT = 56 * 1024 * 1024
SMALL = pl.CostEstimate(flops=1000, bytes_accessed=1000, transcendentals=0)
AHEAD = 3
IMAGE_BLOCK = 16
HALVES = 2
GROUPS = 2


def params():
    return pltpu.CompilerParams(vmem_limit_bytes=VMEM_LIMIT)


def flipped(value, axis, bit):
    pairs = [(source, source ^ bit) for source in range(lax.axis_size(axis))]
    return lax.ppermute(value, axis, pairs)


def x_swap(value):
    return flipped(value, "batch", 1)


def y_swap(value):
    return flipped(value, "tower", 2)


def c_swap(value):
    return flipped(value, "tower", 1)


def line(value, kind):
    steps = {
        "near": ((0, 1), (1, 0), (2, 3), (3, 2)),
        "middle": ((1, 2), (2, 1)),
        "outward": ((1, 0), (2, 3)),
        "inward": ((0, 1), (3, 2)),
    }[kind]
    pairs = [(2 * a + x, 2 * b + x) for a, b in steps for x in range(2)]
    return lax.ppermute(value, "batch", pairs)


def slab_groups():
    size = lax.axis_size("batch")
    return [list(range(x, size, 2)) for x in range(2)]


def after(value, *others):
    return lax.optimization_barrier((value, *others))[0]


class Order:
    def __init__(self):
        self.last = None

    def then(self, value):
        return value if self.last is None else after(value, self.last)

    def did(self, value):
        self.last = value
        return value


def is_line():
    return lax.axis_size("batch") == 8


def line_order(z):
    rows = jnp.array([[0, 1, 2, 3], [1, 0, 2, 3], [2, 3, 1, 0], [3, 2, 1, 0]])
    return rows[z]


def both_cores(value):
    size = lax.axis_size("tower")
    groups = [[t, t + 1] for t in range(0, size, 2)]
    return lax.all_gather(value, "tower", axis=0, tiled=True, axis_index_groups=groups)


def pool_table(order):
    map_pos = jnp.arange(169)[None, :]
    prow = (order // 6)[:, None]
    pcol = (order % 6)[:, None]
    qrow = map_pos // 13
    qcol = map_pos % 13
    inside = (
        (qrow >= 2 * prow) & (qrow <= 2 * prow + 2) & (qcol >= 2 * pcol) & (qcol <= 2 * pcol + 2)
    )
    small = (prow < 5) & (pcol < 5)
    table = jnp.stack([inside, inside & small]).astype(BF16)
    table = jnp.pad(table, ((0, 0), (0, PITCH - POOLED), (0, 0)))
    both = table[:, None, :, :, None] * jnp.eye(2, dtype=BF16)[None, :, None, None, :]
    return both.reshape(2, 2 * PITCH, 338)


def pool_kernel(start, group, table, first, maps, *refs):
    *feature_outs, pooled_out, own, other, pool0, pool1 = refs[-(2 * HALVES + 5) :]
    count, places, _, ch = maps.shape
    base = (start + pl.program_id(0)) * count

    def image(n, carry):
        window = table[group[base + n]]
        rows_in = maps[n].reshape(2 * places, ch)
        both = jnp.dot(window, rows_in, preferred_element_type=F32) * (1.0 / 9.0)
        p0, p1 = both[:PITCH], both[PITCH:]
        rows = pl.ds(pl.multiple_of(n * PITCH, PITCH), PITCH)
        mixed0 = first[0:1, :] * p0 + first[1:2, :] * p1
        mixed1 = first[2:3, :] * p0 + first[3:4, :] * p1
        for hold, value in ((pool0, p0), (pool1, p1), (own, mixed0), (other, mixed1)):
            for h in range(ch // LANES):
                hold[h, rows, :] = value[:, h * LANES : (h + 1) * LANES]
        return carry

    lax.fori_loop(0, count, image, 0, unroll=2)
    per = POOLED // HALVES
    for p in range(POOLED):
        rows = pl.ds(p, count, stride=PITCH)
        for h in range(ch // LANES):
            lanes = slice(p * ch + h * LANES, p * ch + (h + 1) * LANES)
            part = slice((p % per) * ch + h * LANES, (p % per) * ch + (h + 1) * LANES)
            feature_outs[p // per][:, part] = own[h, rows, :].astype(BF16)
            feature_outs[HALVES + p // per][:, part] = other[h, rows, :].astype(BF16)
            pooled_out[0, :, lanes] = pool0[h, rows, :]
            pooled_out[1, :, lanes] = pool1[h, rows, :]


def pool(convmaps, group, table, first, at, steps, before=()):
    count, _, places, ch = convmaps.shape
    nb = IMAGE_BLOCK
    feats = POOLED * ch
    features = [((count, feats // HALVES), BF16)] * (2 * HALVES)
    return pl.pallas_call(
        functools.partial(pool_kernel, at),
        grid_spec=pltpu.PrefetchScalarGridSpec(
            num_scalar_prefetch=1,
            grid=(steps,),
            in_specs=[
                pl.BlockSpec(table.shape, lambda i, g: (0, 0, 0)),
                pl.BlockSpec((4, ch), lambda i, g: (0, 0)),
                pl.BlockSpec((nb, places, 2, ch), lambda i, g: (at + i, 0, 0, 0)),
            ]
            + [pl.BlockSpec(memory_space=pl.ANY)] * len(before),
            out_specs=[pl.BlockSpec((nb, feats // HALVES), lambda i, g: (at + i, 0))] * (2 * HALVES)
            + [pl.BlockSpec((2, nb, feats), lambda i, g: (0, at + i, 0))],
            scratch_shapes=[pltpu.VMEM((ch // LANES, nb * PITCH, LANES), F32)] * 4,
        ),
        out_shape=[jax.ShapeDtypeStruct(*f) for f in features]
        + [jax.ShapeDtypeStruct((2, count, feats), F32)],
        input_output_aliases={4 + i: i for i in range(len(before))},
        compiler_params=params(),
        cost_estimate=SMALL,
        name="pool",
    )(group, table, first, jnp.swapaxes(convmaps, 1, 2), *before)


def first_grad_kernel(begin, pooled, *refs):
    pieces = (len(refs) - 1) // 2
    out = refs[-1]
    ch = out.shape[2]

    @pl.when(pl.program_id(0) == 0)
    def _():
        out[...] = jnp.zeros_like(out)

    for a in range(2):
        sums = [0.0, 0.0]
        start = begin
        for ref in refs[a * pieces : (a + 1) * pieces]:
            for p in range(ref.shape[1] // ch):
                grad = ref[:, p * ch : (p + 1) * ch].astype(F32)
                lanes = slice(start + p * ch, start + (p + 1) * ch)
                for s in range(2):
                    sums[s] = sums[s] + grad * pooled[s, :, lanes]
            start += ref.shape[1]
        for s in range(2):
            out[2 * a + s] += sums[s]


def first_grad(pooled, own, other, begin):
    count, feats = pooled.shape[1:]
    ch = feats // POOLED
    nb = 16
    specs = [pl.BlockSpec((nb, piece.shape[1]), lambda i: (i, 0)) for piece in own + other]
    sums = pl.pallas_call(
        functools.partial(first_grad_kernel, begin),
        grid=(count // nb,),
        in_specs=[pl.BlockSpec((2, nb, feats), lambda i: (0, i, 0))] + specs,
        out_specs=pl.BlockSpec((4, nb, ch), lambda i: (0, 0, 0)),
        out_shape=jax.ShapeDtypeStruct((4, nb, ch), F32),
        compiler_params=params(),
        cost_estimate=SMALL,
        name="first_grad",
    )(pooled, *own, *other)
    return jnp.sum(sums, axis=1)


def unpool_kernel(start, pieces, group, table, first, *refs):
    out, own, other = refs[-3:]
    count = out.shape[0]
    base = (start + pl.program_id(0)) * count
    ch = out.shape[3]
    places = out.shape[1]

    @pl.when(pl.program_id(0) == 0)
    def _():
        own[...] = jnp.zeros_like(own)
        other[...] = jnp.zeros_like(other)

    for hold, parts in ((own, refs[:pieces]), (other, refs[pieces : 2 * pieces])):
        start = 0
        for ref in parts:
            for p in range(ref.shape[1] // ch):
                for h in range(ch // LANES):
                    lanes = slice(p * ch + h * LANES, p * ch + (h + 1) * LANES)
                    hold[h, pl.ds(start + p, count, stride=PITCH), :] = ref[:, lanes].astype(F32)
            start += ref.shape[1] // ch

    def image(n, carry):
        window = table[group[base + n]]
        rows = pl.ds(pl.multiple_of(n * PITCH, PITCH), PITCH)
        g0, g1 = (
            jnp.concatenate([hold[h, rows, :] for h in range(ch // LANES)], axis=1) for hold in (own, other)
        )
        highs, lows = [], []
        for s in range(2):
            grad = (first[s : s + 1, :] * g0 + first[2 + s : 3 + s, :] * g1) * (1.0 / 9.0)
            highs.append(grad.astype(BF16))
            lows.append((grad - highs[s].astype(F32)).astype(BF16))
        parts = jnp.concatenate(highs + lows, axis=0)
        spread = jnp.dot(window, parts, preferred_element_type=F32).astype(BF16)
        out[n] = spread[: 2 * places].reshape(places, 2, ch)
        return carry

    lax.fori_loop(0, count, image, 0, unroll=2)


def unpool(own, other, group, table, first, places, at, steps, before=()):
    count = own[0].shape[0]
    ch = first.shape[1]
    nb = IMAGE_BLOCK
    specs = [pl.BlockSpec((nb, piece.shape[1]), lambda i, g: (at + i, 0)) for piece in own + other]
    specs += [pl.BlockSpec(memory_space=pl.ANY)] * len(before)
    spread = jnp.swapaxes(table, 1, 2)
    spread = jnp.pad(jnp.concatenate([spread, spread], axis=2), ((0, 0), (0, 352 - 2 * places), (0, 0)))
    return pl.pallas_call(
        functools.partial(unpool_kernel, at, len(own)),
        grid_spec=pltpu.PrefetchScalarGridSpec(
            num_scalar_prefetch=1,
            grid=(steps,),
            in_specs=[
                pl.BlockSpec(spread.shape, lambda i, g: (0, 0, 0)),
                pl.BlockSpec((4, ch), lambda i, g: (0, 0)),
            ]
            + specs,
            out_specs=pl.BlockSpec((nb, places, 2, ch), lambda i, g: (at + i, 0, 0, 0)),
            scratch_shapes=[pltpu.VMEM((ch // LANES, nb * PITCH, LANES), F32)] * 2,
        ),
        out_shape=jax.ShapeDtypeStruct((count, places, 2, ch), BF16),
        input_output_aliases={3 + 2 * len(own): 0} if before else {},
        compiler_params=params(),
        cost_estimate=SMALL,
        name="unpool",
    )(group, spread, first, *own, *other, *before)


def tile_of(rows):
    return next(t for t in (1152, 768, 576, 512, 384, 256, 128) if rows % t == 0)


def fetch(outer, terms, rows, target, sem):
    def copy(term):
        return pltpu.make_async_copy(term.at[rows, :], target, sem)

    if len(terms) == 1:
        copy(terms[0]).start()
    else:
        pl.when(outer == 1)(lambda: copy(terms[0]).start())
        pl.when(outer == 0)(lambda: copy(terms[1]).start())


def chunk_kernel(layout, blocks, roles, vectors, cot_own, cot_other, *refs):
    chunks, count = len(layout), len(layout[0])
    feats, refs = refs[: blocks * HALVES], refs[blocks * HALVES :]
    at = 0
    pieces = []
    for counts in layout:
        pieces.append([])
        for many in counts:
            pieces[-1].append(refs[at : at + many])
            at += many
    act_out, dpre_out, sums_out = refs[at : at + 3]
    outs = [refs[at + 3 + i * count : at + 3 + (i + 1) * count] for i in range(chunks)]
    held, weight, total, k_own, k_other, high, low, in_sems, w_sems, cot_sems, out_sems = refs[-11:]
    steps, images, tile = held.shape
    per = steps // count
    units = total.shape[1] // chunks
    half, height = steps // HALVES, images // blocks

    def columns(i):
        return slice(i * units, (i + 1) * units)

    def begin(k):
        for s in range(count):

            @pl.when(k // per == s)
            def _(s=s):
                rows = pl.ds(pl.multiple_of((k - s * per) * tile, tile), tile)
                for i in range(chunks):
                    fetch(roles[0], pieces[i][s], rows, weight.at[k, :, columns(i)], w_sems.at[k])

        for h in range(HALVES):

            @pl.when(k // half == h)
            def _(h=h):
                cols = pl.ds(pl.multiple_of((k - h * half) * tile, tile), tile)
                for r in range(blocks):
                    part = feats[r * HALVES + h]
                    start = 0 if part.shape[0] == height else pl.multiple_of(roles[1] * height, height)
                    part = part.at[pl.ds(start, height), cols]
                    rows = pl.ds(r * height, height)
                    pltpu.make_async_copy(part, held.at[k, rows, :], in_sems.at[k]).start()

    def arrive(target, sem):
        pltpu.make_async_copy(target, target, sem).wait()

    ahead = min(AHEAD, steps)
    for k in range(ahead):
        begin(jnp.int32(k))
    cot_copies = [
        pltpu.make_async_copy(cot_own, k_own, cot_sems.at[0]),
        pltpu.make_async_copy(cot_other, k_other, cot_sems.at[1]),
    ]
    for copy in cot_copies:
        copy.start()
    total[...] = jnp.zeros_like(total)

    def forward_step(k, carry):
        pl.when(k + ahead < steps)(lambda: begin(k + ahead))
        arrive(held.at[k], in_sems.at[k])
        arrive(weight.at[k], w_sems.at[k])
        total[...] += jnp.dot(held[k], weight[k], preferred_element_type=F32)
        return carry

    lax.fori_loop(0, steps, forward_step, 0)
    for copy in cot_copies:
        copy.wait()

    bias, own_coef, other_coef = (vectors[i : i + 1, :] for i in range(3))
    c = 0.7978845608028654
    block = 32

    def rows_of(i, sums):
        rows = pl.ds(pl.multiple_of(i * block, block), block)
        x = total[rows, :] + bias
        x2 = x * x
        t = jnp.tanh(c * (x + 0.044715 * (x2 * x)))
        half = 0.5 * (1.0 + t)
        act = (x * half).astype(BF16)
        slope = half + (0.5 * c) * x * (1.0 - t * t) * (1.0 + (3.0 * 0.044715) * x2)
        k0 = k_own[rows, :].astype(F32)
        k1 = k_other[rows, :].astype(F32)
        dpre = ((own_coef * k0 + other_coef * k1) * slope).astype(BF16)
        act_out[rows, :] = act
        dpre_out[rows, :] = dpre
        actf = act.astype(F32)

        def fold(v):
            return jnp.sum(v.reshape(block // 8, 8, v.shape[1]), axis=0)

        return (
            sums[0] + fold(dpre.astype(F32)),
            sums[1] + fold(k0 * actf),
            sums[2] + fold(k1 * actf),
        )

    zero = jnp.zeros((8, total.shape[1]), F32)
    sums = lax.fori_loop(0, images // block, rows_of, (zero, zero, zero))
    for i in range(3):
        sums_out[i] = sums[i]

    def product(k):
        return lax.dot_general(
            held[k], dpre_out[...], (((0,), (0,)), ((), ())), preferred_element_type=F32
        )

    def last_steps(k, carry):
        made = product(k).astype(BF16)
        for i in range(chunks):
            low[k - per, i] = made[:, columns(i)]
        for s in range(1, count):

            @pl.when(k // per == s)
            def _(s=s):
                rows = pl.ds(pl.multiple_of((k - s * per) * tile, tile), tile)
                for i in range(chunks):
                    pltpu.make_async_copy(low.at[k - per, i], outs[i][s].at[rows, :], out_sems.at[k]).start()

        return carry

    def first_steps(k, carry):
        made = product(k)
        rows = pl.ds(pl.multiple_of(k * tile, tile), tile)
        for i in range(chunks):
            high[k, i] = made[:, columns(i)]
            pltpu.make_async_copy(high.at[k, i], outs[i][0].at[rows, :], out_sems.at[k]).start()
        return carry

    if count > 1:
        lax.fori_loop(per, steps, last_steps, 0)
    lax.fori_loop(0, per, first_steps, 0)
    for k in range(steps):
        arrive(high.at[k] if k < per else low.at[k - per], out_sems.at[k])


def chunk(roles, feats, pieces, vectors, cot_own, cot_other):
    images, width = cot_own.shape
    units = width // len(pieces)
    depth = sum(part.shape[1] for part in feats[0])
    count = len(pieces[0])
    height = pieces[0][0][0].shape[0]
    tile = tile_of(height)
    steps, per = depth // tile, height // tile
    terms = [term for chunk in pieces for piece in chunk for term in piece]
    anywhere = pl.BlockSpec(memory_space=pl.ANY)
    vmem = pl.BlockSpec(memory_space=pltpu.VMEM)
    kinds = ([F32] + [BF16] * (count - 1)) * len(pieces)
    return pl.pallas_call(
        functools.partial(chunk_kernel, [[len(p) for p in chunk] for chunk in pieces], len(feats)),
        in_specs=[pl.BlockSpec(memory_space=pltpu.SMEM), vmem]
        + [anywhere] * (2 + len(feats) * HALVES + len(terms)),
        out_specs=[vmem] * 3 + [anywhere] * len(kinds),
        out_shape=[
            jax.ShapeDtypeStruct((images, width), BF16),
            jax.ShapeDtypeStruct((images, width), BF16),
            jax.ShapeDtypeStruct((3, 8, width), F32),
        ]
        + [jax.ShapeDtypeStruct((height, units), kind) for kind in kinds],
        scratch_shapes=[
            pltpu.VMEM((steps, images, tile), BF16),
            pltpu.VMEM((steps, tile, width), BF16),
            pltpu.VMEM((images, width), F32),
            pltpu.VMEM((images, width), BF16),
            pltpu.VMEM((images, width), BF16),
            pltpu.VMEM((per, len(pieces), tile, units), F32),
            pltpu.VMEM((max(steps - per, 1), len(pieces), tile, units), BF16),
            pltpu.SemaphoreType.DMA((steps,)),
            pltpu.SemaphoreType.DMA((steps,)),
            pltpu.SemaphoreType.DMA((2,)),
            pltpu.SemaphoreType.DMA((steps,)),
        ],
        compiler_params=params(),
        cost_estimate=SMALL,
        name="chunk",
    )(roles, vectors, cot_own, cot_other, *[part for block in feats for part in block], *terms)


def back_kernel(layout, groups, roles, *refs):
    count = len(layout)
    grads = refs[:groups]
    at = groups
    pieces = []
    for many in layout:
        pieces.append(refs[at : at + many])
        at += many
    keep_out, send_out, grad, weight, keep, send, grad_sems, w_sems, out_sems = refs[at:]
    steps, tile, total = weight.shape
    units, width = total // count, total // groups
    half = keep.shape[1]
    grad_copies = []
    for j in range(groups):
        cols = pl.ds(j * width, width)
        grad_copies.append(pltpu.make_async_copy(grads[j], grad.at[:, cols], grad_sems.at[j]))
        grad_copies[j].start()
    for k in range(steps):
        for j in range(count):
            rows, cols = pl.ds(k * tile, tile), pl.ds(j * units, units)
            fetch(roles[0], pieces[j], rows, weight.at[k, :, cols], w_sems.at[k])
    for copy in grad_copies:
        copy.wait()
    contract = (((1,), (1,)), ((), ()))

    def step(k, carry):
        pltpu.make_async_copy(weight.at[k], weight.at[k], w_sems.at[k]).wait()
        cols = pl.ds(pl.multiple_of(k * tile, tile), tile)
        send[k] = lax.dot_general(grad[half:, :], weight[k], contract, preferred_element_type=F32).astype(BF16)
        pltpu.make_async_copy(send.at[k], send_out.at[:, cols], out_sems.at[k, 0]).start()
        keep[k] = lax.dot_general(grad[:half, :], weight[k], contract, preferred_element_type=F32)
        pltpu.make_async_copy(keep.at[k], keep_out.at[:, cols], out_sems.at[k, 1]).start()
        return carry

    lax.fori_loop(0, steps, step, 0)
    for k in range(steps):
        pltpu.make_async_copy(send.at[k], send.at[k], out_sems.at[k, 0]).wait()
        pltpu.make_async_copy(keep.at[k], keep.at[k], out_sems.at[k, 1]).wait()


def back(roles, grads, piece):
    rows, width = grads[0].shape
    depth = piece[0][0].shape[0]
    tile = next(t for t in (768, 512, 384, 256, 128) if depth % t == 0)
    steps = depth // tile
    terms = [term for part in piece for term in part]
    anywhere = pl.BlockSpec(memory_space=pl.ANY)
    half, total, groups = rows // 2, width * len(grads), len(grads)
    return pl.pallas_call(
        functools.partial(back_kernel, [len(c) for c in piece], groups),
        in_specs=[pl.BlockSpec(memory_space=pltpu.SMEM)] + [anywhere] * (groups + len(terms)),
        out_specs=[anywhere, anywhere],
        out_shape=[
            jax.ShapeDtypeStruct((half, depth), F32),
            jax.ShapeDtypeStruct((half, depth), BF16),
        ],
        scratch_shapes=[
            pltpu.VMEM((rows, total), BF16),
            pltpu.VMEM((steps, tile, total), BF16),
            pltpu.VMEM((steps, half, tile), F32),
            pltpu.VMEM((steps, half, tile), BF16),
            pltpu.SemaphoreType.DMA((groups,)),
            pltpu.SemaphoreType.DMA((steps,)),
            pltpu.SemaphoreType.DMA((steps, 2)),
        ],
        compiler_params=params(),
        cost_estimate=SMALL,
        name="back",
    )(roles, *grads, *terms)


def tile_of(rows):
    return next(t for t in (1152, 768, 576, 512, 384, 256, 128) if rows % t == 0)


def either(flag, value, axis):
    return jnp.where(flag, jnp.flip(value, axis), value)


class Program:
    def __init__(self, convmaps, group, alpha1, weight, bias, alpha2, cotangent):
        self.order = Order()
        self.convmaps, self.group, self.weight = convmaps, group, weight
        self.count, _, self.places, self.channels = convmaps.shape
        batch_id = lax.axis_index("batch")
        tower_id = lax.axis_index("tower")
        self.x, self.z = batch_id % 2, batch_id // 2
        self.y, self.core = tower_id // 2, tower_id % 2
        self.depth, self.width = weight.shape
        self.units = self.width // 2
        self.m = self.units // GROUPS
        self.n = self.m // 2 if is_line() else self.m
        self.images = 8 * self.count
        self.mine, self.theirs = self.x * self.units, (1 - self.x) * self.units
        units = self.units
        second = lax.dynamic_slice_in_dim(alpha2, self.mine, units, 1)
        self.own_coef = lax.dynamic_index_in_dim(second, self.y, 0, keepdims=True).astype(F32)
        self.cross = lax.dynamic_index_in_dim(second, 1 - self.y, 0, keepdims=True)
        own_bias = lax.dynamic_slice_in_dim(bias, self.mine, units, 0)[None, :].astype(F32)
        self.own_bias = own_bias
        cot = cotangent.reshape(2, 2, self.count, self.width)
        cot = either(self.core == 1, either(self.y == 1, cot, 0), 1).swapaxes(0, 1)
        self.cot_mine = lax.dynamic_slice_in_dim(cot, self.mine, units, 3)
        self.cot_theirs = lax.dynamic_slice_in_dim(cot, self.theirs, units, 3)
        places = jnp.arange(POOLED)
        if is_line():
            places = places.reshape(4, -1)[line_order(self.z)].reshape(-1)
        self.table = pool_table(places)
        self.first = either(self.y == 1, alpha1.astype(F32), 0).reshape(4, self.channels)
        self.weight_grad = jnp.zeros((self.depth, self.width), F32)
        self.is_outer = (self.z == 0) | (self.z == 3)
        self.roles = jnp.stack([self.is_outer.astype(jnp.int32), 1 - self.core])
        self.cot_own, self.cot_other = {}, {}
        self.acts, self.grads, self.sums = {}, {}, {}
        self.stitched, self.crossed = {}, {}

    def then(self, value):
        return self.order.then(value)

    def did(self, value):
        return self.order.did(value)

    def send_cross(self):
        return self.send(y_swap, self.cross)

    def keep_cross(self, came):
        cross_back = self.then(came).astype(F32)
        zeros = jnp.zeros((5, self.units), F32)
        self.vectors = jnp.concatenate([self.own_bias, self.own_coef, cross_back, zeros])
        self.cross = self.cross.astype(F32)

    def group_cols(self, g):
        return slice(g * self.m, (g + 1) * self.m)

    def weight_part(self, start, j, many=1):
        return lax.dynamic_slice(self.weight, (0, start + j * self.n), (self.depth, many * self.n))

    def swap_weight(self, j, many=1):
        return self.send(x_swap, self.weight_part(self.theirs, j, many))

    def slab_weight(self, j, came):
        a, b = self.weight_part(self.mine, j), self.then(came)
        return self.did(jnp.where(self.x == 0, jnp.concatenate([a, b]), jnp.concatenate([b, a])))

    def swap_cotangents(self, g):
        return self.send(x_swap, self.cot_theirs[..., self.group_cols(g)])

    def pass_cotangents(self, g, came):
        cot = self.did(jnp.stack([self.cot_mine[..., self.group_cols(g)], self.then(came)], axis=1))
        self.cot_own[g] = cot.reshape(self.images, self.m)
        return self.send(y_swap, cot)

    def keep_cotangents(self, g, came):
        self.cot_other[g] = self.did(jnp.flip(self.then(came), 2).reshape(self.images, self.m))

    def send(self, move, value, *args):
        return move(self.did(self.then(value)), *args)

    def chunk(self, g, feats, pieces):
        act, dpre, sums, *products = chunk(
            self.roles,
            feats,
            pieces,
            self.then(self.vectors[:, self.group_cols(g)]),
            self.cot_own[g],
            self.cot_other[g],
        )
        self.did(dpre)
        self.acts[g], self.grads[g], self.sums[g] = act, dpre, sums
        count = len(pieces[0])
        return [products[i * count : (i + 1) * count] for i in range(len(pieces))]

    def swap_act(self, g):
        return self.send(y_swap, self.acts[g])

    def stitch(self, g, came):
        cols = self.group_cols(g)
        other_act = jnp.flip(self.then(came).reshape(4, 2, self.count, self.m), 1).reshape(self.images, self.m)
        mix = self.own_coef[:, cols] * self.acts[g].astype(F32) + self.cross[:, cols] * other_act.astype(F32)
        mix = self.did(mix.astype(BF16)).reshape(2, 2, 2, self.count, self.m)
        self.stitched[g] = mix[:, 0]
        return mix[:, 1]

    def swap_grad(self, j, slab):
        leave = lax.dynamic_slice_in_dim(slab, (1 - self.x) * self.depth, self.depth, 0)
        came = self.send(x_swap, leave.astype(BF16))
        stay = lax.dynamic_slice_in_dim(slab, self.x * self.depth, self.depth, 0)
        self.weight_grad = self.did(
            lax.dynamic_update_slice(self.weight_grad, stay, (0, self.mine + j * self.n))
        )
        return came

    def store_grad(self, j, came):
        self.weight_grad = self.did(
            lax.dynamic_update_slice(
                self.weight_grad, self.then(came).astype(F32), (0, self.theirs + j * self.n)
            )
        )

    def activations(self):
        left = jnp.concatenate([self.stitched[g] for g in range(GROUPS)], axis=3)
        right = jnp.concatenate([self.crossed[g] for g in range(GROUPS)], axis=3)
        rows = jnp.where(
            self.x == 0, jnp.concatenate([left, right], 3), jnp.concatenate([right, left], 3)
        )
        rows = either(self.y == 1, either(self.core == 1, rows, 0), 1).swapaxes(0, 1)
        return rows.reshape(4 * self.count, self.width)

    def unit_sums(self):
        return self.did(
            jnp.concatenate([jnp.sum(self.then(self.sums[g]), axis=1) for g in range(GROUPS)], axis=1)
        )

    def small_grads(self, sums, far, other_second):
        sums, other_second = (
            jnp.where(self.x == 0, jnp.concatenate([a, b], -1), jnp.concatenate([b, a], -1))
            for a, b in ((sums, far), other_second)
        )
        return sums[0], either(self.y == 1, jnp.stack([sums[1], other_second]), 0)

    def back(self, s, chunks):
        grads = [self.grads[g] for g in range(GROUPS)]
        keep, send = back(self.roles, [self.then(grads[0])] + grads[1:], [chunk[s] for chunk in chunks])
        return keep, self.did(send)

    def back_x(self, keep, came):
        part = keep + self.then(came).astype(F32)
        return part[: 2 * self.count], self.did(part[2 * self.count :].astype(BF16))

    def back_y(self, keep, came):
        part = keep + self.then(came).astype(F32)
        return part[: self.count], self.did(part[self.count :].astype(BF16))

    def first_grad(self, own, other, pooled, begin=0):
        return self.did(first_grad(pooled, [self.then(own[0])] + own[1:], other, begin))

    def by_tower(self, partial):
        return either(self.y == 1, partial.reshape(2, 2, self.channels), 0)

    def unpool(self, own, other, at, steps, before=()):
        return unpool(
            [self.then(own[0])] + own[1:],
            other,
            self.group,
            self.table,
            self.first,
            self.places,
            at,
            steps,
            before,
        )


def line_program(p):
    then, did = p.then, p.did
    came, blocks, near, inner, outer, first_out, last_out = {}, {}, {}, {}, {}, {}, {}
    total, into, crossed, middle, final, slab_came = {}, {}, {}, {}, {}, {}
    from_own, swapped = {}, {}

    def send(kind, value):
        return p.send(line, value, kind)

    def arrive(value):
        return did(then(value))

    def block(j):
        blocks[j] = p.slab_weight(j, came[j])

    def pieces(j):
        beside = (near[j],) if j < 2 else (from_own[j], swapped[j])
        return [(blocks[j],), beside, (first_out[j], inner[j]), (last_out[j], outer[j])]

    def part(j, s):
        return total[j][s]

    def payload(inward, outward):
        return did(jnp.where(p.is_outer, then(inward), outward))

    def ends(value):
        return send("near", value)

    def inward(j, s):
        return send("inward", then(part(j, s)))

    def plus(j, s, value):
        return (part(j, s).astype(F32) + then(value).astype(F32)).astype(BF16)

    def slab(j):
        ends = jnp.where(
            p.is_outer,
            then(final[j]).astype(F32),
            into[j, 1].astype(F32) + then(middle[j]).astype(F32),
        )
        slab_came[j] = p.swap_grad(j, did(part(j, 0) + ends))

    image_blocks = p.count // IMAGE_BLOCK
    early = image_blocks // 8
    came[0] = p.swap_weight(0)
    made = pool(p.convmaps, p.group, then(p.table), p.first, 0, early)
    did(made[0])
    came[0] = arrive(came[0])
    block(0)
    near[0] = ends(blocks[0])
    inner[0] = send("middle", blocks[0])
    came[1] = p.swap_weight(1)
    cot_came = p.swap_cotangents(0)
    cross_came = p.send_cross()
    kept_a, kept_b, sent_a, sent_b, pooled = pool(
        p.convmaps, p.group, then(p.table), p.first, early, image_blocks - early, made
    )
    did(kept_a)
    came[1] = arrive(came[1])
    block(1)
    near[0] = arrive(near[0])
    near[1] = ends(blocks[1])
    inner[0] = arrive(inner[0])
    inner[1] = send("middle", blocks[1])
    cot_came = arrive(cot_came)
    p.keep_cross(cross_came)
    x_a = p.send(x_swap, kept_a)
    y_a = p.send(y_swap, sent_a)
    near[1] = arrive(near[1])
    first_out[0] = send("outward", inner[0])
    inner[1] = arrive(inner[1])
    outer[0] = send("middle", near[0])
    x_a = arrive(x_a)
    came_pair = p.swap_weight(2, 2)
    y_a = arrive(y_a)
    y_b = p.send(y_swap, sent_b)
    c_kept = [both_cores(arrive(kept_a)), both_cores(arrive(kept_b))]
    c_x_a, c_y_a = both_cores(x_a), both_cores(y_a)
    first_out[0] = arrive(first_out[0])
    first_out[1] = send("outward", inner[1])
    outer[0] = arrive(outer[0])
    outer[1] = send("middle", near[1])
    came_pair = arrive(came_pair)
    x_b = p.send(x_swap, kept_b)
    y_b = arrive(y_b)
    cot_passed = p.pass_cotangents(0, cot_came)
    c_y_b = both_cores(y_b)
    came[2], came[3] = came_pair[:, : p.n], came_pair[:, p.n :]
    block(2)
    block(3)
    value = payload(blocks[2], outer[0])
    first_out[1] = arrive(first_out[1])
    swapped[2] = last_out[0] = ends(value)
    outer[1] = arrive(outer[1])
    inner[2] = send("middle", blocks[2])
    x_b = arrive(x_b)
    x_y_a = p.send(x_swap, y_a)
    c_x_b = both_cores(x_b)
    value = payload(blocks[3], outer[1])
    cot_passed = arrive(cot_passed)
    p.keep_cotangents(0, cot_passed)
    swapped[2] = last_out[0] = arrive(swapped[2])
    swapped[3] = last_out[1] = ends(value)
    inner[2] = arrive(inner[2])
    inner[3] = send("middle", blocks[3])
    x_y_a = arrive(x_y_a)
    x_y_b = p.send(x_swap, y_b)
    c_x_y_a = p.send(c_swap, x_y_a)
    swapped[3] = last_out[1] = arrive(swapped[3])
    from_own[2] = send("outward", blocks[2])
    inner[3] = arrive(inner[3])
    outer[2] = send("middle", swapped[2])
    c_x_y_a = arrive(c_x_y_a)
    x_y_b = arrive(x_y_b)
    c_x_y_b = p.send(c_swap, x_y_b)
    cot_came = p.swap_cotangents(1)
    c_x_y_b = arrive(c_x_y_b)
    feats = [
        [kept_a, kept_b],
        [y_a, y_b],
        [x_a, x_b],
        [x_y_a, x_y_b],
        c_kept,
        [c_y_a, c_y_b],
        [c_x_a, c_x_b],
        [c_x_y_a, c_x_y_b],
    ]
    total[0], total[1] = p.chunk(0, feats, [pieces(0), pieces(1)])
    value = payload(part(0, 3), blocks[3])
    from_own[2] = arrive(from_own[2])
    into[0, 3] = from_own[3] = ends(value)
    outer[2] = arrive(outer[2])
    outer[3] = send("middle", swapped[3])
    cot_came = arrive(cot_came)
    act_came = p.swap_act(0)
    value = payload(part(0, 2), inner[2])
    into[0, 3] = from_own[3] = arrive(into[0, 3])
    into[0, 2] = first_out[2] = ends(value)
    outer[3] = arrive(outer[3])
    crossed[0] = send("middle", plus(0, 3, into[0, 3]))
    act_came = arrive(act_came)
    cot_passed = p.pass_cotangents(1, cot_came)
    value = payload(part(0, 1), inner[3])
    mix = p.stitch(0, act_came)
    into[0, 2] = first_out[2] = arrive(into[0, 2])
    into[0, 1] = first_out[3] = ends(value)
    crossed[0] = arrive(crossed[0])
    middle[0] = send("middle", plus(0, 2, into[0, 2]))
    p.crossed[0] = p.send(x_swap, mix)
    value = payload(part(1, 3), outer[2])
    cot_passed = arrive(cot_passed)
    p.keep_cotangents(1, cot_passed)
    into[0, 1] = first_out[3] = arrive(into[0, 1])
    into[1, 3] = last_out[2] = ends(value)
    middle[0] = arrive(middle[0])
    p.crossed[0] = arrive(p.crossed[0])
    value = payload(part(1, 2), outer[3])
    into[1, 3] = last_out[2] = arrive(into[1, 3])
    into[1, 2] = last_out[3] = ends(value)
    crossed[1] = send("middle", plus(1, 3, into[1, 3]))
    value = payload(part(1, 1), plus(0, 1, crossed[0]))
    into[1, 2] = last_out[3] = arrive(into[1, 2])
    into[1, 1] = final[0] = ends(value)
    crossed[1] = arrive(crossed[1])
    middle[1] = send("middle", plus(1, 2, into[1, 2]))
    total[2], total[3] = p.chunk(1, feats, [pieces(2), pieces(3)])
    value = payload(part(2, 3), plus(1, 1, crossed[1]))
    chunks = [pieces(j) for j in range(4)]
    kept_c, send_c, came_c, kept_x, send_x, came_x = {}, {}, {}, {}, {}, {}
    own, send_y, other = {}, {}, {}
    into[1, 1] = final[0] = arrive(into[1, 1])
    into[2, 3] = final[1] = ends(value)
    middle[1] = arrive(middle[1])
    kept_c[0], send_c[0] = p.back(0, chunks)
    came_c[0] = p.send(c_swap, send_c[0])
    slab(0)
    sums = p.unit_sums()
    sums_came = p.send(flipped, sums, "batch", 2)
    act_came = p.swap_act(1)
    came_c[0] = arrive(came_c[0])
    kept_x[0], send_x[0] = p.back_x(kept_c[0], came_c[0])
    came_x[0] = p.send(x_swap, send_x[0])
    kept_c[1], send_c[1] = p.back(1, chunks)
    into[2, 3] = final[1] = arrive(into[2, 3])
    into[3, 3] = inward(3, 3)
    crossed[2] = send("middle", plus(2, 3, into[2, 3]))
    came_c[1] = p.send(c_swap, send_c[1])
    act_came = arrive(act_came)
    sums = did(sums + then(sums_came))
    slab_came[0] = arrive(slab_came[0])
    kept_c[2], send_c[2] = p.back(2, chunks)
    came_c[1] = arrive(came_c[1])
    kept_x[1], send_x[1] = p.back_x(kept_c[1], came_c[1])
    mix = p.stitch(1, act_came)
    came_x[0] = arrive(came_x[0])
    came_x[1] = p.send(x_swap, send_x[1])
    own[0], send_y[0] = p.back_y(kept_x[0], came_x[0])
    into[3, 3] = arrive(into[3, 3])
    into[2, 2] = inward(2, 2)
    crossed[2] = arrive(crossed[2])
    crossed[3] = send("middle", plus(3, 3, into[3, 3]))
    came_c[2] = p.send(c_swap, send_c[2])
    other[0] = p.send(y_swap, send_y[0])
    kept_c[3], send_c[3] = p.back(3, chunks)
    came_c[2] = arrive(came_c[2])
    kept_x[2], send_x[2] = p.back_x(kept_c[2], came_c[2])
    came_x[1] = arrive(came_x[1])
    came_x[2] = p.send(x_swap, send_x[2])
    own[1], send_y[1] = p.back_y(kept_x[1], came_x[1])
    into[2, 2] = arrive(into[2, 2])
    into[3, 2] = inward(3, 2)
    crossed[3] = arrive(crossed[3])
    middle[2] = send("middle", plus(2, 2, into[2, 2]))
    other[0] = arrive(other[0])
    came_c[3] = p.send(c_swap, send_c[3])
    other[1] = p.send(y_swap, send_y[1])
    value = payload(part(2, 1), plus(2, 1, crossed[2]))
    p.store_grad(0, slab_came[0])
    came_c[3] = arrive(came_c[3])
    kept_x[3], send_x[3] = p.back_x(kept_c[3], came_c[3])
    came_x[2] = arrive(came_x[2])
    came_x[3] = p.send(x_swap, send_x[3])
    own[2], send_y[2] = p.back_y(kept_x[2], came_x[2])
    into[3, 2] = arrive(into[3, 2])
    into[2, 1] = final[2] = ends(value)
    middle[2] = arrive(middle[2])
    middle[3] = send("middle", plus(3, 2, into[3, 2]))
    other[1] = arrive(other[1])
    other[2] = p.send(y_swap, send_y[2])
    sums_came = p.send(flipped, sums, "batch", 4)
    value = payload(part(3, 1), plus(3, 1, crossed[3]))
    quarter = p.channels * POOLED // 4
    partial = p.first_grad([own[0], own[1]], [other[0], other[1]], pooled)
    came_x[3] = arrive(came_x[3])
    own[3], send_y[3] = p.back_y(kept_x[3], came_x[3])
    slab(1)
    into[2, 1] = final[2] = arrive(into[2, 1])
    into[3, 1] = final[3] = ends(value)
    middle[3] = arrive(middle[3])
    other[2] = arrive(other[2])
    other[3] = p.send(y_swap, send_y[3])
    sums = did(sums + then(sums_came))
    far = p.send(x_swap, sums)
    slab(2)
    p.crossed[1] = p.send(x_swap, mix)
    other[3] = arrive(other[3])
    owns, others = ([parts[s] for s in range(4)] for parts in (own, other))
    partial = partial + p.first_grad(owns[2:], others[2:], pooled, 2 * quarter)
    partial = did(p.by_tower(partial))
    partial_came = p.send(c_swap, partial)
    grad = did(p.unpool(owns, others, 0, image_blocks // 2))
    into[3, 1] = final[3] = arrive(into[3, 1])
    slab(3)
    partial = did(partial + then(partial_came))
    partial_came = p.send(y_swap, partial)
    far = arrive(far)
    other_second = p.send(y_swap, jnp.stack([sums[2], far[2]]))
    slab_came[1] = arrive(slab_came[1])
    slab_came[2] = arrive(slab_came[2])
    p.crossed[1] = arrive(p.crossed[1])
    grad = did(p.unpool(owns, others, image_blocks // 2, image_blocks - image_blocks // 2, (grad,)))
    partial = did(partial + then(partial_came))
    partial_came = p.send(x_swap, partial)
    p.store_grad(1, slab_came[1])
    partial = did(partial + then(partial_came))
    partial_came = p.send(flipped, partial, "batch", 2)
    p.store_grad(2, slab_came[2])
    partial = did(partial + then(partial_came))
    partial_came = p.send(flipped, partial, "batch", 4)
    p.store_grad(3, slab_came[3])
    alpha1_grad = partial + then(partial_came)
    bias_grad, alpha2_grad = p.small_grads(sums, far, other_second)
    input_grad = jnp.swapaxes(grad, 1, 2)
    return (p.activations(), input_grad, p.weight_grad, bias_grad, alpha1_grad, alpha2_grad)


def plain_program(p):
    groups = slab_groups()
    p.keep_cross(p.send_cross())
    *features, pooled = pool(p.convmaps, p.group, p.table, p.first, 0, p.count // IMAGE_BLOCK)
    feats = [features[:HALVES], [y_swap(part) for part in features[HALVES:]]]
    feats += [[x_swap(part) for part in block] for block in feats]
    feats += [[c_swap(part) for part in block] for block in feats]
    chunks = []
    for g in range(GROUPS):
        p.keep_cotangents(g, p.pass_cotangents(g, p.swap_cotangents(g)))
        block = p.slab_weight(g, p.swap_weight(g))
        rows = lax.all_gather(block, "batch", axis=0, tiled=True, axis_index_groups=groups)
        chunks.append([(rows,)])
        [[total]] = p.chunk(g, feats, [chunks[g]])
        slab = lax.psum_scatter(total, "batch", scatter_dimension=0, tiled=True, axis_index_groups=groups)
        p.store_grad(g, p.swap_grad(g, slab))
        p.crossed[g] = p.send(x_swap, p.stitch(g, p.swap_act(g)))
    sums = lax.psum(p.unit_sums(), "batch", axis_index_groups=groups)
    far = x_swap(sums)
    bias_grad, alpha2_grad = p.small_grads(sums, far, y_swap(jnp.stack([sums[2], far[2]])))
    keep, send = p.back(0, chunks)
    keep, send = p.back_x(keep, c_swap(send))
    own, send = p.back_y(keep, x_swap(send))
    other = y_swap(send)
    alpha1_grad = lax.psum(p.by_tower(p.first_grad([own], [other], pooled)), ("batch", "tower"))
    grad = p.unpool([own], [other], 0, p.count // IMAGE_BLOCK)
    input_grad = jnp.swapaxes(grad, 1, 2)
    return (p.activations(), input_grad, p.weight_grad, bias_grad, alpha1_grad, alpha2_grad)


def shards(*args):
    return (line_program if is_line() else plain_program)(Program(*args))


def solution(mesh):
    in_specs = (
        P(("batch", "tower"), None, None, None),
        P(("batch", "tower")),
        P(),
        P("batch", "tower"),
        P("tower"),
        P(None, "tower"),
        P("batch", "tower"),
    )
    out_specs = (
        P("batch", "tower"),
        P(("batch", "tower"), None, None, None),
        P("batch", "tower"),
        P("tower"),
        P(),
        P(None, "tower"),
    )
    return jax.shard_map(shards, mesh=mesh, in_specs=in_specs, out_specs=out_specs, check_vma=False)
```

```python
import functools

import jax
import jax.numpy as jnp
from jax import lax
from jax.experimental import pallas as pl
from jax.experimental.pallas import tpu as pltpu
from jax.sharding import PartitionSpec as P

F32 = jnp.float32
BF16 = jnp.bfloat16
POOLED = 36
PITCH = 48
LANES = 128
VMEM_LIMIT = 56 * 1024 * 1024
SMALL = pl.CostEstimate(flops=1000, bytes_accessed=1000, transcendentals=0)
AHEAD = 2
IMAGE_BLOCK = 16
HALVES = 2


def params():
    return pltpu.CompilerParams(vmem_limit_bytes=VMEM_LIMIT)


def flipped(value, axis, bit):
    pairs = [(source, source ^ bit) for source in range(lax.axis_size(axis))]
    return lax.ppermute(value, axis, pairs)


def x_swap(value):
    return flipped(value, "batch", 1)


def y_swap(value):
    return flipped(value, "tower", 2)


def c_swap(value):
    return flipped(value, "tower", 1)


def line(value, kind):
    steps = {
        "near": ((0, 1), (1, 0), (2, 3), (3, 2)),
        "middle": ((1, 2), (2, 1)),
        "outward": ((1, 0), (2, 3)),
        "inward": ((0, 1), (3, 2)),
    }[kind]
    pairs = [(2 * a + x, 2 * b + x) for a, b in steps for x in range(2)]
    return lax.ppermute(value, "batch", pairs)


def slab_groups():
    size = lax.axis_size("batch")
    return [list(range(x, size, 2)) for x in range(2)]


def after(value, *others):
    return lax.optimization_barrier((value, *others))[0]


class Order:
    def __init__(self):
        self.last = None

    def then(self, value):
        return value if self.last is None else after(value, self.last)

    def did(self, value):
        self.last = value
        return value


def is_line():
    return lax.axis_size("batch") == 8


def line_order(z):
    rows = jnp.array([[0, 1, 2, 3], [1, 0, 2, 3], [2, 3, 1, 0], [3, 2, 1, 0]])
    return rows[z]


def core_groups():
    return [[t, t + 1] for t in range(0, lax.axis_size("tower"), 2)]


def both_cores(value):
    return lax.all_gather(value, "tower", axis=0, tiled=True, axis_index_groups=core_groups())


def pool_table(order):
    map_pos = jnp.arange(169)[None, :]
    prow = (order // 6)[:, None]
    pcol = (order % 6)[:, None]
    qrow = map_pos // 13
    qcol = map_pos % 13
    inside = (
        (qrow >= 2 * prow) & (qrow <= 2 * prow + 2) & (qcol >= 2 * pcol) & (qcol <= 2 * pcol + 2)
    )
    small = (prow < 5) & (pcol < 5)
    table = jnp.stack([inside, inside & small]).astype(BF16)
    table = jnp.pad(table, ((0, 0), (0, PITCH - POOLED), (0, 0)))
    both = table[:, None, :, :, None] * jnp.eye(2, dtype=BF16)[None, :, None, None, :]
    return both.reshape(2, 2 * PITCH, 338)


def pool_kernel(start, group, table, first, maps, *refs):
    *feature_outs, pooled_out, own, other, pool0, pool1 = refs[-(2 * HALVES + 5) :]
    count, places, _, ch = maps.shape
    base = (start + pl.program_id(0)) * count

    def image(n, carry):
        window = table[group[base + n]]
        rows_in = maps[n].reshape(2 * places, ch)
        both = jnp.dot(window, rows_in, preferred_element_type=F32) * (1.0 / 9.0)
        p0, p1 = both[:PITCH], both[PITCH:]
        rows = pl.ds(pl.multiple_of(n * PITCH, PITCH), PITCH)
        mixed0 = first[0:1, :] * p0 + first[1:2, :] * p1
        mixed1 = first[2:3, :] * p0 + first[3:4, :] * p1
        for hold, value in ((pool0, p0), (pool1, p1), (own, mixed0), (other, mixed1)):
            for h in range(ch // LANES):
                hold[h, rows, :] = value[:, h * LANES : (h + 1) * LANES]
        return carry

    lax.fori_loop(0, count, image, 0, unroll=2)
    per = POOLED // HALVES
    for p in range(POOLED):
        rows = pl.ds(p, count, stride=PITCH)
        for h in range(ch // LANES):
            lanes = slice(p * ch + h * LANES, p * ch + (h + 1) * LANES)
            part = slice((p % per) * ch + h * LANES, (p % per) * ch + (h + 1) * LANES)
            feature_outs[p // per][:, part] = own[h, rows, :].astype(BF16)
            feature_outs[HALVES + p // per][:, part] = other[h, rows, :].astype(BF16)
            pooled_out[0, :, lanes] = pool0[h, rows, :]
            pooled_out[1, :, lanes] = pool1[h, rows, :]


def pool(convmaps, group, table, first, at, steps, before=()):
    count, _, places, ch = convmaps.shape
    nb = IMAGE_BLOCK
    feats = POOLED * ch
    features = [((count, feats // HALVES), BF16)] * (2 * HALVES)
    return pl.pallas_call(
        functools.partial(pool_kernel, at),
        grid_spec=pltpu.PrefetchScalarGridSpec(
            num_scalar_prefetch=1,
            grid=(steps,),
            in_specs=[
                pl.BlockSpec(table.shape, lambda i, g: (0, 0, 0)),
                pl.BlockSpec((4, ch), lambda i, g: (0, 0)),
                pl.BlockSpec((nb, places, 2, ch), lambda i, g: (at + i, 0, 0, 0)),
            ]
            + [pl.BlockSpec(memory_space=pl.ANY)] * len(before),
            out_specs=[pl.BlockSpec((nb, feats // HALVES), lambda i, g: (at + i, 0))] * (2 * HALVES)
            + [pl.BlockSpec((2, nb, feats), lambda i, g: (0, at + i, 0))],
            scratch_shapes=[pltpu.VMEM((ch // LANES, nb * PITCH, LANES), F32)] * 4,
        ),
        out_shape=[jax.ShapeDtypeStruct(*f) for f in features]
        + [jax.ShapeDtypeStruct((2, count, feats), F32)],
        input_output_aliases={4 + i: i for i in range(len(before))},
        compiler_params=params(),
        cost_estimate=SMALL,
        name="pool",
    )(group, table, first, jnp.swapaxes(convmaps, 1, 2), *before)


def first_grad_kernel(pooled, keep, came, other, out):
    ch = out.shape[2]

    @pl.when(pl.program_id(0) == 0)
    def _():
        out[...] = jnp.zeros_like(out)

    for a in range(2):
        sums = [0.0, 0.0]
        for p in range(POOLED):
            lanes = slice(p * ch, (p + 1) * ch)
            if a == 0:
                grad = keep[:, lanes].astype(F32) + came[:, lanes].astype(F32)
            else:
                grad = other[:, lanes].astype(F32)
            for s in range(2):
                sums[s] = sums[s] + grad * pooled[s, :, lanes]
        for s in range(2):
            out[2 * a + s] += sums[s]


def first_grad(pooled, keep, came, other, at):
    images, feats = keep.shape
    ch = feats // POOLED
    nb = IMAGE_BLOCK
    rows = pl.BlockSpec((nb, feats), lambda i: (i, 0))
    sums = pl.pallas_call(
        first_grad_kernel,
        grid=(images // nb,),
        in_specs=[pl.BlockSpec((2, nb, feats), lambda i: (0, at // nb + i, 0)), rows, rows, rows],
        out_specs=pl.BlockSpec((4, nb, ch), lambda i: (0, 0, 0)),
        out_shape=jax.ShapeDtypeStruct((4, nb, ch), F32),
        compiler_params=params(),
        cost_estimate=SMALL,
        name="first_grad",
    )(pooled, keep, came, other)
    return jnp.sum(sums, axis=1)


def unpool_kernel(start, group, table, first, keep_in, came_in, other_in, *refs):
    out, own, other = refs[-3:]
    count = out.shape[0]
    base = start + pl.program_id(0) * count
    ch = out.shape[3]
    places = out.shape[1]

    @pl.when(pl.program_id(0) == 0)
    def _():
        own[...] = jnp.zeros_like(own)
        other[...] = jnp.zeros_like(other)

    for p in range(POOLED):
        for h in range(ch // LANES):
            lanes = slice(p * ch + h * LANES, p * ch + (h + 1) * LANES)
            rows = pl.ds(p, count, stride=PITCH)
            own[h, rows, :] = keep_in[:, lanes].astype(F32) + came_in[:, lanes].astype(F32)
            other[h, rows, :] = other_in[:, lanes].astype(F32)

    def image(n, carry):
        window = table[group[base + n]]
        rows = pl.ds(pl.multiple_of(n * PITCH, PITCH), PITCH)
        g0, g1 = (
            jnp.concatenate([hold[h, rows, :] for h in range(ch // LANES)], axis=1) for hold in (own, other)
        )
        highs, lows = [], []
        for s in range(2):
            grad = (first[s : s + 1, :] * g0 + first[2 + s : 3 + s, :] * g1) * (1.0 / 9.0)
            highs.append(grad.astype(BF16))
            lows.append((grad - highs[s].astype(F32)).astype(BF16))
        parts = jnp.concatenate(highs + lows, axis=0)
        spread = jnp.dot(window, parts, preferred_element_type=F32).astype(BF16)
        out[n] = spread[: 2 * places].reshape(places, 2, ch)
        return carry

    lax.fori_loop(0, count, image, 0, unroll=2)


def unpool(keep, came, other, group, table, first, places, at, count, before=()):
    images, feats = keep.shape
    ch = first.shape[1]
    nb = IMAGE_BLOCK
    rows = pl.BlockSpec((nb, feats), lambda i, g: (i, 0))
    spread = jnp.swapaxes(table, 1, 2)
    spread = jnp.pad(jnp.concatenate([spread, spread], axis=2), ((0, 0), (0, 352 - 2 * places), (0, 0)))
    return pl.pallas_call(
        functools.partial(unpool_kernel, at),
        grid_spec=pltpu.PrefetchScalarGridSpec(
            num_scalar_prefetch=1,
            grid=(images // nb,),
            in_specs=[
                pl.BlockSpec(spread.shape, lambda i, g: (0, 0, 0)),
                pl.BlockSpec((4, ch), lambda i, g: (0, 0)),
                rows,
                rows,
                rows,
            ]
            + [pl.BlockSpec(memory_space=pl.ANY)] * len(before),
            out_specs=pl.BlockSpec((nb, places, 2, ch), lambda i, g: (at // nb + i, 0, 0, 0)),
            scratch_shapes=[pltpu.VMEM((ch // LANES, nb * PITCH, LANES), F32)] * 2,
        ),
        out_shape=jax.ShapeDtypeStruct((count, places, 2, ch), BF16),
        input_output_aliases={6: 0} if before else {},
        compiler_params=params(),
        cost_estimate=SMALL,
        name="unpool",
    )(group, spread, first, keep, came, other, *before)


def store_kernel(chunk, chunks, x, own, came, *refs):
    out, stay, go, sems = refs[-4:]
    rows, width = came.shape

    def columns(at):
        return out.at[:, pl.ds(pl.multiple_of(at * width, width), width)]

    source = own.at[pl.ds(pl.multiple_of(x[0] * rows, rows), rows), :]
    read = pltpu.make_async_copy(source, stay, sems.at[0])
    read.start()
    go[...] = came[...].astype(F32)
    write = pltpu.make_async_copy(go, columns((1 - x[0]) * chunks + chunk), sems.at[1])
    write.start()
    read.wait()
    write_own = pltpu.make_async_copy(stay, columns(x[0] * chunks + chunk), sems.at[2])
    write_own.start()
    write.wait()
    write_own.wait()


def store(own, came, x, chunk, chunks, shape, before=()):
    anywhere = pl.BlockSpec(memory_space=pl.ANY)
    return pl.pallas_call(
        functools.partial(store_kernel, chunk, chunks),
        in_specs=[pl.BlockSpec(memory_space=pltpu.SMEM), anywhere, pl.BlockSpec(memory_space=pltpu.VMEM)]
        + [anywhere] * len(before),
        out_specs=anywhere,
        out_shape=jax.ShapeDtypeStruct(shape, F32),
        scratch_shapes=[pltpu.VMEM(came.shape, F32)] * 2 + [pltpu.SemaphoreType.DMA((3,))],
        input_output_aliases={3: 0} if before else {},
        compiler_params=params(),
        cost_estimate=SMALL,
        name="store",
    )(x, own, came, *before)


def place_rows_kernel(places, *refs):
    *parts, out, sem = refs
    height, width = parts[0].shape[0] // 4, parts[0].shape[1]
    chunks = len(parts) // 2
    x, y, core = places[0], places[1], places[2]
    copies = []
    for i, part in enumerate(parts):
        side, j = i // chunks, i % chunks
        col = (jnp.where(x == side, 0, chunks) + j) * width
        cols = pl.ds(pl.multiple_of(col, width), width)
        for b in range(4):
            row = (2 * ((b % 2) ^ y) + ((b // 2) ^ core)) * height
            target = out.at[pl.ds(pl.multiple_of(row, height), height), cols]
            copies.append(pltpu.make_async_copy(part.at[pl.ds(b * height, height), :], target, sem.at[i, b]))
            copies[-1].start()
    for copy in copies:
        copy.wait()


def place_rows(places, own, other):
    parts = own + other
    rows, width = parts[0].shape
    return pl.pallas_call(
        place_rows_kernel,
        in_specs=[pl.BlockSpec(memory_space=pltpu.SMEM)] + [pl.BlockSpec(memory_space=pltpu.VMEM)] * len(parts),
        out_specs=pl.BlockSpec(memory_space=pl.ANY),
        out_shape=jax.ShapeDtypeStruct((rows, width * len(parts)), BF16),
        scratch_shapes=[pltpu.SemaphoreType.DMA((len(parts), 4))],
        compiler_params=params(),
        cost_estimate=SMALL,
        name="place_rows",
    )(places, *parts)


def tile_of(rows):
    return next(t for t in (1152, 768, 576, 512, 384, 256, 128) if rows % t == 0)


def fetch(outer, terms, rows, target, sem):
    def copy(term):
        return pltpu.make_async_copy(term.at[rows, :], target, sem)

    if len(terms) == 1:
        copy(terms[0]).start()
    else:
        pl.when(outer == 1)(lambda: copy(terms[0]).start())
        pl.when(outer == 0)(lambda: copy(terms[1]).start())


def chunk_kernel(layout, starts, cot_cols, roles, vectors, *refs):
    chunks, count = len(layout), len(layout[0])
    cots, refs = refs[:4], refs[4:]
    blocks = len(starts) // HALVES
    feats, refs = refs[: blocks * HALVES], refs[blocks * HALVES :]
    at = 0
    pieces = []
    for counts in layout:
        pieces.append([])
        for many in counts:
            pieces[-1].append(refs[at : at + many])
            at += many
    act_out, keep_out, send_out, sums_out = refs[at : at + 4]
    outs = [refs[at + 4 + i * count : at + 4 + (i + 1) * count] for i in range(chunks)]
    held, weight, total, dpre_out, k_own, k_other, high, low, in_sems, w_sems, cot_sems, out_sems = refs[-12:]
    steps, images, tile = held.shape
    per = steps // count
    units = total.shape[1] // chunks
    half, height = steps // HALVES, images // blocks

    def columns(i):
        return slice(i * units, (i + 1) * units)

    def begin(k):
        for s in range(count):

            @pl.when(k // per == s)
            def _(s=s):
                rows = pl.ds(pl.multiple_of((k - s * per) * tile, tile), tile)
                for i in range(chunks):
                    fetch(roles[0], pieces[i][s], rows, weight.at[k, :, columns(i)], w_sems.at[k])

        for h in range(HALVES):

            @pl.when(k // half == h)
            def _(h=h):
                cols = pl.ds(pl.multiple_of((k - h * half) * tile, tile), tile)
                for r in range(blocks):
                    at = r * HALVES + h
                    start = starts[at]
                    if start is None:
                        start = pl.multiple_of(roles[1] * height, height)
                    part = feats[at].at[pl.ds(start, height), cols]
                    rows = pl.ds(r * height, height)
                    pltpu.make_async_copy(part, held.at[k, rows, :], in_sems.at[k]).start()

    def arrive(target, sem):
        pltpu.make_async_copy(target, target, sem).wait()

    ahead = min(AHEAD, steps)
    for k in range(ahead):
        begin(jnp.int32(k))
    for tower, target in enumerate((k_own, k_other)):
        for r in range(blocks):
            core, x, y = r // 4, r // 2 % 2, r % 2
            source, col = cots[2 * tower + x], cot_cols[2 * tower + x]
            rows = pl.ds((2 * core + (y ^ tower)) * height, height)
            source = source.at[rows, pl.ds(col, total.shape[1])]
            target_rows = target.at[pl.ds(r * height, height), :]
            pltpu.make_async_copy(source, target_rows, cot_sems.at[tower]).start()
    total[...] = jnp.zeros_like(total)

    def forward_step(k, carry):
        pl.when(k + ahead < steps)(lambda: begin(k + ahead))
        arrive(held.at[k], in_sems.at[k])
        arrive(weight.at[k], w_sems.at[k])
        total[...] += jnp.dot(held[k], weight[k], preferred_element_type=F32)
        return carry

    lax.fori_loop(0, steps, forward_step, 0)
    arrive(k_own, cot_sems.at[0])
    arrive(k_other, cot_sems.at[1])

    bias, own_coef, other_coef = (vectors[i : i + 1, :] for i in range(3))
    c = 0.7978845608028654
    block = 32

    def rows_of(i, sums):
        rows = pl.ds(pl.multiple_of(i * block, block), block)
        x = total[rows, :] + bias
        x2 = x * x
        t = jnp.tanh(c * (x + 0.044715 * (x2 * x)))
        half = 0.5 * (1.0 + t)
        act = (x * half).astype(BF16)
        slope = half + (0.5 * c) * x * (1.0 - t * t) * (1.0 + (3.0 * 0.044715) * x2)
        k0 = k_own[rows, :].astype(F32)
        k1 = k_other[rows, :].astype(F32)
        dpre = ((own_coef * k0 + other_coef * k1) * slope).astype(BF16)
        act_out[rows, :] = act
        dpre_out[rows, :] = dpre
        actf = act.astype(F32)

        def fold(v):
            return jnp.sum(v.reshape(block // 8, 8, v.shape[1]), axis=0)

        return (
            sums[0] + fold(dpre.astype(F32)),
            sums[1] + fold(k0 * actf),
            sums[2] + fold(k1 * actf),
        )

    zero = jnp.zeros((8, total.shape[1]), F32)
    sums = lax.fori_loop(0, images // block, rows_of, (zero, zero, zero))
    for i in range(3):
        sums_out[i : i + 1, :] = jnp.sum(sums[i], axis=0, keepdims=True)
    keep_out[...] = dpre_out[: images // 2]
    send_out[...] = dpre_out[images // 2 :]

    def product(k):
        return lax.dot_general(
            held[k], dpre_out[...], (((0,), (0,)), ((), ())), preferred_element_type=F32
        )

    def last_steps(k, carry):
        made = product(k).astype(BF16)
        for i in range(chunks):
            low[k - per, i] = made[:, columns(i)]
        for s in range(1, count):

            @pl.when(k // per == s)
            def _(s=s):
                rows = pl.ds(pl.multiple_of((k - s * per) * tile, tile), tile)
                for i in range(chunks):
                    pltpu.make_async_copy(low.at[k - per, i], outs[i][s].at[rows, :], out_sems.at[k]).start()

        return carry

    def first_steps(k, carry):
        made = product(k)
        rows = pl.ds(pl.multiple_of(k * tile, tile), tile)
        for i in range(chunks):
            high[k, i] = made[:, columns(i)]
            pltpu.make_async_copy(high.at[k, i], outs[i][0].at[rows, :], out_sems.at[k]).start()
        return carry

    if count > 1:
        lax.fori_loop(per, steps, last_steps, 0)
    lax.fori_loop(0, per, first_steps, 0)
    for k in range(steps):
        arrive(high.at[k] if k < per else low.at[k - per], out_sems.at[k])


def chunk(roles, feats, pieces, vectors, cots):
    images = len(feats) * feats[-1][-1][0].shape[0]
    units = pieces[0][0][0].shape[1]
    width = units * len(pieces)
    depth = sum(part.shape[1] for part, _ in feats[0])
    starts = [start for block in feats for _, start in block]
    count = len(pieces[0])
    height = pieces[0][0][0].shape[0]
    tile = tile_of(height)
    steps, per = depth // tile, height // tile
    terms = [term for chunk in pieces for piece in chunk for term in piece]
    anywhere = pl.BlockSpec(memory_space=pl.ANY)
    vmem = pl.BlockSpec(memory_space=pltpu.VMEM)
    kinds = ([F32] + [BF16] * (count - 1)) * len(pieces)
    return pl.pallas_call(
        functools.partial(chunk_kernel, [[len(p) for p in chunk] for chunk in pieces], starts, [c for _, c in cots]),
        in_specs=[pl.BlockSpec(memory_space=pltpu.SMEM), vmem]
        + [anywhere] * (len(cots) + len(feats) * HALVES + len(terms)),
        out_specs=[vmem] * 4 + [anywhere] * len(kinds),
        out_shape=[
            jax.ShapeDtypeStruct((images, width), BF16),
            jax.ShapeDtypeStruct((images // 2, width), BF16),
            jax.ShapeDtypeStruct((images // 2, width), BF16),
            jax.ShapeDtypeStruct((8, width), F32),
        ]
        + [jax.ShapeDtypeStruct((height, units), kind) for kind in kinds],
        scratch_shapes=[
            pltpu.VMEM((steps, images, tile), BF16),
            pltpu.VMEM((steps, tile, width), BF16),
            pltpu.VMEM((images, width), F32),
            pltpu.VMEM((images, width), BF16),
            pltpu.VMEM((images, width), BF16),
            pltpu.VMEM((images, width), BF16),
            pltpu.VMEM((per, len(pieces), tile, units), F32),
            pltpu.VMEM((max(steps - per, 1), len(pieces), tile, units), BF16),
            pltpu.SemaphoreType.DMA((steps,)),
            pltpu.SemaphoreType.DMA((steps,)),
            pltpu.SemaphoreType.DMA((2,)),
            pltpu.SemaphoreType.DMA((steps,)),
        ],
        compiler_params=params(),
        cost_estimate=SMALL,
        name="chunk",
    )(roles, vectors, *[cot for cot, _ in cots], *[part for block in feats for part, _ in block], *terms)


def back_kernel(count, *refs):
    outs = refs[-14:-6]
    grad, weight, made, grad_sems, w_sems, out_sems = refs[-6:]
    sources = (len(refs) - 14) // (1 + count)
    grads, pieces = refs[:sources], refs[sources:-14]
    slots, tile, total = weight.shape
    units = total // sources
    steps = made.shape[0]
    per = steps // count
    share = made.shape[1] // len(outs)

    def columns(j):
        return slice(j * units, (j + 1) * units)

    def begin(k):
        slot = lax.rem(k, slots)
        for s in range(count):

            @pl.when(k // per == s)
            def _(s=s):
                rows = pl.ds(pl.multiple_of((k - s * per) * tile, tile), tile)
                for j in range(sources):
                    piece = pieces[j * count + s].at[rows, :]
                    pltpu.make_async_copy(piece, weight.at[slot, :, columns(j)], w_sems.at[slot]).start()

    def arrive(target, sem):
        pltpu.make_async_copy(target, target, sem).wait()

    copies = []
    for j in range(sources):
        copies.append(pltpu.make_async_copy(grads[j], grad.at[:, columns(j)], grad_sems.at[j]))
        copies[-1].start()
    ahead = min(slots - 1, steps)
    for k in range(ahead):
        begin(jnp.int32(k))
    for copy in copies:
        copy.wait()

    def step(k, carry):
        pl.when(k + ahead < steps)(lambda: begin(k + ahead))
        slot = lax.rem(k, slots)
        arrive(weight.at[slot], w_sems.at[slot])
        made[k] = lax.dot_general(
            grad[...], weight[slot], (((1,), (1,)), ((), ())), preferred_element_type=F32
        ).astype(BF16)
        cols = pl.ds(pl.multiple_of(k * tile, tile), tile)
        for i, out in enumerate(outs):
            source = made.at[k, pl.ds(i * share, share), :]
            pltpu.make_async_copy(source, out.at[:, cols], out_sems.at[k]).start()
        return carry

    lax.fori_loop(0, steps, step, 0)
    for k in range(steps):
        arrive(made.at[k], out_sems.at[k])


def back(grads, pieces):
    images, units = grads[0].shape
    count = len(pieces[0])
    height = pieces[0][0].shape[0]
    depth = height * count
    tile = next(t for t in (768, 512, 384, 256, 128) if height % t == 0)
    steps = depth // tile
    total = units * len(grads)
    terms = [piece for chunk in pieces for piece in chunk]
    anywhere = pl.BlockSpec(memory_space=pl.ANY)
    return pl.pallas_call(
        functools.partial(back_kernel, count),
        in_specs=[anywhere] * (len(grads) + len(terms)),
        out_specs=[anywhere] * 8,
        out_shape=[jax.ShapeDtypeStruct((images // 8, depth), BF16)] * 8,
        scratch_shapes=[
            pltpu.VMEM((images, total), BF16),
            pltpu.VMEM((AHEAD + 1, tile, total), BF16),
            pltpu.VMEM((steps, images, tile), BF16),
            pltpu.SemaphoreType.DMA((len(grads),)),
            pltpu.SemaphoreType.DMA((AHEAD + 1,)),
            pltpu.SemaphoreType.DMA((steps,)),
        ],
        compiler_params=params(),
        cost_estimate=SMALL,
        name="back",
    )(*grads, *terms)


def either(flag, value, axis):
    return jnp.where(flag, jnp.flip(value, axis), value)


class Program:
    def __init__(self, convmaps, group, alpha1, weight, bias, alpha2, cotangent):
        self.order = Order()
        self.convmaps, self.group, self.weight = convmaps, group, weight
        self.count, _, self.places, self.channels = convmaps.shape
        batch_id = lax.axis_index("batch")
        tower_id = lax.axis_index("tower")
        self.x, self.z = batch_id % 2, batch_id // 2
        self.y, self.core = tower_id // 2, tower_id % 2
        self.depth, self.width = weight.shape
        self.units = self.width // 2
        self.n = self.units // (4 if is_line() else 2)
        self.chunks = self.units // self.n
        self.images = 8 * self.count
        self.mine, self.theirs = self.x * self.units, (1 - self.x) * self.units
        units = self.units
        second = lax.dynamic_slice_in_dim(alpha2, self.mine, units, 1)
        self.own_coef = lax.dynamic_index_in_dim(second, self.y, 0, keepdims=True).astype(F32)
        self.cross = lax.dynamic_index_in_dim(second, 1 - self.y, 0, keepdims=True)
        own_bias = lax.dynamic_slice_in_dim(bias, self.mine, units, 0)[None, :].astype(F32)
        self.own_bias = own_bias
        cot = cotangent.reshape(2, 2, self.count, self.width)
        cot = either(self.core == 1, either(self.y == 1, cot, 0), 1).swapaxes(0, 1)
        cot = cot.reshape(-1, self.width)
        self.cot_mine = lax.dynamic_slice_in_dim(cot, self.mine, units, 1)
        self.cot_theirs = lax.dynamic_slice_in_dim(cot, self.theirs, units, 1)
        places = jnp.arange(POOLED)
        if is_line():
            places = places.reshape(4, -1)[line_order(self.z)].reshape(-1)
        self.table = pool_table(places)
        self.first = either(self.y == 1, alpha1.astype(F32), 0).reshape(4, self.channels)
        self.is_outer = (self.z == 0) | (self.z == 3)
        self.roles = jnp.stack([self.is_outer.astype(jnp.int32), 1 - self.core])
        self.cots = {}
        self.places_of = jnp.stack([self.x, self.y, self.core]).astype(jnp.int32)
        self.weight_grad = ()
        self.acts, self.grads, self.far_grads, self.sums = {}, {}, {}, {}
        self.stitched, self.crossed = {}, {}

    def then(self, value):
        return self.order.then(value)

    def did(self, value):
        return self.order.did(value)

    def keep_cross(self, came):
        cross_back = self.did(self.then(came)).astype(F32)
        zeros = jnp.zeros((5, self.units), F32)
        self.vectors = jnp.concatenate([self.own_bias, self.own_coef, cross_back, zeros])
        self.cross = self.cross.astype(F32)

    def cols(self, j):
        return slice(j * self.n, (j + 1) * self.n)

    def span(self, js):
        return slice(js[0] * self.n, (js[-1] + 1) * self.n)

    def weight_part(self, start, j, many=1):
        return lax.dynamic_slice(self.weight, (0, start + j * self.n), (self.depth, many * self.n))

    def swap_weight(self, j, many=1):
        return self.send(x_swap, self.weight_part(self.theirs, j, many))

    def slab_weight(self, j, came):
        a, b = self.weight_part(self.mine, j), self.then(came)
        return self.did(jnp.where(self.x == 0, jnp.concatenate([a, b]), jnp.concatenate([b, a])))

    def swap_cotangents(self, js):
        return self.send(x_swap, self.cot_theirs[:, self.span(js)])

    def cots_of(self, j):
        here, there = self.cots[j]
        first = (j - min(i for i in self.cots if self.cots[i][0] is here)) * self.n
        return [(self.cot_mine, j * self.n), (here, first), (self.cot_across, j * self.n), (there, first)]

    def send(self, move, value, *args):
        return move(self.did(self.then(value)), *args)

    def chunk(self, j, feats, pieces):
        act, keep, send, sums, *products = chunk(
            self.roles,
            feats,
            [pieces],
            self.then(self.vectors[:, self.cols(j)]),
            self.cots_of(j),
        )
        self.did(act)
        self.acts[j], self.grads[j], self.far_grads[j], self.sums[j] = act, keep, send, sums
        return products

    def stitch(self, j, came):
        cols = self.cols(j)
        other_act = jnp.flip(self.then(came).reshape(4, 2, self.count, self.n), 1).reshape(self.images, self.n)
        mix = self.own_coef[:, cols] * self.acts[j].astype(F32) + self.cross[:, cols] * other_act.astype(F32)
        mix = self.did(mix.astype(BF16)).reshape(2, 2, 2 * self.count, self.n)
        self.stitched[j] = mix[:, 0].reshape(-1, self.n)
        return mix[:, 1].reshape(-1, self.n)

    def leaving(self, slab):
        return lax.dynamic_slice_in_dim(slab, (1 - self.x) * self.depth, self.depth, 0).astype(BF16)

    def store(self, j, rows, came):
        shape = (self.depth, self.width)
        made = store(self.then(rows), came, self.places_of, j, self.chunks, shape, self.weight_grad)
        self.weight_grad = (self.did(made),)

    def activations(self):
        own, other = ([parts[j] for j in range(self.chunks)] for parts in (self.stitched, self.crossed))
        return place_rows(self.places_of, [self.then(own[0])] + own[1:], other)

    def unit_sums(self):
        return jnp.concatenate([self.sums[j][:3] for j in range(self.chunks)], axis=1)

    def small_grads(self, sums):
        mine, far = sums[:3], sums[3:6]
        wide = jnp.where(
            self.x == 0, jnp.concatenate([mine, far], -1), jnp.concatenate([far, mine], -1)
        )
        return wide[0], either(self.y == 1, wide[1:3], 0)

    def back(self, came_grads, pieces, came_pieces):
        chunks = range(self.chunks)
        grads = [self.grads[j] for j in chunks] + [came_grads[j] for j in chunks]
        parts = back(
            [self.then(grads[0])] + grads[1:],
            [pieces[j] for j in chunks] + [came_pieces[j] for j in chunks],
        )
        self.did(parts[0])
        return parts[:4], parts[4:]

    def add(self, keep, came):
        return self.did((keep.astype(F32) + self.then(came).astype(F32)).astype(BF16))

    def first_grad(self, i, keep, came, other, pooled):
        return self.did(first_grad(pooled, self.then(keep), came, other, i * keep.shape[0]))

    def by_tower(self, partial):
        return either(self.y == 1, partial.reshape(2, 2, self.channels), 0)

    def unpool(self, i, keep, came, other, before=()):
        at = i * keep.shape[0]
        return self.did(
            unpool(
                self.then(keep),
                came,
                other,
                self.group,
                self.table,
                self.first,
                self.places,
                at,
                self.count,
                before,
            )
        )


def line_program(p):
    then, did = p.then, p.did
    came, blocks, near, inner, outer, first_out, last_out = {}, {}, {}, {}, {}, {}, {}
    total, into, crossed, middle, final, slab_came = {}, {}, {}, {}, {}, {}
    from_own, swapped = {}, {}

    def send(kind, value):
        return p.send(line, value, kind)

    def arrive(value):
        return did(then(value))

    def block(j):
        blocks[j] = p.slab_weight(j, came[j])

    def pieces(j):
        beside = (near[j],) if j < 2 else (from_own[j], swapped[j])
        return [(blocks[j],), beside, (first_out[j], inner[j]), (last_out[j], outer[j])]

    def part(j, s):
        return total[j][s]

    def payload(inward, outward):
        return did(jnp.where(p.is_outer, then(inward), outward))

    def ends(value):
        return send("near", value)

    def inward(j, s):
        return send("inward", then(part(j, s)))

    def plus(j, s, value):
        return (part(j, s).astype(F32) + then(value).astype(F32)).astype(BF16)

    def edge(j):
        return jnp.where(
            p.is_outer, then(final[j]).astype(F32), into[j, 1].astype(F32) + middle[j].astype(F32)
        )

    def pick(a, b):
        return did(jnp.where(p.is_outer, then(a), b))

    def core_swap(j, s):
        came_pieces[j, s] = p.send(c_swap, picked[j, s])

    def core_came(j, s):
        came_pieces[j, s] = arrive(came_pieces[j, s])

    picked, came_pieces, came_grads = {}, {}, {}

    def far_end(j):
        return plus(j, 3, into[j, 3])

    image_blocks = p.count // IMAGE_BLOCK
    cuts = [0, image_blocks // 4, image_blocks]

    def pool_part(i, before=()):
        made = pool(
            p.convmaps, p.group, then(p.table), p.first, cuts[i], cuts[i + 1] - cuts[i], before
        )
        did(made[0])
        return made

    came[0] = p.swap_weight(0)
    came[1] = p.swap_weight(1)
    cross_came = p.send(y_swap, p.cross)
    made = pool_part(0)
    came[0] = arrive(came[0])
    block(0)
    near[0] = ends(blocks[0])
    inner[0] = send("middle", blocks[0])
    p.keep_cross(cross_came)
    came[1] = arrive(came[1])
    came_pair = p.swap_weight(2, 2)
    p.cot_across = p.send(y_swap, p.cot_mine)
    cot_came = p.swap_cotangents([0, 1])
    block(1)
    kept_a, kept_b, sent_a, sent_b, pooled = pool_part(1, made)
    near[0] = arrive(near[0])
    near[1] = ends(blocks[1])
    inner[0] = arrive(inner[0])
    inner[1] = send("middle", blocks[1])
    came_pair = arrive(came_pair)
    p.cot_across = arrive(p.cot_across)
    cot_came = arrive(cot_came)
    x_a = p.send(x_swap, kept_a)
    y_a = p.send(y_swap, sent_a)
    came[2], came[3] = came_pair[:, : p.n], came_pair[:, p.n :]
    block(2)
    block(3)
    near[1] = arrive(near[1])
    first_out[0] = send("outward", inner[0])
    inner[1] = arrive(inner[1])
    outer[0] = send("middle", near[0])
    x_a = arrive(x_a)
    x_b = p.send(x_swap, kept_b)
    y_a = arrive(y_a)
    y_b = p.send(y_swap, sent_b)
    c_kept = [both_cores(arrive(kept_a)), both_cores(arrive(kept_b))]
    c_x_a, c_y_a = both_cores(x_a), both_cores(y_a)
    first_out[0] = arrive(first_out[0])
    first_out[1] = send("outward", inner[1])
    outer[0] = arrive(outer[0])
    outer[1] = send("middle", near[1])
    x_b = arrive(x_b)
    x_y_a = p.send(x_swap, y_a)
    y_b = arrive(y_b)
    cot_crossed = p.send(y_swap, cot_came)
    c_x_b, c_y_b = both_cores(x_b), both_cores(y_b)
    value = payload(blocks[2], outer[0])
    first_out[1] = arrive(first_out[1])
    swapped[2] = last_out[0] = ends(value)
    outer[1] = arrive(outer[1])
    inner[2] = send("middle", blocks[2])
    x_y_a = arrive(x_y_a)
    x_y_b = p.send(x_swap, y_b)
    p.cots[0] = p.cots[1] = (cot_came, arrive(cot_crossed))
    for j in range(4):
        picked[j, 0] = blocks[j]
    picked[0, 1], picked[1, 1] = near[0], near[1]
    core_swap(0, 0)
    value = payload(blocks[3], outer[1])
    picked[0, 2] = pick(first_out[0], inner[0])
    picked[1, 2] = pick(first_out[1], inner[1])
    swapped[2] = last_out[0] = arrive(swapped[2])
    swapped[3] = last_out[1] = ends(value)
    inner[2] = arrive(inner[2])
    inner[3] = send("middle", blocks[3])
    x_y_b = arrive(x_y_b)
    core_came(0, 0)
    c_x_y_a = p.send(c_swap, x_y_a)
    core_swap(0, 1)
    core_swap(1, 0)
    picked[0, 3] = pick(last_out[0], outer[0])
    swapped[3] = last_out[1] = arrive(swapped[3])
    from_own[2] = send("outward", blocks[2])
    inner[3] = arrive(inner[3])
    outer[2] = send("middle", swapped[2])
    c_x_y_a = arrive(c_x_y_a)
    c_x_y_b = p.send(c_swap, x_y_b)
    core_came(0, 1)
    core_came(1, 0)
    c_x_y_b = arrive(c_x_y_b)
    feats = [
        [(kept_a, 0), (kept_b, 0)],
        [(y_a, 0), (y_b, 0)],
        [(x_a, 0), (x_b, 0)],
        [(x_y_a, 0), (x_y_b, 0)],
        [(c_kept[0], None), (c_kept[1], None)],
        [(c_y_a, None), (c_y_b, None)],
        [(c_x_a, None), (c_x_b, None)],
        [(c_x_y_a, 0), (c_x_y_b, 0)],
    ]
    total[0] = p.chunk(0, feats, pieces(0))
    value = payload(part(0, 3), inner[2])
    from_own[2] = arrive(from_own[2])
    into[0, 3] = first_out[2] = ends(value)
    outer[2] = arrive(outer[2])
    outer[3] = send("middle", swapped[3])
    cot_came = p.swap_cotangents([2, 3])
    act_came = p.send(y_swap, p.acts[0])
    core_swap(1, 1)
    total[1] = p.chunk(1, feats, pieces(1))
    value = payload(part(0, 2), outer[2])
    into[0, 3] = first_out[2] = arrive(into[0, 3])
    into[0, 2] = last_out[2] = ends(value)
    outer[3] = arrive(outer[3])
    crossed[0] = send("middle", far_end(0))
    cot_came = arrive(cot_came)
    act_came = arrive(act_came)
    cot_crossed = p.send(y_swap, cot_came)
    core_came(1, 1)
    core_swap(0, 2)
    core_swap(1, 2)
    value = payload(part(0, 1), blocks[3])
    mix = p.stitch(0, act_came)
    picked[1, 3] = pick(last_out[1], outer[1])
    picked[2, 1] = pick(from_own[2], swapped[2])
    into[0, 2] = last_out[2] = arrive(into[0, 2])
    into[0, 1] = from_own[3] = ends(value)
    crossed[0] = arrive(crossed[0])
    middle[0] = send("middle", plus(0, 2, into[0, 2]))
    p.cots[2] = p.cots[3] = (cot_came, arrive(cot_crossed))
    core_came(0, 2)
    core_came(1, 2)
    p.crossed[0] = p.send(x_swap, mix)
    act_came = p.send(y_swap, p.acts[1])
    core_swap(0, 3)
    total[2] = p.chunk(2, feats, pieces(2))
    value = payload(part(1, 3), inner[3])
    into[0, 1] = from_own[3] = arrive(into[0, 1])
    into[1, 3] = first_out[3] = ends(value)
    middle[0] = arrive(middle[0])
    p.crossed[0] = arrive(p.crossed[0])
    act_came = arrive(act_came)
    core_came(0, 3)
    act_came2 = p.send(y_swap, p.acts[2])
    core_swap(1, 3)
    core_swap(2, 0)
    core_swap(3, 0)
    value = payload(part(1, 2), outer[3])
    mix = p.stitch(1, act_came)
    picked[2, 2] = pick(first_out[2], inner[2])
    picked[2, 3] = pick(last_out[2], outer[2])
    picked[3, 1] = pick(from_own[3], swapped[3])
    into[1, 3] = first_out[3] = arrive(into[1, 3])
    into[1, 2] = last_out[3] = ends(value)
    for at in ((1, 3), (2, 0), (3, 0)):
        core_came(*at)
    crossed[1] = send("middle", far_end(1))
    act_came = arrive(act_came2)
    p.crossed[1] = p.send(x_swap, mix)
    core_swap(2, 1)
    core_swap(2, 2)
    value = payload(part(1, 1), plus(0, 1, crossed[0]))
    picked[3, 2] = pick(first_out[3], inner[3])
    mix = p.stitch(2, act_came)
    for j in range(3):
        came_grads[j] = arrive(p.send(c_swap, p.far_grads[j]))
    into[1, 2] = last_out[3] = arrive(into[1, 2])
    into[1, 1] = final[0] = ends(value)
    crossed[1] = arrive(crossed[1])
    middle[1] = send("middle", plus(1, 2, into[1, 2]))
    p.crossed[1] = arrive(p.crossed[1])
    core_came(2, 1)
    core_came(2, 2)
    p.crossed[2] = p.send(x_swap, mix)
    core_swap(2, 3)
    core_swap(3, 1)
    picked[3, 3] = pick(last_out[3], outer[3])
    total[3] = p.chunk(3, feats, pieces(3))
    value = payload(part(2, 3), plus(1, 1, crossed[1]))
    into[1, 1] = final[0] = arrive(into[1, 1])
    into[2, 3] = final[1] = ends(value)
    middle[1] = arrive(middle[1])
    p.crossed[2] = arrive(p.crossed[2])
    core_came(2, 3)
    core_came(3, 1)
    core_swap(3, 2)
    core_swap(3, 3)
    came_grads[3] = p.send(c_swap, p.far_grads[3])
    rows = {0: did(part(0, 0) + edge(0))}
    core_came(3, 2)
    core_came(3, 3)
    came_grads[3] = arrive(came_grads[3])
    slab_came[0] = p.send(x_swap, p.leaving(rows[0]))
    act_came = p.send(y_swap, p.acts[3])
    keep, leave = p.back(
        came_grads,
        [[picked[j, s] for s in range(4)] for j in range(4)],
        [[came_pieces[j, s] for s in range(4)] for j in range(4)],
    )
    came_x, own_y = {}, {}
    into[2, 3] = final[1] = arrive(into[2, 3])
    into[3, 3] = inward(3, 3)
    slab_came[0] = arrive(slab_came[0])
    crossed[2] = send("middle", far_end(2))
    came_x[0] = p.send(x_swap, leave[2])
    act_came = arrive(act_came)
    p.store(0, rows[0], slab_came[0])
    rows[1] = did(part(1, 0) + edge(1))
    mix = p.stitch(3, act_came)
    into[3, 3] = arrive(into[3, 3])
    into[2, 2] = inward(2, 2)
    crossed[2] = arrive(crossed[2])
    crossed[3] = send("middle", far_end(3))
    came_x[0] = arrive(came_x[0])
    came_x[1] = p.send(x_swap, leave[3])
    own_y[0] = p.send(y_swap, p.add(keep[2], came_x[0]))
    sums = did(then(p.unit_sums()))
    into[2, 2] = arrive(into[2, 2])
    into[3, 2] = inward(3, 2)
    crossed[3] = arrive(crossed[3])
    middle[2] = send("middle", plus(2, 2, into[2, 2]))
    came_x[1] = arrive(came_x[1])
    came_x[2] = p.send(x_swap, leave[0])
    own_y[0] = arrive(own_y[0])
    own_y[1] = p.send(y_swap, p.add(keep[3], came_x[1]))
    value = payload(part(2, 1), plus(2, 1, crossed[2]))
    into[3, 2] = arrive(into[3, 2])
    into[2, 1] = final[2] = ends(value)
    middle[2] = arrive(middle[2])
    middle[3] = send("middle", plus(3, 2, into[3, 2]))
    came_x[2] = arrive(came_x[2])
    came_x[3] = p.send(x_swap, leave[1])
    own_y[1] = arrive(own_y[1])
    value = payload(part(3, 1), plus(3, 1, crossed[3]))
    partial = p.first_grad(0, keep[0], came_x[2], own_y[0], pooled)
    grad = (p.unpool(0, keep[0], came_x[2], own_y[0]),)
    into[2, 1] = final[2] = arrive(into[2, 1])
    into[3, 1] = final[3] = ends(value)
    middle[3] = arrive(middle[3])
    came_x[3] = arrive(came_x[3])
    slab_came[1] = p.send(x_swap, p.leaving(rows[1]))
    rows[2] = did(part(2, 0) + edge(2))
    slab_came[2] = p.send(x_swap, p.leaving(rows[2]))
    p.crossed[3] = p.send(x_swap, mix)
    partial = partial + p.first_grad(1, keep[1], came_x[3], own_y[1], pooled)
    partial = did(p.by_tower(partial).reshape(1, -1))
    partial_came = p.send(c_swap, partial)
    grad = p.unpool(1, keep[1], came_x[3], own_y[1], grad)
    partial = did(partial + then(partial_came))
    second_came = p.send(y_swap, jnp.concatenate([sums[2:], partial]))
    into[3, 1] = final[3] = arrive(into[3, 1])
    rows[3] = did(part(3, 0) + edge(3))
    slab_came[1] = arrive(slab_came[1])
    slab_came[3] = p.send(x_swap, p.leaving(rows[3]))
    second_came = arrive(second_came)
    sums = did(jnp.concatenate([sums[:2], second_came[:1], partial + second_came[1:]]))
    sums_came = p.send(flipped, sums, "batch", 2)
    p.store(1, rows[1], slab_came[1])
    sums = did(sums + then(sums_came))
    sums_came = p.send(flipped, sums, "batch", 4)
    slab_came[2] = arrive(slab_came[2])
    p.store(2, rows[2], slab_came[2])
    p.crossed[3] = arrive(p.crossed[3])
    activations = did(p.activations())
    sums = did(sums + then(sums_came))
    slab_came[3] = arrive(slab_came[3])
    sums_came = p.send(x_swap, sums)
    p.store(3, rows[3], slab_came[3])
    sums_came = then(sums_came)
    bias_grad, alpha2_grad = p.small_grads(jnp.concatenate([sums[:3], sums_came[:3]]))
    alpha1_grad = (sums[3] + sums_came[3]).reshape(2, 2, p.channels)
    input_grad = jnp.swapaxes(grad, 1, 2)
    return (activations, input_grad, p.weight_grad[0], bias_grad, alpha1_grad, alpha2_grad)


def plain_program(p):
    groups = slab_groups()
    p.keep_cross(p.send(y_swap, p.cross))
    p.cot_across = p.send(y_swap, p.cot_mine)
    *features, pooled = pool(p.convmaps, p.group, p.table, p.first, 0, p.count // IMAGE_BLOCK)
    feats = [features[:HALVES], [y_swap(part) for part in features[HALVES:]]]
    feats += [[x_swap(part) for part in block] for block in feats]
    feats += [[c_swap(part) for part in block] for block in feats]
    feats = [[(part, 0) for part in block] for block in feats]
    chunks = []
    for j in range(p.chunks):
        came = p.swap_cotangents([j])
        p.cots[j] = (came, p.send(y_swap, came))
        block = p.slab_weight(j, p.swap_weight(j))
        rows = lax.all_gather(block, "batch", axis=0, tiled=True, axis_index_groups=groups)
        chunks.append([(rows,)])
        [total] = p.chunk(j, feats, chunks[j])
        slab = lax.psum_scatter(total, "batch", scatter_dimension=0, tiled=True, axis_index_groups=groups)
        p.store(j, slab, p.send(x_swap, p.leaving(slab)))
        p.crossed[j] = p.send(x_swap, p.stitch(j, p.send(y_swap, p.acts[j])))
    sums = lax.psum(p.unit_sums(), "batch", axis_index_groups=groups)
    far = x_swap(sums)
    second = y_swap(jnp.concatenate([sums[2:], far[2:]]))
    bias_grad, alpha2_grad = p.small_grads(
        jnp.concatenate([sums[:2], second[:1], far[:2], second[1:]])
    )
    own_pieces = [[term for [term] in chunk] for chunk in chunks]
    keep, leave = p.back(
        [c_swap(p.far_grads[j]) for j in range(p.chunks)],
        own_pieces,
        [[c_swap(term) for term in chunk] for chunk in own_pieces],
    )
    partial, grad = 0.0, ()
    for i in range(2):
        other = y_swap(p.add(keep[2 + i], x_swap(leave[2 + i])))
        came = x_swap(leave[i])
        partial = partial + p.first_grad(i, keep[i], came, other, pooled)
        grad = (p.unpool(i, keep[i], came, other, grad),)
    alpha1_grad = lax.psum(p.by_tower(partial), ("batch", "tower"))
    input_grad = jnp.swapaxes(grad[0], 1, 2)
    return (p.activations(), input_grad, p.weight_grad[0], bias_grad, alpha1_grad, alpha2_grad)


def shards(*args):
    return (line_program if is_line() else plain_program)(Program(*args))


def solution(mesh):
    in_specs = (
        P(("batch", "tower"), None, None, None),
        P(("batch", "tower")),
        P(),
        P("batch", "tower"),
        P("tower"),
        P(None, "tower"),
        P("batch", "tower"),
    )
    out_specs = (
        P("batch", "tower"),
        P(("batch", "tower"), None, None, None),
        P("batch", "tower"),
        P("tower"),
        P(),
        P(None, "tower"),
    )
    return jax.shard_map(shards, mesh=mesh, in_specs=in_specs, out_specs=out_specs, check_vma=False)
```

```python
import functools

import jax
import jax.numpy as jnp
from jax import lax
from jax.experimental import pallas as pl
from jax.experimental.pallas import tpu as pltpu
from jax.sharding import PartitionSpec as P

F32 = jnp.float32
BF16 = jnp.bfloat16
POOLED = 36
PITCH = 48
LANES = 128
VMEM_LIMIT = 56 * 1024 * 1024
SMALL = pl.CostEstimate(flops=1000, bytes_accessed=1000, transcendentals=0)
AHEAD = 2
IMAGE_BLOCK = 16
HALVES = 2


def params():
    return pltpu.CompilerParams(vmem_limit_bytes=VMEM_LIMIT)


def flipped(value, axis, bit):
    pairs = [(source, source ^ bit) for source in range(lax.axis_size(axis))]
    return lax.ppermute(value, axis, pairs)


def x_swap(value):
    return flipped(value, "batch", 1)


def y_swap(value):
    return flipped(value, "tower", 2)


def c_swap(value):
    return flipped(value, "tower", 1)


def line(value, kind):
    steps = {
        "near": ((0, 1), (1, 0), (2, 3), (3, 2)),
        "middle": ((1, 2), (2, 1)),
        "outward": ((1, 0), (2, 3)),
        "inward": ((0, 1), (3, 2)),
    }[kind]
    pairs = [(2 * a + x, 2 * b + x) for a, b in steps for x in range(2)]
    return lax.ppermute(value, "batch", pairs)


def slab_groups():
    size = lax.axis_size("batch")
    return [list(range(x, size, 2)) for x in range(2)]


def after(value, *others):
    return lax.optimization_barrier((value, *others))[0]


class Order:
    def __init__(self):
        self.last = None

    def then(self, value):
        return value if self.last is None else after(value, self.last)

    def did(self, value):
        self.last = value
        return value


def is_line():
    return lax.axis_size("batch") == 8


def line_order(z):
    rows = jnp.array([[0, 1, 2, 3], [1, 0, 2, 3], [2, 3, 1, 0], [3, 2, 1, 0]])
    return rows[z]


def core_groups():
    return [[t, t + 1] for t in range(0, lax.axis_size("tower"), 2)]


def both_cores(value):
    return lax.all_gather(value, "tower", axis=0, tiled=True, axis_index_groups=core_groups())


def windows(order):
    map_pos = jnp.arange(169)[None, :]
    prow = (order // 6)[:, None]
    pcol = (order % 6)[:, None]
    qrow = map_pos // 13
    qcol = map_pos % 13
    inside = (
        (qrow >= 2 * prow) & (qrow <= 2 * prow + 2) & (qcol >= 2 * pcol) & (qcol <= 2 * pcol + 2)
    )
    return inside, (prow < 5) & (pcol < 5)


def spread_table(order):
    inside, small = windows(order)
    table = jnp.stack([inside, inside & small]).astype(BF16)
    table = jnp.pad(table, ((0, 0), (0, PITCH - POOLED), (0, 0)))
    both = table[:, None, :, :, None] * jnp.eye(2, dtype=BF16)[None, :, None, None, :]
    spread = jnp.swapaxes(both.reshape(2, 2 * PITCH, 338), 1, 2)
    return jnp.pad(jnp.concatenate([spread, spread], axis=2), ((0, 0), (0, 352 - 338), (0, 0)))


def mix_kernel(group, keep, first, summed, *refs):
    *feature_outs, pooled_out, own, other, pool0, pool1 = refs
    count, _, places, ch = summed.shape
    base = pl.program_id(0) * count

    def image(n, carry):
        scale = keep[group[base + n]]
        p0 = summed[n, 0] * scale
        p1 = summed[n, 1] * scale
        rows = pl.ds(pl.multiple_of(n * PITCH, PITCH), places)
        mixed0 = first[0:1, :] * p0 + first[1:2, :] * p1
        mixed1 = first[2:3, :] * p0 + first[3:4, :] * p1
        for hold, value in ((pool0, p0), (pool1, p1), (own, mixed0), (other, mixed1)):
            for h in range(ch // LANES):
                hold[h, rows, :] = value[:, h * LANES : (h + 1) * LANES]
        return carry

    lax.fori_loop(0, count, image, 0, unroll=2)
    per = POOLED // HALVES
    for p in range(POOLED):
        rows = pl.ds(p, count, stride=PITCH)
        for h in range(ch // LANES):
            lanes = slice(p * ch + h * LANES, p * ch + (h + 1) * LANES)
            part = slice((p % per) * ch + h * LANES, (p % per) * ch + (h + 1) * LANES)
            feature_outs[p // per][:, part] = own[h, rows, :].astype(BF16)
            feature_outs[HALVES + p // per][:, part] = other[h, rows, :].astype(BF16)
            pooled_out[0, :, lanes] = pool0[h, rows, :]
            pooled_out[1, :, lanes] = pool1[h, rows, :]


def mix(summed, group, keep, first):
    count, _, places, ch = summed.shape
    nb = IMAGE_BLOCK
    feats = places * ch
    features = [((count, feats // HALVES), BF16)] * (2 * HALVES)
    return pl.pallas_call(
        mix_kernel,
        grid_spec=pltpu.PrefetchScalarGridSpec(
            num_scalar_prefetch=1,
            grid=(count // nb,),
            in_specs=[
                pl.BlockSpec(keep.shape, lambda i, g: (0, 0, 0)),
                pl.BlockSpec((4, ch), lambda i, g: (0, 0)),
                pl.BlockSpec((nb, 2, places, ch), lambda i, g: (i, 0, 0, 0)),
            ],
            out_specs=[pl.BlockSpec((nb, feats // HALVES), lambda i, g: (i, 0))] * (2 * HALVES)
            + [pl.BlockSpec((2, nb, feats), lambda i, g: (0, i, 0))],
            scratch_shapes=[pltpu.VMEM((ch // LANES, nb * PITCH, LANES), F32)] * 4,
        ),
        out_shape=[jax.ShapeDtypeStruct(*f) for f in features]
        + [jax.ShapeDtypeStruct((2, count, feats), F32)],
        compiler_params=params(),
        cost_estimate=SMALL,
        name="mix",
    )(group, keep, first, summed)


def first_grad_kernel(pooled, keep, came, other, out):
    ch = out.shape[2]

    @pl.when(pl.program_id(0) == 0)
    def _():
        out[...] = jnp.zeros_like(out)

    for a in range(2):
        sums = [0.0, 0.0]
        for p in range(POOLED):
            lanes = slice(p * ch, (p + 1) * ch)
            if a == 0:
                grad = keep[:, lanes].astype(F32) + came[:, lanes].astype(F32)
            else:
                grad = other[:, lanes].astype(F32)
            for s in range(2):
                sums[s] = sums[s] + grad * pooled[s, :, lanes]
        for s in range(2):
            out[2 * a + s] += sums[s]


def first_grad(pooled, keep, came, other, at):
    images, feats = keep.shape
    ch = feats // POOLED
    nb = IMAGE_BLOCK
    rows = pl.BlockSpec((nb, feats), lambda i: (i, 0))
    sums = pl.pallas_call(
        first_grad_kernel,
        grid=(images // nb,),
        in_specs=[pl.BlockSpec((2, nb, feats), lambda i: (0, at // nb + i, 0)), rows, rows, rows],
        out_specs=pl.BlockSpec((4, nb, ch), lambda i: (0, 0, 0)),
        out_shape=jax.ShapeDtypeStruct((4, nb, ch), F32),
        compiler_params=params(),
        cost_estimate=SMALL,
        name="first_grad",
    )(pooled, keep, came, other)
    return jnp.sum(sums, axis=1)


def unpool_kernel(start, group, table, first, keep_in, came_in, other_in, *refs):
    out, own, other = refs[-3:]
    count = out.shape[0]
    base = start + pl.program_id(0) * count
    ch = out.shape[3]
    places = out.shape[1]

    @pl.when(pl.program_id(0) == 0)
    def _():
        own[...] = jnp.zeros_like(own)
        other[...] = jnp.zeros_like(other)

    for p in range(POOLED):
        for h in range(ch // LANES):
            lanes = slice(p * ch + h * LANES, p * ch + (h + 1) * LANES)
            rows = pl.ds(p, count, stride=PITCH)
            own[h, rows, :] = keep_in[:, lanes].astype(F32) + came_in[:, lanes].astype(F32)
            other[h, rows, :] = other_in[:, lanes].astype(F32)

    def image(n, carry):
        window = table[group[base + n]]
        rows = pl.ds(pl.multiple_of(n * PITCH, PITCH), PITCH)
        g0, g1 = (
            jnp.concatenate([hold[h, rows, :] for h in range(ch // LANES)], axis=1) for hold in (own, other)
        )
        highs, lows = [], []
        for s in range(2):
            grad = (first[s : s + 1, :] * g0 + first[2 + s : 3 + s, :] * g1) * (1.0 / 9.0)
            highs.append(grad.astype(BF16))
            lows.append((grad - highs[s].astype(F32)).astype(BF16))
        parts = jnp.concatenate(highs + lows, axis=0)
        spread = jnp.dot(window, parts, preferred_element_type=F32).astype(BF16)
        out[n] = spread[: 2 * places].reshape(places, 2, ch)
        return carry

    lax.fori_loop(0, count, image, 0, unroll=2)


def unpool(keep, came, other, group, table, first, places, at, count, before=()):
    images, feats = keep.shape
    ch = first.shape[1]
    nb = IMAGE_BLOCK
    rows = pl.BlockSpec((nb, feats), lambda i, g: (i, 0))
    return pl.pallas_call(
        functools.partial(unpool_kernel, at),
        grid_spec=pltpu.PrefetchScalarGridSpec(
            num_scalar_prefetch=1,
            grid=(images // nb,),
            in_specs=[
                pl.BlockSpec(table.shape, lambda i, g: (0, 0, 0)),
                pl.BlockSpec((4, ch), lambda i, g: (0, 0)),
                rows,
                rows,
                rows,
            ]
            + [pl.BlockSpec(memory_space=pl.ANY)] * len(before),
            out_specs=pl.BlockSpec((nb, places, 2, ch), lambda i, g: (at // nb + i, 0, 0, 0)),
            scratch_shapes=[pltpu.VMEM((ch // LANES, nb * PITCH, LANES), F32)] * 2,
        ),
        out_shape=jax.ShapeDtypeStruct((count, places, 2, ch), BF16),
        input_output_aliases={6: 0} if before else {},
        compiler_params=params(),
        cost_estimate=SMALL,
        name="unpool",
    )(group, table, first, keep, came, other, *before)


def store_kernel(chunk, chunks, x, own, came, *refs):
    out, stay, go, sems = refs[-4:]
    rows, width = came.shape

    def columns(at):
        return out.at[:, pl.ds(pl.multiple_of(at * width, width), width)]

    source = own.at[pl.ds(pl.multiple_of(x[0] * rows, rows), rows), :]
    read = pltpu.make_async_copy(source, stay, sems.at[0])
    read.start()
    go[...] = came[...].astype(F32)
    write = pltpu.make_async_copy(go, columns((1 - x[0]) * chunks + chunk), sems.at[1])
    write.start()
    read.wait()
    write_own = pltpu.make_async_copy(stay, columns(x[0] * chunks + chunk), sems.at[2])
    write_own.start()
    write.wait()
    write_own.wait()


def store(own, came, x, chunk, chunks, shape, before=()):
    anywhere = pl.BlockSpec(memory_space=pl.ANY)
    return pl.pallas_call(
        functools.partial(store_kernel, chunk, chunks),
        in_specs=[pl.BlockSpec(memory_space=pltpu.SMEM), anywhere, pl.BlockSpec(memory_space=pltpu.VMEM)]
        + [anywhere] * len(before),
        out_specs=anywhere,
        out_shape=jax.ShapeDtypeStruct(shape, F32),
        scratch_shapes=[pltpu.VMEM(came.shape, F32)] * 2 + [pltpu.SemaphoreType.DMA((3,))],
        input_output_aliases={3: 0} if before else {},
        compiler_params=params(),
        cost_estimate=SMALL,
        name="store",
    )(x, own, came, *before)


def place_rows_kernel(places, *refs):
    *parts, out, sem = refs
    height, width = parts[0].shape[0] // 4, parts[0].shape[1]
    chunks = len(parts) // 2
    x, y, core = places[0], places[1], places[2]
    copies = []
    for i, part in enumerate(parts):
        side, j = i // chunks, i % chunks
        col = (jnp.where(x == side, 0, chunks) + j) * width
        cols = pl.ds(pl.multiple_of(col, width), width)
        for b in range(4):
            row = (2 * ((b % 2) ^ y) + ((b // 2) ^ core)) * height
            target = out.at[pl.ds(pl.multiple_of(row, height), height), cols]
            copies.append(pltpu.make_async_copy(part.at[pl.ds(b * height, height), :], target, sem.at[i, b]))
            copies[-1].start()
    for copy in copies:
        copy.wait()


def place_rows(places, own, other):
    parts = own + other
    rows, width = parts[0].shape
    return pl.pallas_call(
        place_rows_kernel,
        in_specs=[pl.BlockSpec(memory_space=pltpu.SMEM)] + [pl.BlockSpec(memory_space=pltpu.VMEM)] * len(parts),
        out_specs=pl.BlockSpec(memory_space=pl.ANY),
        out_shape=jax.ShapeDtypeStruct((rows, width * len(parts)), BF16),
        scratch_shapes=[pltpu.SemaphoreType.DMA((len(parts), 4))],
        compiler_params=params(),
        cost_estimate=SMALL,
        name="place_rows",
    )(places, *parts)


def tile_of(rows):
    return next(t for t in (1152, 768, 576, 512, 384, 256, 128) if rows % t == 0)


def fetch(outer, terms, rows, target, sem):
    def copy(term):
        return pltpu.make_async_copy(term.at[rows, :], target, sem)

    if len(terms) == 1:
        copy(terms[0]).start()
    else:
        pl.when(outer == 1)(lambda: copy(terms[0]).start())
        pl.when(outer == 0)(lambda: copy(terms[1]).start())


def chunk_kernel(layout, starts, cot_cols, roles, vectors, *refs):
    chunks, count = len(layout), len(layout[0])
    cots, refs = refs[:4], refs[4:]
    blocks = len(starts) // HALVES
    feats, refs = refs[: blocks * HALVES], refs[blocks * HALVES :]
    at = 0
    pieces = []
    for counts in layout:
        pieces.append([])
        for many in counts:
            pieces[-1].append(refs[at : at + many])
            at += many
    act_out, keep_out, send_out, sums_out = refs[at : at + 4]
    outs = [refs[at + 4 + i * count : at + 4 + (i + 1) * count] for i in range(chunks)]
    held, weight, total, dpre_out, k_own, k_other, high, low, in_sems, w_sems, cot_sems, out_sems = refs[-12:]
    steps, images, tile = held.shape
    per = steps // count
    units = total.shape[1] // chunks
    half, height = steps // HALVES, images // blocks

    def columns(i):
        return slice(i * units, (i + 1) * units)

    def begin(k):
        for s in range(count):

            @pl.when(k // per == s)
            def _(s=s):
                rows = pl.ds(pl.multiple_of((k - s * per) * tile, tile), tile)
                for i in range(chunks):
                    fetch(roles[0], pieces[i][s], rows, weight.at[k, :, columns(i)], w_sems.at[k])

        for h in range(HALVES):

            @pl.when(k // half == h)
            def _(h=h):
                cols = pl.ds(pl.multiple_of((k - h * half) * tile, tile), tile)
                for r in range(blocks):
                    at = r * HALVES + h
                    start = starts[at]
                    if start is None:
                        start = pl.multiple_of(roles[1] * height, height)
                    part = feats[at].at[pl.ds(start, height), cols]
                    rows = pl.ds(r * height, height)
                    pltpu.make_async_copy(part, held.at[k, rows, :], in_sems.at[k]).start()

    def arrive(target, sem):
        pltpu.make_async_copy(target, target, sem).wait()

    ahead = min(AHEAD, steps)
    for k in range(ahead):
        begin(jnp.int32(k))
    for tower, target in enumerate((k_own, k_other)):
        for r in range(blocks):
            core, x, y = r // 4, r // 2 % 2, r % 2
            source, col = cots[2 * tower + x], cot_cols[2 * tower + x]
            rows = pl.ds((2 * core + (y ^ tower)) * height, height)
            source = source.at[rows, pl.ds(col, total.shape[1])]
            target_rows = target.at[pl.ds(r * height, height), :]
            pltpu.make_async_copy(source, target_rows, cot_sems.at[tower]).start()
    total[...] = jnp.zeros_like(total)

    def forward_step(k, carry):
        pl.when(k + ahead < steps)(lambda: begin(k + ahead))
        arrive(held.at[k], in_sems.at[k])
        arrive(weight.at[k], w_sems.at[k])
        total[...] += jnp.dot(held[k], weight[k], preferred_element_type=F32)
        return carry

    lax.fori_loop(0, steps, forward_step, 0)
    arrive(k_own, cot_sems.at[0])
    arrive(k_other, cot_sems.at[1])

    bias, own_coef, other_coef = (vectors[i : i + 1, :] for i in range(3))
    c = 0.7978845608028654
    block = 32

    def rows_of(i, sums):
        rows = pl.ds(pl.multiple_of(i * block, block), block)
        x = total[rows, :] + bias
        x2 = x * x
        t = jnp.tanh(c * (x + 0.044715 * (x2 * x)))
        half = 0.5 * (1.0 + t)
        act = (x * half).astype(BF16)
        slope = half + (0.5 * c) * x * (1.0 - t * t) * (1.0 + (3.0 * 0.044715) * x2)
        k0 = k_own[rows, :].astype(F32)
        k1 = k_other[rows, :].astype(F32)
        dpre = ((own_coef * k0 + other_coef * k1) * slope).astype(BF16)
        act_out[rows, :] = act
        dpre_out[rows, :] = dpre
        actf = act.astype(F32)

        def fold(v):
            return jnp.sum(v.reshape(block // 8, 8, v.shape[1]), axis=0)

        return (
            sums[0] + fold(dpre.astype(F32)),
            sums[1] + fold(k0 * actf),
            sums[2] + fold(k1 * actf),
        )

    zero = jnp.zeros((8, total.shape[1]), F32)
    sums = lax.fori_loop(0, images // block, rows_of, (zero, zero, zero))
    for i in range(3):
        sums_out[i : i + 1, :] = jnp.sum(sums[i], axis=0, keepdims=True)
    keep_out[...] = dpre_out[: images // 2]
    send_out[...] = dpre_out[images // 2 :]

    def product(k):
        return lax.dot_general(
            held[k], dpre_out[...], (((0,), (0,)), ((), ())), preferred_element_type=F32
        )

    def last_steps(k, carry):
        made = product(k).astype(BF16)
        for i in range(chunks):
            low[k - per, i] = made[:, columns(i)]
        for s in range(1, count):

            @pl.when(k // per == s)
            def _(s=s):
                rows = pl.ds(pl.multiple_of((k - s * per) * tile, tile), tile)
                for i in range(chunks):
                    pltpu.make_async_copy(low.at[k - per, i], outs[i][s].at[rows, :], out_sems.at[k]).start()

        return carry

    def first_steps(k, carry):
        made = product(k)
        rows = pl.ds(pl.multiple_of(k * tile, tile), tile)
        for i in range(chunks):
            high[k, i] = made[:, columns(i)]
            pltpu.make_async_copy(high.at[k, i], outs[i][0].at[rows, :], out_sems.at[k]).start()
        return carry

    if count > 1:
        lax.fori_loop(per, steps, last_steps, 0)
    lax.fori_loop(0, per, first_steps, 0)
    for k in range(steps):
        arrive(high.at[k] if k < per else low.at[k - per], out_sems.at[k])


def chunk(roles, feats, pieces, vectors, cots):
    images = len(feats) * feats[-1][-1][0].shape[0]
    units = pieces[0][0][0].shape[1]
    width = units * len(pieces)
    depth = sum(part.shape[1] for part, _ in feats[0])
    starts = [start for block in feats for _, start in block]
    count = len(pieces[0])
    height = pieces[0][0][0].shape[0]
    tile = tile_of(height)
    steps, per = depth // tile, height // tile
    terms = [term for chunk in pieces for piece in chunk for term in piece]
    anywhere = pl.BlockSpec(memory_space=pl.ANY)
    vmem = pl.BlockSpec(memory_space=pltpu.VMEM)
    kinds = ([F32] + [BF16] * (count - 1)) * len(pieces)
    return pl.pallas_call(
        functools.partial(chunk_kernel, [[len(p) for p in chunk] for chunk in pieces], starts, [c for _, c in cots]),
        in_specs=[pl.BlockSpec(memory_space=pltpu.SMEM), vmem]
        + [anywhere] * (len(cots) + len(feats) * HALVES + len(terms)),
        out_specs=[vmem] * 4 + [anywhere] * len(kinds),
        out_shape=[
            jax.ShapeDtypeStruct((images, width), BF16),
            jax.ShapeDtypeStruct((images // 2, width), BF16),
            jax.ShapeDtypeStruct((images // 2, width), BF16),
            jax.ShapeDtypeStruct((8, width), F32),
        ]
        + [jax.ShapeDtypeStruct((height, units), kind) for kind in kinds],
        scratch_shapes=[
            pltpu.VMEM((steps, images, tile), BF16),
            pltpu.VMEM((steps, tile, width), BF16),
            pltpu.VMEM((images, width), F32),
            pltpu.VMEM((images, width), BF16),
            pltpu.VMEM((images, width), BF16),
            pltpu.VMEM((images, width), BF16),
            pltpu.VMEM((per, len(pieces), tile, units), F32),
            pltpu.VMEM((max(steps - per, 1), len(pieces), tile, units), BF16),
            pltpu.SemaphoreType.DMA((steps,)),
            pltpu.SemaphoreType.DMA((steps,)),
            pltpu.SemaphoreType.DMA((2,)),
            pltpu.SemaphoreType.DMA((steps,)),
        ],
        compiler_params=params(),
        cost_estimate=SMALL,
        name="chunk",
    )(roles, vectors, *[cot for cot, _ in cots], *[part for block in feats for part, _ in block], *terms)


def back_kernel(layout, firsts, blocks, roles, *refs):
    outs = refs[-10:-6]
    grad, weight, made, grad_sems, w_sems, out_sems = refs[-6:]
    sources, count = len(layout), len(layout[0])
    grads = refs[:sources]
    at = sources
    pieces = []
    for counts in layout:
        pieces.append([])
        for many in counts:
            pieces[-1].append(refs[at : at + many])
            at += many
    slots, tile, total = weight.shape
    units = total // sources
    steps = made.shape[0]
    per = steps // count
    share = made.shape[1] // len(outs)

    def columns(j):
        return slice(j * units, (j + 1) * units)

    def begin(k):
        slot = lax.rem(k, slots)
        for s in range(count):

            @pl.when(k // per == s)
            def _(s=s):
                rows = pl.ds(pl.multiple_of((k - s * per) * tile, tile), tile)
                for j in range(sources):
                    fetch(roles[0], pieces[j][s], rows, weight.at[slot, :, columns(j)], w_sems.at[slot])

    def arrive(target, sem):
        pltpu.make_async_copy(target, target, sem).wait()

    copies = []
    for j in range(sources):
        for i, block in enumerate(blocks):
            rows = grad.shape[0] // len(blocks)
            source = grads[j].at[pl.ds(firsts[j] + block * rows, rows), :]
            target = grad.at[pl.ds(i * rows, rows), columns(j)]
            copies.append(pltpu.make_async_copy(source, target, grad_sems.at[j, i]))
            copies[-1].start()
    ahead = min(slots - 1, steps)
    for k in range(ahead):
        begin(jnp.int32(k))
    for copy in copies:
        copy.wait()

    def step(k, carry):
        pl.when(k + ahead < steps)(lambda: begin(k + ahead))
        slot = lax.rem(k, slots)
        arrive(weight.at[slot], w_sems.at[slot])
        made[k] = lax.dot_general(
            grad[...], weight[slot], (((1,), (1,)), ((), ())), preferred_element_type=F32
        ).astype(BF16)
        cols = pl.ds(pl.multiple_of(k * tile, tile), tile)
        for i, out in enumerate(outs):
            source = made.at[k, pl.ds(i * share, share), :]
            pltpu.make_async_copy(source, out.at[:, cols], out_sems.at[k]).start()
        return carry

    lax.fori_loop(0, steps, step, 0)
    for k in range(steps):
        arrive(made.at[k], out_sems.at[k])


def back(roles, grads, pieces, blocks):
    units = grads[0][0].shape[1]
    images = min(grad.shape[0] for grad, _ in grads) // 4 * len(blocks)
    count = len(pieces[0])
    height = pieces[0][0][0].shape[0]
    depth = height * count
    tile = next(t for t in (768, 512, 384, 256, 128) if height % t == 0)
    steps = depth // tile
    total = units * len(grads)
    terms = [term for chunk in pieces for piece in chunk for term in piece]
    layout = [[len(piece) for piece in chunk] for chunk in pieces]
    anywhere = pl.BlockSpec(memory_space=pl.ANY)
    return pl.pallas_call(
        functools.partial(back_kernel, layout, [row for _, row in grads], blocks),
        in_specs=[pl.BlockSpec(memory_space=pltpu.SMEM)] + [anywhere] * (len(grads) + len(terms)),
        out_specs=[anywhere] * 4,
        out_shape=[jax.ShapeDtypeStruct((images // 4, depth), BF16)] * 4,
        scratch_shapes=[
            pltpu.VMEM((images, total), BF16),
            pltpu.VMEM((AHEAD + 1, tile, total), BF16),
            pltpu.VMEM((steps, images, tile), BF16),
            pltpu.SemaphoreType.DMA((len(grads), len(blocks))),
            pltpu.SemaphoreType.DMA((AHEAD + 1,)),
            pltpu.SemaphoreType.DMA((steps,)),
        ],
        compiler_params=params(),
        cost_estimate=SMALL,
        name="back",
    )(roles, *[grad for grad, _ in grads], *terms)


def either(flag, value, axis):
    return jnp.where(flag, jnp.flip(value, axis), value)


class Program:
    def __init__(self, convmaps, group, alpha1, weight, bias, alpha2, cotangent):
        self.order = Order()
        self.convmaps, self.group, self.weight = convmaps, group, weight
        self.count, _, self.places, self.channels = convmaps.shape
        batch_id = lax.axis_index("batch")
        tower_id = lax.axis_index("tower")
        self.x, self.z = batch_id % 2, batch_id // 2
        self.y, self.core = tower_id // 2, tower_id % 2
        self.depth, self.width = weight.shape
        self.units = self.width // 2
        self.n = self.units // (4 if is_line() else 2)
        self.chunks = self.units // self.n
        self.images = 8 * self.count
        self.mine, self.theirs = self.x * self.units, (1 - self.x) * self.units
        units = self.units
        second = lax.dynamic_slice_in_dim(alpha2, self.mine, units, 1)
        self.own_coef = lax.dynamic_index_in_dim(second, self.y, 0, keepdims=True).astype(F32)
        self.cross = lax.dynamic_index_in_dim(second, 1 - self.y, 0, keepdims=True)
        own_bias = lax.dynamic_slice_in_dim(bias, self.mine, units, 0)[None, :].astype(F32)
        self.own_bias = own_bias
        self.cotangent = cotangent
        places = jnp.arange(POOLED)
        if is_line():
            places = places.reshape(4, -1)[line_order(self.z)].reshape(-1)
        self.table = spread_table(places)
        inside, small = windows(places)
        self.pool_table = inside.astype(BF16)
        keep = jnp.stack([jnp.ones_like(small), small]).astype(F32) * (1.0 / 9.0)
        self.keep = jnp.broadcast_to(keep, (2, POOLED, self.channels))
        self.first = either(self.y == 1, alpha1.astype(F32), 0).reshape(4, self.channels)
        self.is_outer = (self.z == 0) | (self.z == 3)
        self.roles = jnp.stack([self.is_outer.astype(jnp.int32), 1 - self.core])
        self.cots = {}
        self.places_of = jnp.stack([self.x, self.y, self.core]).astype(jnp.int32)
        self.weight_grad = ()
        self.acts, self.grads, self.far_grads, self.sums = {}, {}, {}, {}
        self.stitched, self.crossed = {}, {}

    def then(self, value):
        return self.order.then(value)

    def did(self, value):
        return self.order.did(value)

    def keep_cross(self, came):
        cross_back = self.did(self.then(came)).astype(F32)
        zeros = jnp.zeros((5, self.units), F32)
        self.vectors = jnp.concatenate([self.own_bias, self.own_coef, cross_back, zeros])
        self.cross = self.cross.astype(F32)

    def load_cotangents(self):
        cot = self.then(self.cotangent).reshape(2, 2, self.count, self.width)
        cot = either(self.core == 1, either(self.y == 1, cot, 0), 1).swapaxes(0, 1).reshape(-1, self.width)
        self.cot_mine = self.did(lax.dynamic_slice_in_dim(cot, self.mine, self.units, 1))
        self.cot_theirs = lax.dynamic_slice_in_dim(cot, self.theirs, self.units, 1)

    def pool(self):
        return jnp.einsum("pq,nsqc->nspc", self.pool_table, self.convmaps, preferred_element_type=F32)

    def mix(self, summed):
        return mix(summed, self.group, self.keep, self.first)

    def cols(self, j):
        return slice(j * self.n, (j + 1) * self.n)

    def span(self, js):
        return slice(js[0] * self.n, (js[-1] + 1) * self.n)

    def weight_part(self, start, j, many=1):
        return lax.dynamic_slice(self.then(self.weight), (0, start + j * self.n), (self.depth, many * self.n))

    def swap_weight(self, j, many=1):
        return self.send(x_swap, self.weight_part(self.theirs, j, many))

    def slab_weight(self, j, came):
        a, b = self.weight_part(self.mine, j), self.then(came)
        return self.did(jnp.where(self.x == 0, jnp.concatenate([a, b]), jnp.concatenate([b, a])))

    def swap_cotangents(self, js):
        return self.send(x_swap, self.cot_theirs[:, self.span(js)])

    def cots_of(self, j):
        here, there = self.cots[j]
        first = (j - min(i for i in self.cots if self.cots[i][0] is here)) * self.n
        return [(self.cot_mine, j * self.n), (here, first), (self.cot_across, j * self.n), (there, first)]

    def send(self, move, value, *args):
        return move(self.did(self.then(value)), *args)

    def chunk(self, j, feats, pieces):
        act, keep, send, sums, *products = chunk(
            self.roles,
            feats,
            [pieces],
            self.then(self.vectors[:, self.cols(j)]),
            self.cots_of(j),
        )
        self.did(act)
        self.acts[j], self.grads[j], self.far_grads[j], self.sums[j] = act, keep, send, sums
        return products

    def stitch(self, j, came):
        cols = self.cols(j)
        other_act = jnp.flip(self.then(came).reshape(4, 2, self.count, self.n), 1).reshape(self.images, self.n)
        mix = self.own_coef[:, cols] * self.acts[j].astype(F32) + self.cross[:, cols] * other_act.astype(F32)
        mix = self.did(mix.astype(BF16)).reshape(2, 2, 2 * self.count, self.n)
        self.stitched[j] = mix[:, 0].reshape(-1, self.n)
        return mix[:, 1].reshape(-1, self.n)

    def leaving(self, slab):
        return lax.dynamic_slice_in_dim(slab, (1 - self.x) * self.depth, self.depth, 0).astype(BF16)

    def store(self, j, rows, came):
        shape = (self.depth, self.width)
        made = store(self.then(rows), came, self.places_of, j, self.chunks, shape, self.weight_grad)
        self.weight_grad = (self.did(made),)

    def activations(self):
        own, other = ([parts[j] for j in range(self.chunks)] for parts in (self.stitched, self.crossed))
        return place_rows(self.places_of, [self.then(own[0])] + own[1:], other)

    def unit_sums(self):
        return jnp.concatenate([self.sums[j][:3] for j in range(self.chunks)], axis=1)

    def small_grads(self, sums):
        mine, far = sums[:3], sums[3:6]
        wide = jnp.where(
            self.x == 0, jnp.concatenate([mine, far], -1), jnp.concatenate([far, mine], -1)
        )
        return wide[0], either(self.y == 1, wide[1:3], 0)

    def back(self, y, came_grads, pieces, came_pieces):
        chunks = range(self.chunks)
        grads = [(self.grads[j], 0) for j in chunks] + list(came_grads)
        grads[0] = (self.then(grads[0][0]), 0)
        parts = back(
            self.roles,
            grads,
            [pieces[j] for j in chunks] + [came_pieces[j] for j in chunks],
            [y, 2 + y],
        )
        self.did(parts[0])
        return parts[:2], parts[2:]

    def add(self, keep, came):
        return self.did((keep.astype(F32) + self.then(came).astype(F32)).astype(BF16))

    def first_grad(self, i, keep, came, other, pooled):
        return self.did(first_grad(pooled, self.then(keep), came, other, i * keep.shape[0]))

    def by_tower(self, partial):
        return either(self.y == 1, partial.reshape(2, 2, self.channels), 0)

    def unpool(self, i, keep, came, other, before=()):
        at = i * keep.shape[0]
        return self.did(
            unpool(
                self.then(keep),
                came,
                other,
                self.group,
                self.table,
                self.first,
                self.places,
                at,
                self.count,
                before,
            )
        )


def line_program(p):
    then, did = p.then, p.did
    came, blocks, near, inner, outer, first_out, last_out = {}, {}, {}, {}, {}, {}, {}
    total, into, crossed, middle, final, slab_came = {}, {}, {}, {}, {}, {}
    from_own, swapped = {}, {}

    def send(kind, value):
        return p.send(line, value, kind)

    def arrive(value):
        return did(then(value))

    def block(j):
        blocks[j] = p.slab_weight(j, came[j])

    def pieces(j):
        beside = (near[j],) if j < 2 else (from_own[j], swapped[j])
        return [(blocks[j],), beside, (first_out[j], inner[j]), (last_out[j], outer[j])]

    def part(j, s):
        return total[j][s]

    def payload(inward, outward):
        return did(jnp.where(p.is_outer, then(inward), outward))

    def ends(value):
        return send("near", value)

    def inward(j, s):
        return send("inward", then(part(j, s)))

    def plus(j, s, value):
        return (part(j, s).astype(F32) + then(value).astype(F32)).astype(BF16)

    def edge(j):
        return jnp.where(
            p.is_outer, then(final[j]).astype(F32), into[j, 1].astype(F32) + middle[j].astype(F32)
        )

    def pick(a, b):
        return did(jnp.where(p.is_outer, then(a), b))

    def core_swap(j, s):
        came_pieces[j, s] = p.send(c_swap, picked[j, s])

    def core_came(j, s):
        came_pieces[j, s] = arrive(came_pieces[j, s])

    picked, came_pieces = {}, {}

    def far_end(j):
        return plus(j, 3, into[j, 3])

    came[0] = p.swap_weight(0)
    came[1] = p.swap_weight(1)
    cross_came = p.send(y_swap, p.cross)
    came_pair = p.swap_weight(2, 2)
    p.load_cotangents()
    p.keep_cross(cross_came)
    came[0] = arrive(came[0])
    block(0)
    near[0] = ends(blocks[0])
    inner[0] = send("middle", blocks[0])
    p.cot_across = p.send(y_swap, p.cot_mine)
    p.pool_table = then(p.pool_table)
    summed = did(p.pool())
    came[1] = arrive(came[1])
    cot_came = p.swap_cotangents([0, 1])
    block(1)
    near[0] = arrive(near[0])
    near[1] = ends(blocks[1])
    inner[0] = arrive(inner[0])
    inner[1] = send("middle", blocks[1])
    kept_a, kept_b, sent_a, sent_b, pooled = p.mix(then(summed))
    did(kept_a)
    came_pair = arrive(came_pair)
    p.cot_across = arrive(p.cot_across)
    cot_came = arrive(cot_came)
    x_a = p.send(x_swap, kept_a)
    y_a = p.send(y_swap, sent_a)
    c_kept_a = p.send(c_swap, kept_a)
    came[2], came[3] = came_pair[:, : p.n], came_pair[:, p.n :]
    block(2)
    block(3)
    near[1] = arrive(near[1])
    first_out[0] = send("outward", inner[0])
    inner[1] = arrive(inner[1])
    outer[0] = send("middle", near[0])
    x_a = arrive(x_a)
    x_b = p.send(x_swap, kept_b)
    y_a = arrive(y_a)
    y_b = p.send(y_swap, sent_b)
    c_kept_a = arrive(c_kept_a)
    c_kept_b = p.send(c_swap, kept_b)
    first_out[0] = arrive(first_out[0])
    first_out[1] = send("outward", inner[1])
    outer[0] = arrive(outer[0])
    outer[1] = send("middle", near[1])
    x_b = arrive(x_b)
    x_y_a = p.send(x_swap, y_a)
    y_b = arrive(y_b)
    cot_crossed = p.send(y_swap, cot_came)
    c_kept_b = arrive(c_kept_b)
    c_x_a = p.send(c_swap, x_a)
    value = payload(blocks[2], outer[0])
    first_out[1] = arrive(first_out[1])
    swapped[2] = last_out[0] = ends(value)
    outer[1] = arrive(outer[1])
    inner[2] = send("middle", blocks[2])
    x_y_a = arrive(x_y_a)
    x_y_b = p.send(x_swap, y_b)
    p.cots[0] = p.cots[1] = (cot_came, arrive(cot_crossed))
    c_x_a = arrive(c_x_a)
    c_y_a = p.send(c_swap, y_a)
    c_x_b = p.send(c_swap, x_b)
    value = payload(blocks[3], outer[1])
    for j in range(4):
        picked[j, 0] = blocks[j]
    picked[0, 1], picked[1, 1] = near[0], near[1]
    picked[0, 2] = pick(first_out[0], inner[0])
    swapped[2] = last_out[0] = arrive(swapped[2])
    swapped[3] = last_out[1] = ends(value)
    inner[2] = arrive(inner[2])
    outer[2] = send("middle", swapped[2])
    x_y_b = arrive(x_y_b)
    c_y_a = arrive(c_y_a)
    c_x_b = arrive(c_x_b)
    c_y_b = p.send(c_swap, y_b)
    c_x_y_a = p.send(c_swap, x_y_a)
    c_x_y_b = p.send(c_swap, x_y_b)
    picked[1, 2] = pick(first_out[1], inner[1])
    swapped[3] = last_out[1] = arrive(swapped[3])
    from_own[2] = send("outward", blocks[2])
    c_y_b = arrive(c_y_b)
    c_x_y_a = arrive(c_x_y_a)
    c_x_y_b = arrive(c_x_y_b)
    core_swap(0, 0)
    core_swap(0, 1)
    core_swap(1, 0)
    feats = [
        [(kept_a, 0), (kept_b, 0)],
        [(y_a, 0), (y_b, 0)],
        [(x_a, 0), (x_b, 0)],
        [(x_y_a, 0), (x_y_b, 0)],
        [(c_kept_a, 0), (c_kept_b, 0)],
        [(c_y_a, 0), (c_y_b, 0)],
        [(c_x_a, 0), (c_x_b, 0)],
        [(c_x_y_a, 0), (c_x_y_b, 0)],
    ]
    total[0] = p.chunk(0, feats, pieces(0))
    value = payload(part(0, 3), inner[2])
    from_own[2] = arrive(from_own[2])
    into[0, 3] = first_out[2] = ends(value)
    for at in ((0, 0), (0, 1), (1, 0)):
        core_came(*at)
    outer[2] = arrive(outer[2])
    inner[3] = send("middle", blocks[3])
    cot_came = p.swap_cotangents([2, 3])
    act_came = p.send(y_swap, p.acts[0])
    core_swap(1, 1)
    total[1] = p.chunk(1, feats, pieces(1))
    value = payload(part(0, 2), outer[2])
    into[0, 3] = first_out[2] = arrive(into[0, 3])
    into[0, 2] = last_out[2] = ends(value)
    inner[3] = arrive(inner[3])
    outer[3] = send("middle", swapped[3])
    value = payload(part(0, 1), blocks[3])
    cot_came = arrive(cot_came)
    act_came = arrive(act_came)
    core_came(1, 1)
    cot_crossed = p.send(y_swap, cot_came)
    core_swap(0, 2)
    core_swap(1, 2)
    act_mix = p.stitch(0, act_came)
    picked[0, 3] = pick(last_out[0], outer[0])
    into[0, 2] = last_out[2] = arrive(into[0, 2])
    into[0, 1] = from_own[3] = ends(value)
    rest = did(far_end(0))
    outer[3] = arrive(outer[3])
    crossed[0] = send("middle", rest)
    p.cots[2] = p.cots[3] = (cot_came, arrive(cot_crossed))
    core_came(0, 2)
    core_came(1, 2)
    p.crossed[0] = p.send(x_swap, act_mix)
    act_came = p.send(y_swap, p.acts[1])
    core_swap(0, 3)
    total[2] = p.chunk(2, feats, pieces(2))
    value = payload(part(1, 3), inner[3])
    into[0, 1] = from_own[3] = arrive(into[0, 1])
    into[1, 3] = first_out[3] = ends(value)
    rest = did(plus(0, 2, into[0, 2]))
    picked[1, 3] = pick(last_out[1], outer[1])
    crossed[0] = arrive(crossed[0])
    middle[0] = send("middle", rest)
    p.crossed[0] = arrive(p.crossed[0])
    act_came = arrive(act_came)
    core_came(0, 3)
    act_came2 = p.send(y_swap, p.acts[2])
    core_swap(1, 3)
    core_swap(2, 0)
    value = payload(part(1, 2), outer[3])
    act_mix = p.stitch(1, act_came)
    picked[2, 1] = pick(from_own[2], swapped[2])
    picked[2, 2] = pick(first_out[2], inner[2])
    picked[3, 1] = pick(from_own[3], swapped[3])
    into[1, 3] = first_out[3] = arrive(into[1, 3])
    into[1, 2] = last_out[3] = ends(value)
    rest = did(far_end(1))
    value = payload(part(1, 1), plus(0, 1, crossed[0]))
    picked[2, 3] = pick(last_out[2], outer[2])
    middle[0] = arrive(middle[0])
    crossed[1] = send("middle", rest)
    act_came = arrive(act_came2)
    core_came(1, 3)
    core_came(2, 0)
    p.crossed[1] = p.send(x_swap, act_mix)
    core_swap(3, 0)
    core_swap(3, 1)
    act_mix = p.stitch(2, act_came)
    picked[3, 2] = pick(first_out[3], inner[3])
    far = did(jnp.concatenate([then(p.far_grads[0]), p.far_grads[1], p.far_grads[2]]))
    into[1, 2] = last_out[3] = arrive(into[1, 2])
    into[1, 1] = final[0] = ends(value)
    p.crossed[1] = arrive(p.crossed[1])
    core_came(3, 0)
    core_came(3, 1)
    p.crossed[2] = p.send(x_swap, act_mix)
    core_swap(2, 1)
    core_swap(2, 2)
    total[3] = p.chunk(3, feats, pieces(3))
    crossed[1] = arrive(crossed[1])
    value = payload(part(2, 3), plus(1, 1, crossed[1]))
    into[1, 1] = final[0] = arrive(into[1, 1])
    into[2, 3] = final[1] = ends(value)
    p.crossed[2] = arrive(p.crossed[2])
    core_came(2, 1)
    core_came(2, 2)
    core_swap(2, 3)
    core_swap(3, 2)
    far = p.send(c_swap, far)
    came_last = p.send(c_swap, last_out[3])
    middle[1] = send("middle", did(plus(1, 2, into[1, 2])))
    core_came(2, 3)
    came_outer = p.send(c_swap, outer[3])
    core_came(3, 2)
    far = arrive(far)
    far3 = p.send(c_swap, p.far_grads[3])
    rows = {0: did(part(0, 0) + edge(0))}
    came_last = arrive(came_last)
    slab_came[0] = p.send(x_swap, p.leaving(rows[0]))
    came_outer = arrive(came_outer)
    far3 = arrive(far3)
    act_came = p.send(y_swap, p.acts[3])
    third = far.shape[0] // 3
    came_grads = [(far, 0), (far, third), (far, 2 * third), (far3, 0)]
    picked[3, 3], came_pieces[3, 3] = (last_out[3], outer[3]), (came_last, came_outer)
    own_pieces, far_pieces = (
        [[terms if isinstance(terms := kind[j, s], tuple) else (terms,) for s in range(4)] for j in range(4)]
        for kind in (picked, came_pieces)
    )
    keep_far, leave_far = p.back(1, came_grads, own_pieces, far_pieces)
    came_far, came_x, own_y = {}, {}, {}
    into[2, 3] = final[1] = arrive(into[2, 3])
    into[3, 3] = inward(3, 3)
    slab_came[0] = arrive(slab_came[0])
    came_far[0] = p.send(x_swap, leave_far[0])
    act_came = arrive(act_came)
    rest = did(far_end(2))
    middle[1] = arrive(middle[1])
    crossed[2] = send("middle", rest)
    keep, leave = p.back(0, came_grads, own_pieces, far_pieces)
    into[3, 3] = arrive(into[3, 3])
    into[2, 2] = inward(2, 2)
    rest = did(far_end(3))
    came_far[0] = arrive(came_far[0])
    came_far[1] = p.send(x_swap, leave_far[1])
    crossed[2] = arrive(crossed[2])
    crossed[3] = send("middle", rest)
    own_y[0] = p.send(y_swap, p.add(keep_far[0], came_far[0]))
    sums = did(then(p.unit_sums()))
    act_mix = p.stitch(3, act_came)
    p.store(0, rows[0], slab_came[0])
    into[2, 2] = arrive(into[2, 2])
    into[3, 2] = inward(3, 2)
    rest = did(plus(2, 2, into[2, 2]))
    came_far[1] = arrive(came_far[1])
    came_x[0] = p.send(x_swap, leave[0])
    crossed[3] = arrive(crossed[3])
    middle[2] = send("middle", rest)
    own_y[0] = arrive(own_y[0])
    own_y[1] = p.send(y_swap, p.add(keep_far[1], came_far[1]))
    value = payload(part(2, 1), plus(2, 1, crossed[2]))
    rows[1] = did(part(1, 0) + edge(1))
    into[3, 2] = arrive(into[3, 2])
    into[2, 1] = final[2] = ends(value)
    rest = did(plus(3, 2, into[3, 2]))
    came_x[0] = arrive(came_x[0])
    came_x[1] = p.send(x_swap, leave[1])
    middle[2] = arrive(middle[2])
    middle[3] = send("middle", rest)
    own_y[1] = arrive(own_y[1])
    value = payload(part(3, 1), plus(3, 1, crossed[3]))
    partial = p.first_grad(0, keep[0], came_x[0], own_y[0], pooled)
    into[2, 1] = final[2] = arrive(into[2, 1])
    into[3, 1] = final[3] = ends(value)
    came_x[1] = arrive(came_x[1])
    slab_came[1] = p.send(x_swap, p.leaving(rows[1]))
    middle[3] = arrive(middle[3])
    rows[2] = did(part(2, 0) + edge(2))
    slab_came[2] = p.send(x_swap, p.leaving(rows[2]))
    p.crossed[3] = p.send(x_swap, act_mix)
    partial = partial + p.first_grad(1, keep[1], came_x[1], own_y[1], pooled)
    partial = did(p.by_tower(partial).reshape(1, -1))
    grad = (p.unpool(0, keep[0], came_x[0], own_y[0]),)
    into[3, 1] = final[3] = arrive(into[3, 1])
    rows[3] = did(part(3, 0) + edge(3))
    slab_came[3] = p.send(x_swap, p.leaving(rows[3]))
    partial_came = p.send(c_swap, partial)
    slab_came[1] = arrive(slab_came[1])
    p.store(1, rows[1], slab_came[1])
    partial = did(partial + then(partial_came))
    second_came = p.send(y_swap, jnp.concatenate([sums[2:], partial]))
    slab_came[2] = arrive(slab_came[2])
    p.store(2, rows[2], slab_came[2])
    second_came = arrive(second_came)
    sums = did(jnp.concatenate([sums[:2], second_came[:1], partial + second_came[1:]]))
    sums_came = p.send(flipped, sums, "batch", 2)
    grad = p.unpool(1, keep[1], came_x[1], own_y[1], grad)
    sums = did(sums + then(sums_came))
    sums_came = p.send(flipped, sums, "batch", 4)
    slab_came[3] = arrive(slab_came[3])
    p.store(3, rows[3], slab_came[3])
    sums = did(sums + then(sums_came))
    sums_came = p.send(x_swap, sums)
    p.crossed[3] = arrive(p.crossed[3])
    activations = did(p.activations())
    sums_came = then(sums_came)
    bias_grad, alpha2_grad = p.small_grads(jnp.concatenate([sums[:3], sums_came[:3]]))
    alpha1_grad = (sums[3] + sums_came[3]).reshape(2, 2, p.channels)
    input_grad = jnp.swapaxes(grad, 1, 2)
    return (activations, input_grad, p.weight_grad[0], bias_grad, alpha1_grad, alpha2_grad)


def plain_program(p):
    groups = slab_groups()
    p.keep_cross(p.send(y_swap, p.cross))
    p.load_cotangents()
    p.cot_across = p.send(y_swap, p.cot_mine)
    *features, pooled = p.mix(p.pool())
    feats = [features[:HALVES], [y_swap(part) for part in features[HALVES:]]]
    feats += [[x_swap(part) for part in block] for block in feats]
    feats += [[c_swap(part) for part in block] for block in feats]
    feats = [[(part, 0) for part in block] for block in feats]
    chunks = []
    for j in range(p.chunks):
        came = p.swap_cotangents([j])
        p.cots[j] = (came, p.send(y_swap, came))
        block = p.slab_weight(j, p.swap_weight(j))
        rows = lax.all_gather(block, "batch", axis=0, tiled=True, axis_index_groups=groups)
        chunks.append([(rows,)])
        [total] = p.chunk(j, feats, chunks[j])
        slab = lax.psum_scatter(total, "batch", scatter_dimension=0, tiled=True, axis_index_groups=groups)
        p.store(j, slab, p.send(x_swap, p.leaving(slab)))
        p.crossed[j] = p.send(x_swap, p.stitch(j, p.send(y_swap, p.acts[j])))
    sums = lax.psum(p.unit_sums(), "batch", axis_index_groups=groups)
    far = x_swap(sums)
    second = y_swap(jnp.concatenate([sums[2:], far[2:]]))
    bias_grad, alpha2_grad = p.small_grads(
        jnp.concatenate([sums[:2], second[:1], far[:2], second[1:]])
    )
    own_pieces = chunks
    far = [(c_swap(p.far_grads[j]), 0) for j in range(p.chunks)]
    far_pieces = [[(c_swap(term),) for [term] in chunk] for chunk in own_pieces]
    keep, leave = p.back(0, far, own_pieces, far_pieces)
    keep_far, leave_far = p.back(1, far, own_pieces, far_pieces)
    partial, grad = 0.0, ()
    for i in range(2):
        other = y_swap(p.add(keep_far[i], x_swap(leave_far[i])))
        came = x_swap(leave[i])
        partial = partial + p.first_grad(i, keep[i], came, other, pooled)
        grad = (p.unpool(i, keep[i], came, other, grad),)
    alpha1_grad = lax.psum(p.by_tower(partial), ("batch", "tower"))
    input_grad = jnp.swapaxes(grad[0], 1, 2)
    return (p.activations(), input_grad, p.weight_grad[0], bias_grad, alpha1_grad, alpha2_grad)


def shards(*args):
    return (line_program if is_line() else plain_program)(Program(*args))


def solution(mesh):
    in_specs = (
        P(("batch", "tower"), None, None, None),
        P(("batch", "tower")),
        P(),
        P("batch", "tower"),
        P("tower"),
        P(None, "tower"),
        P("batch", "tower"),
    )
    out_specs = (
        P("batch", "tower"),
        P(("batch", "tower"), None, None, None),
        P("batch", "tower"),
        P("tower"),
        P(),
        P(None, "tower"),
    )
    return jax.shard_map(shards, mesh=mesh, in_specs=in_specs, out_specs=out_specs, check_vma=False)
```

```python
import functools

import jax
import jax.numpy as jnp
from jax import lax
from jax.experimental import pallas as pl
from jax.experimental.pallas import tpu as pltpu
from jax.sharding import PartitionSpec as P

F32 = jnp.float32
BF16 = jnp.bfloat16
POOLED = 36
PITCH = 48
LANES = 128
VMEM_LIMIT = 56 * 1024 * 1024
SMALL = pl.CostEstimate(flops=1000, bytes_accessed=1000, transcendentals=0)
AHEAD = 2
IMAGE_BLOCK = 16
BLEND_STEPS = 4
HALVES = 2


def params():
    return pltpu.CompilerParams(vmem_limit_bytes=VMEM_LIMIT)


def flipped(value, axis, bit):
    pairs = [(source, source ^ bit) for source in range(lax.axis_size(axis))]
    return lax.ppermute(value, axis, pairs)


def x_swap(value):
    return flipped(value, "batch", 1)


def y_swap(value):
    return flipped(value, "tower", 2)


def c_swap(value):
    return flipped(value, "tower", 1)


def line(value, kind):
    steps = {
        "near": ((0, 1), (1, 0), (2, 3), (3, 2)),
        "middle": ((1, 2), (2, 1)),
        "outward": ((1, 0), (2, 3)),
        "inward": ((0, 1), (3, 2)),
    }[kind]
    pairs = [(2 * a + x, 2 * b + x) for a, b in steps for x in range(2)]
    return lax.ppermute(value, "batch", pairs)


def slab_groups():
    size = lax.axis_size("batch")
    return [list(range(x, size, 2)) for x in range(2)]


def after(value, *others):
    return lax.optimization_barrier((value, *others))[0]


class Order:
    def __init__(self):
        self.last = None

    def then(self, value):
        return value if self.last is None else after(value, self.last)

    def did(self, value):
        self.last = value
        return value


def is_line():
    return lax.axis_size("batch") == 8


def line_order(z):
    rows = jnp.array([[0, 1, 2, 3], [1, 0, 2, 3], [2, 3, 1, 0], [3, 2, 1, 0]])
    return rows[z]


def core_groups():
    return [[t, t + 1] for t in range(0, lax.axis_size("tower"), 2)]


def both_cores(value):
    return lax.all_gather(value, "tower", axis=0, tiled=True, axis_index_groups=core_groups())


def windows(order):
    map_pos = jnp.arange(169)[None, :]
    prow = (order // 6)[:, None]
    pcol = (order % 6)[:, None]
    qrow = map_pos // 13
    qcol = map_pos % 13
    inside = (
        (qrow >= 2 * prow) & (qrow <= 2 * prow + 2) & (qcol >= 2 * pcol) & (qcol <= 2 * pcol + 2)
    )
    return inside, (prow < 5) & (pcol < 5)


def spread_table(order):
    inside, small = windows(order)
    table = jnp.stack([inside, inside & small]).astype(BF16)
    table = jnp.pad(table, ((0, 0), (0, PITCH - POOLED), (0, 0)))
    both = table[:, None, :, :, None] * jnp.eye(2, dtype=BF16)[None, :, None, None, :]
    spread = jnp.swapaxes(both.reshape(2, 2 * PITCH, 338), 1, 2)
    return jnp.pad(jnp.concatenate([spread, spread], axis=2), ((0, 0), (0, 352 - 338), (0, 0)))


def mix_kernel(group, keep, first, summed, *refs):
    *feature_outs, pooled_out, own, other, pool0, pool1 = refs
    count, _, places, ch = summed.shape
    base = pl.program_id(0) * count

    def image(n, carry):
        scale = keep[group[base + n]]
        p0 = summed[n, 0] * scale
        p1 = summed[n, 1] * scale
        rows = pl.ds(pl.multiple_of(n * PITCH, PITCH), places)
        mixed0 = first[0:1, :] * p0 + first[1:2, :] * p1
        mixed1 = first[2:3, :] * p0 + first[3:4, :] * p1
        for hold, value in ((pool0, p0), (pool1, p1), (own, mixed0), (other, mixed1)):
            for h in range(ch // LANES):
                hold[h, rows, :] = value[:, h * LANES : (h + 1) * LANES]
        return carry

    lax.fori_loop(0, count, image, 0, unroll=2)
    per = POOLED // HALVES
    for p in range(POOLED):
        rows = pl.ds(p, count, stride=PITCH)
        for h in range(ch // LANES):
            lanes = slice(p * ch + h * LANES, p * ch + (h + 1) * LANES)
            part = slice((p % per) * ch + h * LANES, (p % per) * ch + (h + 1) * LANES)
            feature_outs[p // per][:, part] = own[h, rows, :].astype(BF16)
            feature_outs[HALVES + p // per][:, part] = other[h, rows, :].astype(BF16)
            pooled_out[0, :, lanes] = pool0[h, rows, :]
            pooled_out[1, :, lanes] = pool1[h, rows, :]


def mix(summed, group, keep, first):
    count, _, places, ch = summed.shape
    nb = IMAGE_BLOCK
    feats = places * ch
    features = [((count, feats // HALVES), BF16)] * (2 * HALVES)
    return pl.pallas_call(
        mix_kernel,
        grid_spec=pltpu.PrefetchScalarGridSpec(
            num_scalar_prefetch=1,
            grid=(count // nb,),
            in_specs=[
                pl.BlockSpec(keep.shape, lambda i, g: (0, 0, 0)),
                pl.BlockSpec((4, ch), lambda i, g: (0, 0)),
                pl.BlockSpec((nb, 2, places, ch), lambda i, g: (i, 0, 0, 0)),
            ],
            out_specs=[pl.BlockSpec((nb, feats // HALVES), lambda i, g: (i, 0))] * (2 * HALVES)
            + [pl.BlockSpec((2, nb, feats), lambda i, g: (0, i, 0))],
            scratch_shapes=[pltpu.VMEM((ch // LANES, nb * PITCH, LANES), F32)] * 4,
        ),
        out_shape=[jax.ShapeDtypeStruct(*f) for f in features]
        + [jax.ShapeDtypeStruct((2, count, feats), F32)],
        compiler_params=params(),
        cost_estimate=SMALL,
        name="mix",
    )(group, keep, first, summed)


def first_grad_kernel(pooled, keep, came, other, out):
    ch = out.shape[2]

    @pl.when(pl.program_id(0) == 0)
    def _():
        out[...] = jnp.zeros_like(out)

    for a in range(2):
        sums = [0.0, 0.0]
        for p in range(POOLED):
            lanes = slice(p * ch, (p + 1) * ch)
            if a == 0:
                grad = keep[:, lanes].astype(F32) + came[:, lanes].astype(F32)
            else:
                grad = other[:, lanes].astype(F32)
            for s in range(2):
                sums[s] = sums[s] + grad * pooled[s, :, lanes]
        for s in range(2):
            out[2 * a + s] += sums[s]


def first_grad(pooled, keep, came, other, at):
    images, feats = keep.shape
    ch = feats // POOLED
    nb = IMAGE_BLOCK
    rows = pl.BlockSpec((nb, feats), lambda i: (i, 0))
    sums = pl.pallas_call(
        first_grad_kernel,
        grid=(images // nb,),
        in_specs=[pl.BlockSpec((2, nb, feats), lambda i: (0, at // nb + i, 0)), rows, rows, rows],
        out_specs=pl.BlockSpec((4, nb, ch), lambda i: (0, 0, 0)),
        out_shape=jax.ShapeDtypeStruct((4, nb, ch), F32),
        compiler_params=params(),
        cost_estimate=SMALL,
        name="first_grad",
    )(pooled, keep, came, other)
    return jnp.sum(sums, axis=1)


def unpool_kernel(start, group, table, first, keep_in, came_in, other_in, *refs):
    out, own, other = refs[-3:]
    count = out.shape[0]
    base = start + pl.program_id(0) * count
    ch = out.shape[3]
    places = out.shape[1]

    @pl.when(pl.program_id(0) == 0)
    def _():
        own[...] = jnp.zeros_like(own)
        other[...] = jnp.zeros_like(other)

    for p in range(POOLED):
        for h in range(ch // LANES):
            lanes = slice(p * ch + h * LANES, p * ch + (h + 1) * LANES)
            rows = pl.ds(p, count, stride=PITCH)
            own[h, rows, :] = keep_in[:, lanes].astype(F32) + came_in[:, lanes].astype(F32)
            other[h, rows, :] = other_in[:, lanes].astype(F32)

    def image(n, carry):
        window = table[group[base + n]]
        rows = pl.ds(pl.multiple_of(n * PITCH, PITCH), PITCH)
        g0, g1 = (
            jnp.concatenate([hold[h, rows, :] for h in range(ch // LANES)], axis=1) for hold in (own, other)
        )
        highs, lows = [], []
        for s in range(2):
            grad = (first[s : s + 1, :] * g0 + first[2 + s : 3 + s, :] * g1) * (1.0 / 9.0)
            highs.append(grad.astype(BF16))
            lows.append((grad - highs[s].astype(F32)).astype(BF16))
        parts = jnp.concatenate(highs + lows, axis=0)
        spread = jnp.dot(window, parts, preferred_element_type=F32).astype(BF16)
        out[n] = spread[: 2 * places].reshape(places, 2, ch)
        return carry

    lax.fori_loop(0, count, image, 0, unroll=2)


def unpool(keep, came, other, row, images, group, table, first, places, at, count, before=()):
    feats = keep.shape[1]
    ch = first.shape[1]
    nb = IMAGE_BLOCK
    rows = pl.BlockSpec((nb, feats), lambda i, g: (row // nb + i, 0))
    return pl.pallas_call(
        functools.partial(unpool_kernel, at),
        grid_spec=pltpu.PrefetchScalarGridSpec(
            num_scalar_prefetch=1,
            grid=(images // nb,),
            in_specs=[
                pl.BlockSpec(table.shape, lambda i, g: (0, 0, 0)),
                pl.BlockSpec((4, ch), lambda i, g: (0, 0)),
                rows,
                rows,
                rows,
            ]
            + [pl.BlockSpec(memory_space=pl.ANY)] * len(before),
            out_specs=pl.BlockSpec((nb, places, 2, ch), lambda i, g: (at // nb + i, 0, 0, 0)),
            scratch_shapes=[pltpu.VMEM((ch // LANES, nb * PITCH, LANES), F32)] * 2,
        ),
        out_shape=jax.ShapeDtypeStruct((count, places, 2, ch), BF16),
        input_output_aliases={6: 0} if before else {},
        compiler_params=params(),
        cost_estimate=SMALL,
        name="unpool",
    )(group, table, first, keep, came, other, *before)


def store_kernel(chunk, chunks, x, own, came, *refs):
    out, stay, go, sems = refs[-4:]
    rows, width = came.shape

    def columns(at):
        return out.at[:, pl.ds(pl.multiple_of(at * width, width), width)]

    source = own.at[pl.ds(pl.multiple_of(x[0] * rows, rows), rows), :]
    read = pltpu.make_async_copy(source, stay, sems.at[0])
    read.start()
    go[...] = came[...].astype(F32)
    write = pltpu.make_async_copy(go, columns((1 - x[0]) * chunks + chunk), sems.at[1])
    write.start()
    read.wait()
    write_own = pltpu.make_async_copy(stay, columns(x[0] * chunks + chunk), sems.at[2])
    write_own.start()
    write.wait()
    write_own.wait()


def store(own, came, x, chunk, chunks, shape, before=()):
    anywhere = pl.BlockSpec(memory_space=pl.ANY)
    return pl.pallas_call(
        functools.partial(store_kernel, chunk, chunks),
        in_specs=[pl.BlockSpec(memory_space=pltpu.SMEM), anywhere, pl.BlockSpec(memory_space=pltpu.VMEM)]
        + [anywhere] * len(before),
        out_specs=anywhere,
        out_shape=jax.ShapeDtypeStruct(shape, F32),
        scratch_shapes=[pltpu.VMEM(came.shape, F32)] * 2 + [pltpu.SemaphoreType.DMA((3,))],
        input_output_aliases={3: 0} if before else {},
        compiler_params=params(),
        cost_estimate=SMALL,
        name="store",
    )(x, own, came, *before)


def place_rows_kernel(places, *refs):
    *parts, out, sem = refs
    height, width = parts[0].shape[0] // 4, parts[0].shape[1]
    chunks = len(parts) // 2
    x, y, core = places[0], places[1], places[2]
    copies = []
    for i, part in enumerate(parts):
        side, j = i // chunks, i % chunks
        col = (jnp.where(x == side, 0, chunks) + j) * width
        cols = pl.ds(pl.multiple_of(col, width), width)
        for b in range(4):
            row = (2 * ((b % 2) ^ y) + ((b // 2) ^ core)) * height
            target = out.at[pl.ds(pl.multiple_of(row, height), height), cols]
            copies.append(pltpu.make_async_copy(part.at[pl.ds(b * height, height), :], target, sem.at[i, b]))
            copies[-1].start()
    for copy in copies:
        copy.wait()


def place_rows(places, own, other):
    parts = own + other
    rows, width = parts[0].shape
    return pl.pallas_call(
        place_rows_kernel,
        in_specs=[pl.BlockSpec(memory_space=pltpu.SMEM)] + [pl.BlockSpec(memory_space=pltpu.VMEM)] * len(parts),
        out_specs=pl.BlockSpec(memory_space=pl.ANY),
        out_shape=jax.ShapeDtypeStruct((rows, width * len(parts)), BF16),
        scratch_shapes=[pltpu.SemaphoreType.DMA((len(parts), 4))],
        compiler_params=params(),
        cost_estimate=SMALL,
        name="place_rows",
    )(places, *parts)


def blend_kernel(counts, roles, *refs):
    hold, in_sems, out_sems = refs[-3:]
    blocks, outs = refs[: sum(counts)], refs[sum(counts) : -3]
    rows = hold.shape[1] // BLEND_STEPS
    outer = roles[0] == 1

    def span(i):
        return pl.ds(i * rows, rows)

    def bring(block, k, i):
        return pltpu.make_async_copy(block.at[span(i), :], hold.at[k, span(i), :], in_sems.at[k, i])

    def leave(k, out, i):
        return pltpu.make_async_copy(hold.at[k, span(i), :], out.at[span(i), :], out_sems.at[k, i])

    groups, at = [], 0
    for count in counts:
        groups.append(blocks[at : at + count])
        at += count
    slots = [sum(max(count - 1, 1) for count in counts[:g]) for g in range(len(counts))]
    for g, (first, *rest) in enumerate(groups):
        for i in range(BLEND_STEPS):

            @pl.when(outer)
            def _(first=first, g=g, i=i):
                bring(first, slots[g], i).start()

            @pl.when(jnp.logical_not(outer))
            def _(rest=rest, g=g, i=i):
                for k, block in enumerate(rest):
                    bring(block, slots[g] + k, i).start()

    for g, (first, *rest) in enumerate(groups):
        for i in range(BLEND_STEPS):
            bring(first, slots[g], i).wait()
            if len(rest) > 1:

                @pl.when(jnp.logical_not(outer))
                def _(rest=rest, g=g, i=i):
                    for k in range(1, len(rest)):
                        bring(rest[k], slots[g] + k, i).wait()
                    total = sum(hold[slots[g] + k, span(i), :].astype(F32) for k in range(len(rest)))
                    hold[slots[g], span(i), :] = total.astype(BF16)

            leave(slots[g], outs[g], i).start()
    for g in range(len(groups)):
        for i in range(BLEND_STEPS):
            leave(slots[g], outs[g], i).wait()


def blend(roles, groups):
    counts = [len(group) for group in groups]
    shape = groups[0][0].shape
    slots = sum(max(count - 1, 1) for count in counts)
    anywhere = pl.BlockSpec(memory_space=pl.ANY)
    return pl.pallas_call(
        functools.partial(blend_kernel, counts),
        in_specs=[pl.BlockSpec(memory_space=pltpu.SMEM)] + [anywhere] * sum(counts),
        out_specs=[anywhere] * len(groups),
        out_shape=[jax.ShapeDtypeStruct(shape, BF16)] * len(groups),
        scratch_shapes=[
            pltpu.VMEM((slots, *shape), BF16),
            pltpu.SemaphoreType.DMA((slots, BLEND_STEPS)),
            pltpu.SemaphoreType.DMA((slots, BLEND_STEPS)),
        ],
        compiler_params=params(),
        cost_estimate=SMALL,
        name="blend",
    )(roles, *[block for group in groups for block in group])


def tile_of(rows):
    return next(t for t in (1152, 768, 576, 512, 384, 256, 128) if rows % t == 0)


def fetch(outer, terms, rows, target, sem):
    def copy(term):
        return pltpu.make_async_copy(term.at[rows, :], target, sem)

    if len(terms) == 1:
        copy(terms[0]).start()
    else:
        pl.when(outer == 1)(lambda: copy(terms[0]).start())
        pl.when(outer == 0)(lambda: copy(terms[1]).start())


def chunk_kernel(layout, starts, cot_cols, roles, vectors, *refs):
    chunks, count = len(layout), len(layout[0])
    cots, refs = refs[:4], refs[4:]
    blocks = len(starts) // HALVES
    feats, refs = refs[: blocks * HALVES], refs[blocks * HALVES :]
    at = 0
    pieces = []
    for counts in layout:
        pieces.append([])
        for many in counts:
            pieces[-1].append(refs[at : at + many])
            at += many
    act_out, keep_out, send_out, sums_out = refs[at : at + 4]
    outs = [refs[at + 4 + i * count : at + 4 + (i + 1) * count] for i in range(chunks)]
    held, weight, total, dpre_out, k_own, k_other, high, low, in_sems, w_sems, cot_sems, out_sems = refs[-12:]
    steps, images, tile = held.shape
    per = steps // count
    units = total.shape[1] // chunks
    half, height = steps // HALVES, images // blocks

    def columns(i):
        return slice(i * units, (i + 1) * units)

    def begin(k):
        for s in range(count):

            @pl.when(k // per == s)
            def _(s=s):
                rows = pl.ds(pl.multiple_of((k - s * per) * tile, tile), tile)
                for i in range(chunks):
                    fetch(roles[0], pieces[i][s], rows, weight.at[k, :, columns(i)], w_sems.at[k])

        for h in range(HALVES):

            @pl.when(k // half == h)
            def _(h=h):
                cols = pl.ds(pl.multiple_of((k - h * half) * tile, tile), tile)
                for r in range(blocks):
                    at = r * HALVES + h
                    start = starts[at]
                    if start is None:
                        start = pl.multiple_of(roles[1] * height, height)
                    part = feats[at].at[pl.ds(start, height), cols]
                    rows = pl.ds(r * height, height)
                    pltpu.make_async_copy(part, held.at[k, rows, :], in_sems.at[k]).start()

    def arrive(target, sem):
        pltpu.make_async_copy(target, target, sem).wait()

    ahead = min(AHEAD, steps)
    for k in range(ahead):
        begin(jnp.int32(k))
    for tower, target in enumerate((k_own, k_other)):
        for r in range(blocks):
            core, x, y = r // 4, r // 2 % 2, r % 2
            source, col = cots[2 * tower + x], cot_cols[2 * tower + x]
            rows = pl.ds((2 * core + (y ^ tower)) * height, height)
            source = source.at[rows, pl.ds(col, total.shape[1])]
            target_rows = target.at[pl.ds(r * height, height), :]
            pltpu.make_async_copy(source, target_rows, cot_sems.at[tower]).start()
    total[...] = jnp.zeros_like(total)

    def forward_step(k, carry):
        pl.when(k + ahead < steps)(lambda: begin(k + ahead))
        arrive(held.at[k], in_sems.at[k])
        arrive(weight.at[k], w_sems.at[k])
        total[...] += jnp.dot(held[k], weight[k], preferred_element_type=F32)
        return carry

    lax.fori_loop(0, steps, forward_step, 0)
    arrive(k_own, cot_sems.at[0])
    arrive(k_other, cot_sems.at[1])

    bias, own_coef, other_coef = (vectors[i : i + 1, :] for i in range(3))
    c = 0.7978845608028654
    block = 32

    def rows_of(i, sums):
        rows = pl.ds(pl.multiple_of(i * block, block), block)
        x = total[rows, :] + bias
        x2 = x * x
        t = jnp.tanh(c * (x + 0.044715 * (x2 * x)))
        half = 0.5 * (1.0 + t)
        act = (x * half).astype(BF16)
        slope = half + (0.5 * c) * x * (1.0 - t * t) * (1.0 + (3.0 * 0.044715) * x2)
        k0 = k_own[rows, :].astype(F32)
        k1 = k_other[rows, :].astype(F32)
        dpre = ((own_coef * k0 + other_coef * k1) * slope).astype(BF16)
        act_out[rows, :] = act
        dpre_out[rows, :] = dpre
        actf = act.astype(F32)

        def fold(v):
            return jnp.sum(v.reshape(block // 8, 8, v.shape[1]), axis=0)

        return (
            sums[0] + fold(dpre.astype(F32)),
            sums[1] + fold(k0 * actf),
            sums[2] + fold(k1 * actf),
        )

    zero = jnp.zeros((8, total.shape[1]), F32)
    sums = lax.fori_loop(0, images // block, rows_of, (zero, zero, zero))
    for i in range(3):
        sums_out[i : i + 1, :] = jnp.sum(sums[i], axis=0, keepdims=True)
    keep_out[...] = dpre_out[: images // 2]
    send_out[...] = dpre_out[images // 2 :]

    def product(k):
        return lax.dot_general(
            held[k], dpre_out[...], (((0,), (0,)), ((), ())), preferred_element_type=F32
        )

    def last_steps(k, carry):
        made = product(k).astype(BF16)
        for i in range(chunks):
            low[k - per, i] = made[:, columns(i)]
        for s in range(1, count):

            @pl.when(k // per == s)
            def _(s=s):
                rows = pl.ds(pl.multiple_of((k - s * per) * tile, tile), tile)
                for i in range(chunks):
                    pltpu.make_async_copy(low.at[k - per, i], outs[i][s].at[rows, :], out_sems.at[k]).start()

        return carry

    def first_steps(k, carry):
        made = product(k)
        rows = pl.ds(pl.multiple_of(k * tile, tile), tile)
        for i in range(chunks):
            high[k, i] = made[:, columns(i)]
            pltpu.make_async_copy(high.at[k, i], outs[i][0].at[rows, :], out_sems.at[k]).start()
        return carry

    if count > 1:
        lax.fori_loop(per, steps, last_steps, 0)
    lax.fori_loop(0, per, first_steps, 0)
    for k in range(steps):
        arrive(high.at[k] if k < per else low.at[k - per], out_sems.at[k])


def chunk(roles, feats, pieces, vectors, cots):
    images = len(feats) * feats[-1][-1][0].shape[0]
    units = pieces[0][0][0].shape[1]
    width = units * len(pieces)
    depth = sum(part.shape[1] for part, _ in feats[0])
    starts = [start for block in feats for _, start in block]
    count = len(pieces[0])
    height = pieces[0][0][0].shape[0]
    tile = tile_of(height)
    steps, per = depth // tile, height // tile
    terms = [term for chunk in pieces for piece in chunk for term in piece]
    anywhere = pl.BlockSpec(memory_space=pl.ANY)
    vmem = pl.BlockSpec(memory_space=pltpu.VMEM)
    kinds = ([F32] + [BF16] * (count - 1)) * len(pieces)
    return pl.pallas_call(
        functools.partial(chunk_kernel, [[len(p) for p in chunk] for chunk in pieces], starts, [c for _, c in cots]),
        in_specs=[pl.BlockSpec(memory_space=pltpu.SMEM), vmem]
        + [anywhere] * (len(cots) + len(feats) * HALVES + len(terms)),
        out_specs=[vmem] * 4 + [anywhere] * len(kinds),
        out_shape=[
            jax.ShapeDtypeStruct((images, width), BF16),
            jax.ShapeDtypeStruct((images // 2, width), BF16),
            jax.ShapeDtypeStruct((images // 2, width), BF16),
            jax.ShapeDtypeStruct((8, width), F32),
        ]
        + [jax.ShapeDtypeStruct((height, units), kind) for kind in kinds],
        scratch_shapes=[
            pltpu.VMEM((steps, images, tile), BF16),
            pltpu.VMEM((steps, tile, width), BF16),
            pltpu.VMEM((images, width), F32),
            pltpu.VMEM((images, width), BF16),
            pltpu.VMEM((images, width), BF16),
            pltpu.VMEM((images, width), BF16),
            pltpu.VMEM((per, len(pieces), tile, units), F32),
            pltpu.VMEM((max(steps - per, 1), len(pieces), tile, units), BF16),
            pltpu.SemaphoreType.DMA((steps,)),
            pltpu.SemaphoreType.DMA((steps,)),
            pltpu.SemaphoreType.DMA((2,)),
            pltpu.SemaphoreType.DMA((steps,)),
        ],
        compiler_params=params(),
        cost_estimate=SMALL,
        name="chunk",
    )(roles, vectors, *[cot for cot, _ in cots], *[part for block in feats for part, _ in block], *terms)


def back_kernel(layout, firsts, blocks, roles, *refs):
    outs = refs[-10:-6]
    grad, weight, made, grad_sems, w_sems, out_sems = refs[-6:]
    sources, count = len(layout), len(layout[0])
    grads = refs[:sources]
    at = sources
    pieces = []
    for counts in layout:
        pieces.append([])
        for many in counts:
            pieces[-1].append(refs[at : at + many])
            at += many
    slots, tile, total = weight.shape
    units = total // sources
    steps = made.shape[0]
    per = steps // count
    share = made.shape[1] // len(outs)

    def columns(j):
        return slice(j * units, (j + 1) * units)

    def begin(k):
        slot = lax.rem(k, slots)
        for s in range(count):

            @pl.when(k // per == s)
            def _(s=s):
                rows = pl.ds(pl.multiple_of((k - s * per) * tile, tile), tile)
                for j in range(sources):
                    fetch(roles[0], pieces[j][s], rows, weight.at[slot, :, columns(j)], w_sems.at[slot])

    def arrive(target, sem):
        pltpu.make_async_copy(target, target, sem).wait()

    copies = []
    for j in range(sources):
        for i, block in enumerate(blocks):
            rows = grad.shape[0] // len(blocks)
            source = grads[j].at[pl.ds(firsts[j] + block * rows, rows), :]
            target = grad.at[pl.ds(i * rows, rows), columns(j)]
            copies.append(pltpu.make_async_copy(source, target, grad_sems.at[j, i]))
            copies[-1].start()
    ahead = min(slots - 1, steps)
    for k in range(ahead):
        begin(jnp.int32(k))
    for copy in copies:
        copy.wait()

    def step(k, carry):
        pl.when(k + ahead < steps)(lambda: begin(k + ahead))
        slot = lax.rem(k, slots)
        arrive(weight.at[slot], w_sems.at[slot])
        made[k] = lax.dot_general(
            grad[...], weight[slot], (((1,), (1,)), ((), ())), preferred_element_type=F32
        ).astype(BF16)
        cols = pl.ds(pl.multiple_of(k * tile, tile), tile)
        for i, out in enumerate(outs):
            source = made.at[k, pl.ds(i * share, share), :]
            pltpu.make_async_copy(source, out.at[:, cols], out_sems.at[k]).start()
        return carry

    lax.fori_loop(0, steps, step, 0)
    for k in range(steps):
        arrive(made.at[k], out_sems.at[k])


def back(roles, grads, pieces, blocks):
    units = grads[0][0].shape[1]
    images = min(grad.shape[0] for grad, _ in grads) // 4 * len(blocks)
    count = len(pieces[0])
    height = pieces[0][0][0].shape[0]
    depth = height * count
    tile = next(t for t in (768, 512, 384, 256, 128) if height % t == 0)
    steps = depth // tile
    total = units * len(grads)
    terms = [term for chunk in pieces for piece in chunk for term in piece]
    layout = [[len(piece) for piece in chunk] for chunk in pieces]
    anywhere = pl.BlockSpec(memory_space=pl.ANY)
    return pl.pallas_call(
        functools.partial(back_kernel, layout, [row for _, row in grads], blocks),
        in_specs=[pl.BlockSpec(memory_space=pltpu.SMEM)] + [anywhere] * (len(grads) + len(terms)),
        out_specs=[anywhere] * 4,
        out_shape=[jax.ShapeDtypeStruct((images // 4, depth), BF16)] * 4,
        scratch_shapes=[
            pltpu.VMEM((images, total), BF16),
            pltpu.VMEM((AHEAD + 1, tile, total), BF16),
            pltpu.VMEM((steps, images, tile), BF16),
            pltpu.SemaphoreType.DMA((len(grads), len(blocks))),
            pltpu.SemaphoreType.DMA((AHEAD + 1,)),
            pltpu.SemaphoreType.DMA((steps,)),
        ],
        compiler_params=params(),
        cost_estimate=SMALL,
        name="back",
    )(roles, *[grad for grad, _ in grads], *terms)


def either(flag, value, axis):
    return jnp.where(flag, jnp.flip(value, axis), value)


class Program:
    def __init__(self, convmaps, group, alpha1, weight, bias, alpha2, cotangent):
        self.order = Order()
        self.convmaps, self.group, self.weight = convmaps, group, weight
        self.count, _, self.places, self.channels = convmaps.shape
        batch_id = lax.axis_index("batch")
        tower_id = lax.axis_index("tower")
        self.x, self.z = batch_id % 2, batch_id // 2
        self.y, self.core = tower_id // 2, tower_id % 2
        self.depth, self.width = weight.shape
        self.units = self.width // 2
        self.n = self.units // (4 if is_line() else 2)
        self.chunks = self.units // self.n
        self.images = 8 * self.count
        self.mine, self.theirs = self.x * self.units, (1 - self.x) * self.units
        units = self.units
        second = lax.dynamic_slice_in_dim(alpha2, self.mine, units, 1)
        self.own_coef = lax.dynamic_index_in_dim(second, self.y, 0, keepdims=True).astype(F32)
        self.cross = lax.dynamic_index_in_dim(second, 1 - self.y, 0, keepdims=True)
        own_bias = lax.dynamic_slice_in_dim(bias, self.mine, units, 0)[None, :].astype(F32)
        self.own_bias = own_bias
        self.cotangent = cotangent
        places = jnp.arange(POOLED)
        if is_line():
            places = places.reshape(4, -1)[line_order(self.z)].reshape(-1)
        self.table = spread_table(places)
        inside, small = windows(places)
        self.pool_table = inside.astype(BF16)
        keep = jnp.stack([jnp.ones_like(small), small]).astype(F32) * (1.0 / 9.0)
        self.keep = jnp.broadcast_to(keep, (2, POOLED, self.channels))
        self.first = either(self.y == 1, alpha1.astype(F32), 0).reshape(4, self.channels)
        self.is_outer = (self.z == 0) | (self.z == 3)
        self.roles = jnp.stack([self.is_outer.astype(jnp.int32), 1 - self.core])
        self.cots = {}
        self.places_of = jnp.stack([self.x, self.y, self.core]).astype(jnp.int32)
        self.weight_grad = ()
        self.acts, self.grads, self.far_grads, self.sums = {}, {}, {}, {}
        self.stitched, self.crossed = {}, {}

    def then(self, value):
        return self.order.then(value)

    def did(self, value):
        return self.order.did(value)

    def keep_cross(self, came):
        cross_back = self.did(self.then(came)).astype(F32)
        zeros = jnp.zeros((5, self.units), F32)
        self.vectors = jnp.concatenate([self.own_bias, self.own_coef, cross_back, zeros])
        self.cross = self.cross.astype(F32)

    def load_cotangents(self):
        cot = self.then(self.cotangent).reshape(2, 2, self.count, self.width)
        cot = either(self.core == 1, either(self.y == 1, cot, 0), 1).swapaxes(0, 1).reshape(-1, self.width)
        self.cot_mine = self.did(lax.dynamic_slice_in_dim(cot, self.mine, self.units, 1))
        self.cot_theirs = lax.dynamic_slice_in_dim(cot, self.theirs, self.units, 1)

    def pool(self):
        return jnp.einsum("pq,nsqc->nspc", self.pool_table, self.convmaps, preferred_element_type=F32)

    def mix(self, summed):
        return mix(summed, self.group, self.keep, self.first)

    def cols(self, j):
        return slice(j * self.n, (j + 1) * self.n)

    def span(self, js):
        return slice(js[0] * self.n, (js[-1] + 1) * self.n)

    def weight_part(self, start, j, many=1):
        return lax.dynamic_slice(self.then(self.weight), (0, start + j * self.n), (self.depth, many * self.n))

    def swap_weight(self, j, many=1):
        return self.send(x_swap, self.weight_part(self.theirs, j, many))

    def slab_weight(self, j, came):
        a, b = self.weight_part(self.mine, j), self.then(came)
        return self.did(jnp.where(self.x == 0, jnp.concatenate([a, b]), jnp.concatenate([b, a])))

    def swap_cotangents(self, js):
        return self.send(x_swap, self.cot_theirs[:, self.span(js)])

    def cots_of(self, j):
        here, there = self.cots[j]
        first = (j - min(i for i in self.cots if self.cots[i][0] is here)) * self.n
        return [(self.cot_mine, j * self.n), (here, first), (self.cot_across, j * self.n), (there, first)]

    def send(self, move, value, *args):
        return move(self.did(self.then(value)), *args)

    def chunk(self, j, feats, pieces):
        act, keep, send, sums, *products = chunk(
            self.roles,
            feats,
            [pieces],
            self.then(self.vectors[:, self.cols(j)]),
            self.cots_of(j),
        )
        self.did(act)
        self.acts[j], self.grads[j], self.far_grads[j], self.sums[j] = act, keep, send, sums
        return products

    def stitch(self, j, came):
        cols = self.cols(j)
        other_act = jnp.flip(self.then(came).reshape(4, 2, self.count, self.n), 1).reshape(self.images, self.n)
        mix = self.own_coef[:, cols] * self.acts[j].astype(F32) + self.cross[:, cols] * other_act.astype(F32)
        mix = self.did(mix.astype(BF16)).reshape(2, 2, 2 * self.count, self.n)
        self.stitched[j] = mix[:, 0].reshape(-1, self.n)
        return mix[:, 1].reshape(-1, self.n)

    def leaving(self, slab):
        return lax.dynamic_slice_in_dim(slab, (1 - self.x) * self.depth, self.depth, 0).astype(BF16)

    def store(self, j, rows, came):
        shape = (self.depth, self.width)
        made = store(self.then(rows), came, self.places_of, j, self.chunks, shape, self.weight_grad)
        self.weight_grad = (self.did(made),)

    def activations(self):
        own, other = ([parts[j] for j in range(self.chunks)] for parts in (self.stitched, self.crossed))
        return place_rows(self.places_of, [self.then(own[0])] + own[1:], other)

    def unit_sums(self, *parts):
        return jnp.concatenate([part[:3] for part in parts or self.sums.values()], axis=1)

    def small_grads(self, sums):
        mine, far = sums[:3], sums[3:6]
        wide = jnp.where(
            self.x == 0, jnp.concatenate([mine, far], -1), jnp.concatenate([far, mine], -1)
        )
        return wide[0], either(self.y == 1, wide[1:3], 0)

    def back(self, y, came_grads, pieces, came_pieces):
        chunks = range(self.chunks)
        grads = [(self.grads[j], 0) for j in chunks] + list(came_grads)
        grads[0] = (self.then(grads[0][0]), 0)
        parts = back(
            self.roles,
            grads,
            [pieces[j] for j in chunks] + [came_pieces[j] for j in chunks],
            [y, 2 + y],
        )
        self.did(parts[0])
        return parts[:2], parts[2:]

    def add(self, keep, came):
        return self.did((keep.astype(F32) + self.then(came).astype(F32)).astype(BF16))

    def first_grad(self, i, keep, came, other, pooled):
        return self.did(first_grad(pooled, self.then(keep), came, other, i * keep.shape[0]))

    def by_tower(self, partial):
        return either(self.y == 1, partial.reshape(2, 2, self.channels), 0)

    def unpool(self, i, keep, came, other, before=(), part=0, parts=1):
        images = keep.shape[0] // parts
        at = i * keep.shape[0] + part * images
        return self.did(
            unpool(
                self.then(keep),
                came,
                other,
                part * images,
                images,
                self.group,
                self.table,
                self.first,
                self.places,
                at,
                self.count,
                before,
            )
        )


def line_program(p):
    then, did = p.then, p.did
    came, blocks, near, inner, outer, first_out, last_out = {}, {}, {}, {}, {}, {}, {}
    total, into, crossed, middle, final, slab_came = {}, {}, {}, {}, {}, {}
    from_own, swapped = {}, {}

    def send(kind, value):
        return p.send(line, value, kind)

    def arrive(value):
        return did(then(value))

    def block(j):
        blocks[j] = p.slab_weight(j, came[j])

    def pieces(j):
        beside = (near[j],) if j < 2 else (from_own[j], swapped[j])
        return [(blocks[j],), beside, (first_out[j], inner[j]), (last_out[j], outer[j])]

    def part(j, s):
        return total[j][s]

    def payload(inward, outward):
        return did(jnp.where(p.is_outer, then(inward), outward))

    def ends(value):
        return send("near", value)

    def inward(j, s):
        return send("inward", then(part(j, s)))

    def plus(j, s, value):
        return (part(j, s).astype(F32) + then(value).astype(F32)).astype(BF16)

    def edge(j):
        return jnp.where(
            p.is_outer, then(final[j]).astype(F32), into[j, 1].astype(F32) + middle[j].astype(F32)
        )

    def blended(*groups):
        (first, *rest), *others = groups
        made = blend(p.roles, [(then(first), *rest)] + others)
        did(made[0])
        return made

    def pick(a, b):
        return did(jnp.where(p.is_outer, then(a), b))

    def core_swap(j, s):
        came_pieces[j, s] = p.send(c_swap, picked[j, s])

    def core_came(j, s):
        came_pieces[j, s] = arrive(came_pieces[j, s])

    picked, came_pieces = {}, {}

    def far_end(j):
        return plus(j, 3, into[j, 3])

    came[0] = p.swap_weight(0)
    came[1] = p.swap_weight(1)
    cross_came = p.send(y_swap, p.cross)
    came_pair = p.swap_weight(2, 2)
    p.load_cotangents()
    p.keep_cross(cross_came)
    p.table = did(then(p.table))
    came[0] = arrive(came[0])
    block(0)
    near[0] = ends(blocks[0])
    inner[0] = send("middle", blocks[0])
    p.cot_across = p.send(y_swap, p.cot_mine)
    p.pool_table = then(p.pool_table)
    summed = did(p.pool())
    came[1] = arrive(came[1])
    cot_came = p.swap_cotangents([0, 1])
    block(1)
    near[0] = arrive(near[0])
    near[1] = ends(blocks[1])
    inner[0] = arrive(inner[0])
    inner[1] = send("middle", blocks[1])
    kept_a, kept_b, sent_a, sent_b, pooled = p.mix(then(summed))
    did(kept_a)
    came_pair = arrive(came_pair)
    p.cot_across = arrive(p.cot_across)
    cot_came = arrive(cot_came)
    x_a = p.send(x_swap, kept_a)
    y_a = p.send(y_swap, sent_a)
    c_kept_a = p.send(c_swap, kept_a)
    came[2], came[3] = came_pair[:, : p.n], came_pair[:, p.n :]
    block(2)
    block(3)
    near[1] = arrive(near[1])
    first_out[0] = send("outward", inner[0])
    inner[1] = arrive(inner[1])
    outer[0] = send("middle", near[0])
    x_a = arrive(x_a)
    x_b = p.send(x_swap, kept_b)
    y_a = arrive(y_a)
    y_b = p.send(y_swap, sent_b)
    c_kept_a = arrive(c_kept_a)
    c_kept_b = p.send(c_swap, kept_b)
    first_out[0] = arrive(first_out[0])
    first_out[1] = send("outward", inner[1])
    outer[0] = arrive(outer[0])
    outer[1] = send("middle", near[1])
    x_b = arrive(x_b)
    x_y_a = p.send(x_swap, y_a)
    y_b = arrive(y_b)
    cot_crossed = p.send(y_swap, cot_came)
    c_kept_b = arrive(c_kept_b)
    c_x_a = p.send(c_swap, x_a)
    value = payload(blocks[2], outer[0])
    first_out[1] = arrive(first_out[1])
    swapped[2] = last_out[0] = ends(value)
    outer[1] = arrive(outer[1])
    inner[2] = send("middle", blocks[2])
    x_y_a = arrive(x_y_a)
    x_y_b = p.send(x_swap, y_b)
    p.cots[0] = p.cots[1] = (cot_came, arrive(cot_crossed))
    c_x_a = arrive(c_x_a)
    c_y_a = p.send(c_swap, y_a)
    c_x_b = p.send(c_swap, x_b)
    value = payload(blocks[3], outer[1])
    for j in range(4):
        picked[j, 0] = blocks[j]
    picked[0, 1], picked[1, 1] = near[0], near[1]
    swapped[2] = last_out[0] = arrive(swapped[2])
    swapped[3] = last_out[1] = ends(value)
    inner[2] = arrive(inner[2])
    outer[2] = send("middle", swapped[2])
    x_y_b = arrive(x_y_b)
    c_y_a = arrive(c_y_a)
    c_x_b = arrive(c_x_b)
    c_y_b = p.send(c_swap, y_b)
    c_x_y_a = p.send(c_swap, x_y_a)
    c_x_y_b = p.send(c_swap, x_y_b)
    swapped[3] = last_out[1] = arrive(swapped[3])
    from_own[2] = send("outward", blocks[2])
    p.vectors = did(then(p.vectors))
    c_y_b = arrive(c_y_b)
    c_x_y_a = arrive(c_x_y_a)
    c_x_y_b = arrive(c_x_y_b)
    core_swap(0, 0)
    core_swap(0, 1)
    cot_came = p.swap_cotangents([2, 3])
    feats = [
        [(kept_a, 0), (kept_b, 0)],
        [(y_a, 0), (y_b, 0)],
        [(x_a, 0), (x_b, 0)],
        [(x_y_a, 0), (x_y_b, 0)],
        [(c_kept_a, 0), (c_kept_b, 0)],
        [(c_y_a, 0), (c_y_b, 0)],
        [(c_x_a, 0), (c_x_b, 0)],
        [(c_x_y_a, 0), (c_x_y_b, 0)],
    ]
    total[0] = p.chunk(0, feats, pieces(0))
    outer[2] = arrive(outer[2])
    value = payload(part(0, 3), inner[2])
    from_own[2] = arrive(from_own[2])
    into[0, 3] = first_out[2] = ends(value)
    core_came(0, 0)
    core_came(0, 1)
    cot_came = arrive(cot_came)
    inner[3] = send("middle", blocks[3])
    act_came = p.send(y_swap, p.acts[0])
    core_swap(1, 0)
    core_swap(1, 1)
    total[1] = p.chunk(1, feats, pieces(1))
    value = payload(part(0, 2), outer[2])
    into[0, 3] = first_out[2] = arrive(into[0, 3])
    into[0, 2] = last_out[2] = ends(value)
    far0 = did(far_end(0))
    inner[3] = arrive(inner[3])
    outer[3] = send("middle", swapped[3])
    cot_crossed = p.send(y_swap, cot_came)
    act_came = arrive(act_came)
    core_came(1, 0)
    core_came(1, 1)
    core_swap(2, 0)
    core_swap(3, 0)
    picked[0, 2], picked[1, 2], picked[0, 3], picked[1, 3], picked[2, 1], picked[2, 2], value = blended(
        (first_out[0], inner[0]),
        (first_out[1], inner[1]),
        (last_out[0], outer[0]),
        (last_out[1], outer[1]),
        (from_own[2], swapped[2]),
        (first_out[2], inner[2]),
        (part(0, 1), blocks[3]),
    )
    act_mixes = [p.stitch(0, act_came)]
    cot_crossed = arrive(cot_crossed)
    into[0, 2] = last_out[2] = arrive(into[0, 2])
    into[0, 1] = from_own[3] = ends(value)
    p.cots[2] = p.cots[3] = (cot_came, cot_crossed)
    core_came(2, 0)
    core_came(3, 0)
    act_came = p.send(y_swap, p.acts[1])
    core_swap(0, 2)
    core_swap(1, 2)
    total[2] = p.chunk(2, feats, pieces(2))
    outer[3] = arrive(outer[3])
    [value] = blended((part(1, 3), inner[3]))
    into[0, 1] = from_own[3] = arrive(into[0, 1])
    into[1, 3] = first_out[3] = ends(value)
    rest = did(plus(0, 2, into[0, 2]))
    crossed[0] = send("middle", far0)
    act_came = arrive(act_came)
    core_came(0, 2)
    core_came(1, 2)
    act_came2 = p.send(y_swap, p.acts[2])
    core_swap(0, 3)
    core_swap(1, 3)
    value, picked[3, 1], picked[2, 3] = blended(
        (part(1, 2), outer[3]), (from_own[3], swapped[3]), (last_out[2], outer[2])
    )
    act_mixes.append(p.stitch(1, act_came))
    into[1, 3] = first_out[3] = arrive(into[1, 3])
    into[1, 2] = last_out[3] = ends(value)
    far1 = did(far_end(1))
    crossed[0] = arrive(crossed[0])
    middle[0] = send("middle", rest)
    act_came = arrive(act_came2)
    core_came(0, 3)
    core_came(1, 3)
    core_swap(2, 1)
    core_swap(2, 2)
    core_swap(3, 1)
    value, picked[3, 2] = blended((part(1, 1), part(0, 1), crossed[0]), (first_out[3], inner[3]))
    far = did(jnp.concatenate([then(p.far_grads[0]), p.far_grads[1], p.far_grads[2]]))
    act_mixes.append(p.stitch(2, act_came))
    act_mixes = did(jnp.concatenate([then(act_mixes[0]), *act_mixes[1:]]))
    into[1, 2] = last_out[3] = arrive(into[1, 2])
    into[1, 1] = final[0] = ends(value)
    sums = did(p.unit_sums(then(p.sums[0]), p.sums[1], p.sums[2]))
    core_came(2, 1)
    core_came(2, 2)
    core_came(3, 1)
    core_swap(2, 3)
    core_swap(3, 2)
    mixes_came = p.send(x_swap, act_mixes)
    total[3] = p.chunk(3, feats, pieces(3))
    middle[0] = arrive(middle[0])
    into[1, 1] = final[0] = arrive(into[1, 1])
    into[2, 3] = inward(2, 3)
    core_came(2, 3)
    core_came(3, 2)
    mixes_came = arrive(mixes_came)
    far = p.send(c_swap, far)
    came_last = p.send(c_swap, last_out[3])
    came_outer = p.send(c_swap, outer[3])
    rows = {0: did(then(part(0, 0)) + edge(0))}
    far = arrive(far)
    far3 = p.send(c_swap, p.far_grads[3])
    crossed[1] = send("middle", far1)
    rest = did(plus(1, 2, into[1, 2]))
    came_last = arrive(came_last)
    slab_came[0] = p.send(x_swap, p.leaving(rows[0]))
    came_outer = arrive(came_outer)
    far3 = arrive(far3)
    act_came = p.send(y_swap, p.acts[3])
    third = far.shape[0] // 3
    came_grads = [(far, 0), (far, third), (far, 2 * third), (far3, 0)]
    picked[3, 3], came_pieces[3, 3] = (last_out[3], outer[3]), (came_last, came_outer)
    own_pieces, far_pieces = (
        [[terms if isinstance(terms := kind[j, s], tuple) else (terms,) for s in range(4)] for j in range(4)]
        for kind in (picked, came_pieces)
    )
    keep_far, leave_far = p.back(1, came_grads, own_pieces, far_pieces)
    came_far, came_x, own_y = {}, {}, {}
    into[2, 3] = arrive(into[2, 3])
    into[2, 2] = inward(2, 2)
    crossed[1] = arrive(crossed[1])
    slab_came[0] = arrive(slab_came[0])
    act_came = arrive(act_came)
    middle[1] = send("middle", rest)
    came_far[0] = p.send(x_swap, leave_far[0])
    keep, leave = p.back(0, came_grads, own_pieces, far_pieces)
    [far2] = blended((part(2, 3), part(2, 3), into[2, 3]))
    into[2, 2] = arrive(into[2, 2])
    into[3, 3] = inward(3, 3)
    sums = did(jnp.concatenate([then(sums), p.unit_sums(p.sums[3])], axis=1))
    middle[1] = arrive(middle[1])
    crossed[2] = send("middle", far2)
    came_far[0] = arrive(came_far[0])
    came_x[0] = p.send(x_swap, leave[0])
    own_y[0] = p.send(y_swap, p.add(keep_far[0], came_far[0]))
    value, own2 = blended((part(3, 2), part(1, 1), crossed[1]), (part(2, 2), part(2, 2), into[2, 2]))
    act_mix = p.stitch(3, act_came)
    p.store(0, rows[0], slab_came[0])
    into[3, 3] = arrive(into[3, 3])
    into[3, 2] = final[1] = ends(value)
    rest = did(far_end(3))
    came_x[0] = arrive(came_x[0])
    came_far[1] = p.send(x_swap, leave_far[1])
    crossed[2] = arrive(crossed[2])
    crossed[3] = send("middle", rest)
    own_y[0] = arrive(own_y[0])
    p.crossed[3] = p.send(x_swap, act_mix)
    [value] = blended((part(2, 1), part(2, 1), crossed[2]))
    partial = p.first_grad(0, keep[0], came_x[0], own_y[0], pooled)
    grad = (p.unpool(0, keep[0], came_x[0], own_y[0], (), 0, 2),)
    into[3, 2] = final[1] = arrive(into[3, 2])
    into[2, 1] = final[2] = ends(value)
    last = did(plus(3, 2, into[3, 2]))
    came_far[1] = arrive(came_far[1])
    came_x[1] = p.send(x_swap, leave[1])
    crossed[3] = arrive(crossed[3])
    middle[2] = send("middle", own2)
    own_y[1] = p.send(y_swap, p.add(keep_far[1], came_far[1]))
    p.crossed[3] = arrive(p.crossed[3])
    [value] = blended((part(3, 1), part(3, 1), crossed[3]))
    grad = (p.unpool(0, keep[0], came_x[0], own_y[0], grad, 1, 2),)
    rows[1] = did(then(part(1, 0)) + edge(1))
    into[2, 1] = final[2] = arrive(into[2, 1])
    into[3, 1] = final[3] = ends(value)
    came_x[1] = arrive(came_x[1])
    slab_came[1] = p.send(x_swap, p.leaving(rows[1]))
    middle[2] = arrive(middle[2])
    middle[3] = send("middle", last)
    rows[2] = did(part(2, 0) + edge(2))
    slab_came[2] = p.send(x_swap, p.leaving(rows[2]))
    own_y[1] = arrive(own_y[1])
    partial = partial + p.first_grad(1, keep[1], came_x[1], own_y[1], pooled)
    partial = did(p.by_tower(partial).reshape(1, -1))
    partial_came = p.send(c_swap, partial)
    grad = p.unpool(1, keep[1], came_x[1], own_y[1], grad)
    into[3, 1] = final[3] = arrive(into[3, 1])
    partial = did(partial + then(partial_came))
    second_came = p.send(y_swap, jnp.concatenate([sums[2:], partial]))
    slab_came[1] = arrive(slab_came[1])
    middle[3] = arrive(middle[3])
    rows[3] = did(part(3, 0) + edge(3))
    slab_came[3] = p.send(x_swap, p.leaving(rows[3]))
    p.store(1, rows[1], slab_came[1])
    second_came = arrive(second_came)
    sums = did(jnp.concatenate([sums[:2], second_came[:1], partial + second_came[1:]]))
    sums_came = p.send(flipped, sums, "batch", 2)
    slab_came[2] = arrive(slab_came[2])
    p.store(2, rows[2], slab_came[2])
    sums = did(sums + then(sums_came))
    sums_came = p.send(flipped, sums, "batch", 4)
    slab_came[3] = arrive(slab_came[3])
    p.store(3, rows[3], slab_came[3])
    sums = did(sums + then(sums_came))
    sums_came = p.send(x_swap, sums)
    for j in range(3):
        p.crossed[j] = jnp.split(mixes_came, 3)[j]
    activations = did(p.activations())
    sums_came = then(sums_came)
    bias_grad, alpha2_grad = p.small_grads(jnp.concatenate([sums[:3], sums_came[:3]]))
    alpha1_grad = (sums[3] + sums_came[3]).reshape(2, 2, p.channels)
    input_grad = jnp.swapaxes(grad, 1, 2)
    return (activations, input_grad, p.weight_grad[0], bias_grad, alpha1_grad, alpha2_grad)


def plain_program(p):
    groups = slab_groups()
    p.keep_cross(p.send(y_swap, p.cross))
    p.load_cotangents()
    p.cot_across = p.send(y_swap, p.cot_mine)
    *features, pooled = p.mix(p.pool())
    feats = [features[:HALVES], [y_swap(part) for part in features[HALVES:]]]
    feats += [[x_swap(part) for part in block] for block in feats]
    feats += [[c_swap(part) for part in block] for block in feats]
    feats = [[(part, 0) for part in block] for block in feats]
    chunks = []
    for j in range(p.chunks):
        came = p.swap_cotangents([j])
        p.cots[j] = (came, p.send(y_swap, came))
        block = p.slab_weight(j, p.swap_weight(j))
        rows = lax.all_gather(block, "batch", axis=0, tiled=True, axis_index_groups=groups)
        chunks.append([(rows,)])
        [total] = p.chunk(j, feats, chunks[j])
        slab = lax.psum_scatter(total, "batch", scatter_dimension=0, tiled=True, axis_index_groups=groups)
        p.store(j, slab, p.send(x_swap, p.leaving(slab)))
        p.crossed[j] = p.send(x_swap, p.stitch(j, p.send(y_swap, p.acts[j])))
    sums = lax.psum(p.unit_sums(), "batch", axis_index_groups=groups)
    far = x_swap(sums)
    second = y_swap(jnp.concatenate([sums[2:], far[2:]]))
    bias_grad, alpha2_grad = p.small_grads(
        jnp.concatenate([sums[:2], second[:1], far[:2], second[1:]])
    )
    own_pieces = chunks
    far = [(c_swap(p.far_grads[j]), 0) for j in range(p.chunks)]
    far_pieces = [[(c_swap(term),) for [term] in chunk] for chunk in own_pieces]
    keep, leave = p.back(0, far, own_pieces, far_pieces)
    keep_far, leave_far = p.back(1, far, own_pieces, far_pieces)
    partial, grad = 0.0, ()
    for i in range(2):
        other = y_swap(p.add(keep_far[i], x_swap(leave_far[i])))
        came = x_swap(leave[i])
        partial = partial + p.first_grad(i, keep[i], came, other, pooled)
        grad = (p.unpool(i, keep[i], came, other, grad),)
    alpha1_grad = lax.psum(p.by_tower(partial), ("batch", "tower"))
    input_grad = jnp.swapaxes(grad[0], 1, 2)
    return (p.activations(), input_grad, p.weight_grad[0], bias_grad, alpha1_grad, alpha2_grad)


def shards(*args):
    return (line_program if is_line() else plain_program)(Program(*args))


def solution(mesh):
    in_specs = (
        P(("batch", "tower"), None, None, None),
        P(("batch", "tower")),
        P(),
        P("batch", "tower"),
        P("tower"),
        P(None, "tower"),
        P("batch", "tower"),
    )
    out_specs = (
        P("batch", "tower"),
        P(("batch", "tower"), None, None, None),
        P("batch", "tower"),
        P("tower"),
        P(),
        P(None, "tower"),
    )
    return jax.shard_map(shards, mesh=mesh, in_specs=in_specs, out_specs=out_specs, check_vma=False)
```

```python
import functools

import jax
import jax.numpy as jnp
from jax import lax
from jax.experimental import pallas as pl
from jax.experimental.pallas import tpu as pltpu
from jax.sharding import PartitionSpec as P

F32 = jnp.float32
BF16 = jnp.bfloat16
POOLED = 36
PITCH = 48
LANES = 128
VMEM_LIMIT = 56 * 1024 * 1024
SMALL = pl.CostEstimate(flops=1000, bytes_accessed=1000, transcendentals=0)
AHEAD = 2
IMAGE_BLOCK = 16
BLEND_STEPS = 4
HALVES = 2


def params():
    return pltpu.CompilerParams(vmem_limit_bytes=VMEM_LIMIT)


def flipped(value, axis, bit):
    pairs = [(source, source ^ bit) for source in range(lax.axis_size(axis))]
    return lax.ppermute(value, axis, pairs)


def x_swap(value):
    return flipped(value, "batch", 1)


def y_swap(value):
    return flipped(value, "tower", 2)


def c_swap(value):
    return flipped(value, "tower", 1)


def line(value, kind):
    steps = {
        "near": ((0, 1), (1, 0), (2, 3), (3, 2)),
        "middle": ((1, 2), (2, 1)),
        "outward": ((1, 0), (2, 3)),
        "inward": ((0, 1), (3, 2)),
    }[kind]
    pairs = [(2 * a + x, 2 * b + x) for a, b in steps for x in range(2)]
    return lax.ppermute(value, "batch", pairs)


def slab_groups():
    size = lax.axis_size("batch")
    return [list(range(x, size, 2)) for x in range(2)]


def after(value, *others):
    return lax.optimization_barrier((value, *others))[0]


class Order:
    def __init__(self):
        self.last = None

    def then(self, value):
        return value if self.last is None else after(value, self.last)

    def did(self, value):
        self.last = value
        return value


def is_line():
    return lax.axis_size("batch") == 8


def line_order(z):
    rows = jnp.array([[0, 1, 2, 3], [1, 0, 2, 3], [2, 3, 1, 0], [3, 2, 1, 0]])
    return rows[z]


def core_groups():
    return [[t, t + 1] for t in range(0, lax.axis_size("tower"), 2)]


def both_cores(value):
    return lax.all_gather(value, "tower", axis=0, tiled=True, axis_index_groups=core_groups())


def windows(order):
    map_pos = jnp.arange(169)[None, :]
    prow = (order // 6)[:, None]
    pcol = (order % 6)[:, None]
    qrow = map_pos // 13
    qcol = map_pos % 13
    inside = (
        (qrow >= 2 * prow) & (qrow <= 2 * prow + 2) & (qcol >= 2 * pcol) & (qcol <= 2 * pcol + 2)
    )
    return inside, (prow < 5) & (pcol < 5)


def spread_table(order):
    inside, small = windows(order)
    table = jnp.stack([inside, inside & small]).astype(BF16)
    table = jnp.pad(table, ((0, 0), (0, PITCH - POOLED), (0, 0)))
    both = table[:, None, :, :, None] * jnp.eye(2, dtype=BF16)[None, :, None, None, :]
    spread = jnp.swapaxes(both.reshape(2, 2 * PITCH, 338), 1, 2)
    return jnp.pad(jnp.concatenate([spread, spread], axis=2), ((0, 0), (0, 352 - 338), (0, 0)))


def mix_kernel(group, keep, first, summed, *refs):
    *feature_outs, pooled_out, own, other, pool0, pool1 = refs
    count, _, places, ch = summed.shape
    base = pl.program_id(0) * count

    def image(n, carry):
        scale = keep[group[base + n]]
        p0 = summed[n, 0] * scale
        p1 = summed[n, 1] * scale
        rows = pl.ds(pl.multiple_of(n * PITCH, PITCH), places)
        mixed0 = first[0:1, :] * p0 + first[1:2, :] * p1
        mixed1 = first[2:3, :] * p0 + first[3:4, :] * p1
        for hold, value in ((pool0, p0), (pool1, p1), (own, mixed0), (other, mixed1)):
            for h in range(ch // LANES):
                hold[h, rows, :] = value[:, h * LANES : (h + 1) * LANES]
        return carry

    lax.fori_loop(0, count, image, 0, unroll=2)
    per = POOLED // HALVES
    for p in range(POOLED):
        rows = pl.ds(p, count, stride=PITCH)
        for h in range(ch // LANES):
            lanes = slice(p * ch + h * LANES, p * ch + (h + 1) * LANES)
            part = slice((p % per) * ch + h * LANES, (p % per) * ch + (h + 1) * LANES)
            feature_outs[p // per][:, part] = own[h, rows, :].astype(BF16)
            feature_outs[HALVES + p // per][:, part] = other[h, rows, :].astype(BF16)
            pooled_out[0, :, lanes] = pool0[h, rows, :]
            pooled_out[1, :, lanes] = pool1[h, rows, :]


def mix(summed, group, keep, first):
    count, _, places, ch = summed.shape
    nb = IMAGE_BLOCK
    feats = places * ch
    features = [((count, feats // HALVES), BF16)] * (2 * HALVES)
    return pl.pallas_call(
        mix_kernel,
        grid_spec=pltpu.PrefetchScalarGridSpec(
            num_scalar_prefetch=1,
            grid=(count // nb,),
            in_specs=[
                pl.BlockSpec(keep.shape, lambda i, g: (0, 0, 0)),
                pl.BlockSpec((4, ch), lambda i, g: (0, 0)),
                pl.BlockSpec((nb, 2, places, ch), lambda i, g: (i, 0, 0, 0)),
            ],
            out_specs=[pl.BlockSpec((nb, feats // HALVES), lambda i, g: (i, 0))] * (2 * HALVES)
            + [pl.BlockSpec((2, nb, feats), lambda i, g: (0, i, 0))],
            scratch_shapes=[pltpu.VMEM((ch // LANES, nb * PITCH, LANES), F32)] * 4,
        ),
        out_shape=[jax.ShapeDtypeStruct(*f) for f in features]
        + [jax.ShapeDtypeStruct((2, count, feats), F32)],
        compiler_params=params(),
        cost_estimate=SMALL,
        name="mix",
    )(group, keep, first, summed)


def unpool_kernel(start, group, table, first, keep_in, came_in, other_in, pooled, *refs):
    out, sums, own, other = refs[-4:]
    count = out.shape[0]
    base = start + pl.program_id(0) * count
    ch = out.shape[3]
    places = out.shape[1]

    @pl.when(pl.program_id(0) == 0)
    def _():
        own[...] = jnp.zeros_like(own)
        other[...] = jnp.zeros_like(other)
        sums[...] = jnp.zeros_like(sums)

    for h in range(ch // LANES):
        totals = [0.0] * 4
        for p in range(POOLED):
            lanes = slice(p * ch + h * LANES, p * ch + (h + 1) * LANES)
            rows = pl.ds(p, count, stride=PITCH)
            g0 = keep_in[:, lanes].astype(F32) + came_in[:, lanes].astype(F32)
            g1 = other_in[:, lanes].astype(F32)
            own[h, rows, :] = g0
            other[h, rows, :] = g1
            for s in range(2):
                value = pooled[s, :, lanes]
                totals[s] = totals[s] + g0 * value
                totals[2 + s] = totals[2 + s] + g1 * value
        for k in range(4):
            sums[k, :, h * LANES : (h + 1) * LANES] += totals[k]

    def image(n, carry):
        window = table[group[base + n]]
        rows = pl.ds(pl.multiple_of(n * PITCH, PITCH), PITCH)
        g0, g1 = (
            jnp.concatenate([hold[h, rows, :] for h in range(ch // LANES)], axis=1) for hold in (own, other)
        )
        highs, lows = [], []
        for s in range(2):
            grad = (first[s : s + 1, :] * g0 + first[2 + s : 3 + s, :] * g1) * (1.0 / 9.0)
            highs.append(grad.astype(BF16))
            lows.append((grad - highs[s].astype(F32)).astype(BF16))
        parts = jnp.concatenate(highs + lows, axis=0)
        spread = jnp.dot(window, parts, preferred_element_type=F32).astype(BF16)
        out[n] = spread[: 2 * places].reshape(places, 2, ch)
        return carry

    lax.fori_loop(0, count, image, 0, unroll=2)


def unpool(keep, came, other, pooled, row, images, group, table, first, places, at, count, before=()):
    feats = keep.shape[1]
    ch = first.shape[1]
    nb = IMAGE_BLOCK
    rows = pl.BlockSpec((nb, feats), lambda i, g: (row // nb + i, 0))
    grad, sums = pl.pallas_call(
        functools.partial(unpool_kernel, at),
        grid_spec=pltpu.PrefetchScalarGridSpec(
            num_scalar_prefetch=1,
            grid=(images // nb,),
            in_specs=[
                pl.BlockSpec(table.shape, lambda i, g: (0, 0, 0)),
                pl.BlockSpec((4, ch), lambda i, g: (0, 0)),
                rows,
                rows,
                rows,
                pl.BlockSpec((2, nb, feats), lambda i, g: (0, at // nb + i, 0)),
            ]
            + [pl.BlockSpec(memory_space=pl.ANY)] * len(before),
            out_specs=[
                pl.BlockSpec((nb, places, 2, ch), lambda i, g: (at // nb + i, 0, 0, 0)),
                pl.BlockSpec((4, nb, ch), lambda i, g: (0, 0, 0)),
            ],
            scratch_shapes=[pltpu.VMEM((ch // LANES, nb * PITCH, LANES), F32)] * 2,
        ),
        out_shape=[jax.ShapeDtypeStruct((count, places, 2, ch), BF16), jax.ShapeDtypeStruct((4, nb, ch), F32)],
        input_output_aliases={7: 0} if before else {},
        compiler_params=params(),
        cost_estimate=SMALL,
        name="unpool",
    )(group, table, first, keep, came, other, pooled, *before)
    return grad, sums


def store_kernel(chunk, chunks, x, own, came, *refs):
    out, stay, go, sems = refs[-4:]
    rows, width = came.shape

    def columns(at):
        return out.at[:, pl.ds(pl.multiple_of(at * width, width), width)]

    source = own.at[pl.ds(pl.multiple_of(x[0] * rows, rows), rows), :]
    read = pltpu.make_async_copy(source, stay, sems.at[0])
    read.start()
    go[...] = came[...].astype(F32)
    write = pltpu.make_async_copy(go, columns((1 - x[0]) * chunks + chunk), sems.at[1])
    write.start()
    read.wait()
    write_own = pltpu.make_async_copy(stay, columns(x[0] * chunks + chunk), sems.at[2])
    write_own.start()
    write.wait()
    write_own.wait()


def store(own, came, x, chunk, chunks, shape, before=()):
    anywhere = pl.BlockSpec(memory_space=pl.ANY)
    return pl.pallas_call(
        functools.partial(store_kernel, chunk, chunks),
        in_specs=[pl.BlockSpec(memory_space=pltpu.SMEM), anywhere, pl.BlockSpec(memory_space=pltpu.VMEM)]
        + [anywhere] * len(before),
        out_specs=anywhere,
        out_shape=jax.ShapeDtypeStruct(shape, F32),
        scratch_shapes=[pltpu.VMEM(came.shape, F32)] * 2 + [pltpu.SemaphoreType.DMA((3,))],
        input_output_aliases={3: 0} if before else {},
        compiler_params=params(),
        cost_estimate=SMALL,
        name="store",
    )(x, own, came, *before)


def place_rows_kernel(places, *refs):
    *parts, out, sem = refs
    height, width = parts[0].shape[0] // 4, parts[0].shape[1]
    chunks = len(parts) // 2
    x, y, core = places[0], places[1], places[2]
    copies = []
    for i, part in enumerate(parts):
        side, j = i // chunks, i % chunks
        col = (jnp.where(x == side, 0, chunks) + j) * width
        cols = pl.ds(pl.multiple_of(col, width), width)
        for b in range(4):
            row = (2 * ((b % 2) ^ y) + ((b // 2) ^ core)) * height
            target = out.at[pl.ds(pl.multiple_of(row, height), height), cols]
            copies.append(pltpu.make_async_copy(part.at[pl.ds(b * height, height), :], target, sem.at[i, b]))
            copies[-1].start()
    for copy in copies:
        copy.wait()


def place_rows(places, own, other):
    parts = own + other
    rows, width = parts[0].shape
    return pl.pallas_call(
        place_rows_kernel,
        in_specs=[pl.BlockSpec(memory_space=pltpu.SMEM)] + [pl.BlockSpec(memory_space=pltpu.VMEM)] * len(parts),
        out_specs=pl.BlockSpec(memory_space=pl.ANY),
        out_shape=jax.ShapeDtypeStruct((rows, width * len(parts)), BF16),
        scratch_shapes=[pltpu.SemaphoreType.DMA((len(parts), 4))],
        compiler_params=params(),
        cost_estimate=SMALL,
        name="place_rows",
    )(places, *parts)


def blend_kernel(counts, roles, *refs):
    hold, in_sems, out_sems = refs[-3:]
    blocks, outs = refs[: sum(counts)], refs[sum(counts) : -3]
    rows = hold.shape[1] // BLEND_STEPS
    outer = roles[0] == 1

    def span(i):
        return pl.ds(i * rows, rows)

    def bring(block, k, i):
        return pltpu.make_async_copy(block.at[span(i), :], hold.at[k, span(i), :], in_sems.at[k, i])

    def leave(k, out, i):
        return pltpu.make_async_copy(hold.at[k, span(i), :], out.at[span(i), :], out_sems.at[k, i])

    groups, at = [], 0
    for count in counts:
        groups.append(blocks[at : at + count])
        at += count
    slots = [sum(max(count - 1, 1) for count in counts[:g]) for g in range(len(counts))]
    for g, (first, *rest) in enumerate(groups):
        for i in range(BLEND_STEPS):

            @pl.when(outer)
            def _(first=first, g=g, i=i):
                bring(first, slots[g], i).start()

            @pl.when(jnp.logical_not(outer))
            def _(rest=rest, g=g, i=i):
                for k, block in enumerate(rest):
                    bring(block, slots[g] + k, i).start()

    for g, (first, *rest) in enumerate(groups):
        for i in range(BLEND_STEPS):
            bring(first, slots[g], i).wait()
            if len(rest) > 1:

                @pl.when(jnp.logical_not(outer))
                def _(rest=rest, g=g, i=i):
                    for k in range(1, len(rest)):
                        bring(rest[k], slots[g] + k, i).wait()
                    total = sum(hold[slots[g] + k, span(i), :].astype(F32) for k in range(len(rest)))
                    hold[slots[g], span(i), :] = total.astype(BF16)

            leave(slots[g], outs[g], i).start()
    for g in range(len(groups)):
        for i in range(BLEND_STEPS):
            leave(slots[g], outs[g], i).wait()


def blend(roles, groups):
    counts = [len(group) for group in groups]
    shape = groups[0][0].shape
    slots = sum(max(count - 1, 1) for count in counts)
    anywhere = pl.BlockSpec(memory_space=pl.ANY)
    return pl.pallas_call(
        functools.partial(blend_kernel, counts),
        in_specs=[pl.BlockSpec(memory_space=pltpu.SMEM)] + [anywhere] * sum(counts),
        out_specs=[anywhere] * len(groups),
        out_shape=[jax.ShapeDtypeStruct(shape, BF16)] * len(groups),
        scratch_shapes=[
            pltpu.VMEM((slots, *shape), BF16),
            pltpu.SemaphoreType.DMA((slots, BLEND_STEPS)),
            pltpu.SemaphoreType.DMA((slots, BLEND_STEPS)),
        ],
        compiler_params=params(),
        cost_estimate=SMALL,
        name="blend",
    )(roles, *[block for group in groups for block in group])


def tile_of(rows):
    return next(t for t in (1152, 768, 576, 512, 384, 256, 128) if rows % t == 0)


def fetch(outer, terms, rows, target, sem):
    def copy(term):
        return pltpu.make_async_copy(term.at[rows, :], target, sem)

    if len(terms) == 1:
        copy(terms[0]).start()
    else:
        pl.when(outer == 1)(lambda: copy(terms[0]).start())
        pl.when(outer == 0)(lambda: copy(terms[1]).start())


def chunk_kernel(layout, starts, cot_cols, roles, vectors, *refs):
    chunks, count = len(layout), len(layout[0])
    cots, refs = refs[:4], refs[4:]
    blocks = len(starts) // HALVES
    feats, refs = refs[: blocks * HALVES], refs[blocks * HALVES :]
    at = 0
    pieces = []
    for counts in layout:
        pieces.append([])
        for many in counts:
            pieces[-1].append(refs[at : at + many])
            at += many
    act_out, keep_out, send_out, sums_out = refs[at : at + 4]
    outs = [refs[at + 4 + i * count : at + 4 + (i + 1) * count] for i in range(chunks)]
    held, weight, total, dpre_out, k_own, k_other, high, low, in_sems, w_sems, cot_sems, out_sems = refs[-12:]
    steps, images, tile = held.shape
    per = steps // count
    units = total.shape[1] // chunks
    half, height = steps // HALVES, images // blocks

    def columns(i):
        return slice(i * units, (i + 1) * units)

    def begin(k):
        for s in range(count):

            @pl.when(k // per == s)
            def _(s=s):
                rows = pl.ds(pl.multiple_of((k - s * per) * tile, tile), tile)
                for i in range(chunks):
                    fetch(roles[0], pieces[i][s], rows, weight.at[k, :, columns(i)], w_sems.at[k])

        for h in range(HALVES):

            @pl.when(k // half == h)
            def _(h=h):
                cols = pl.ds(pl.multiple_of((k - h * half) * tile, tile), tile)
                for r in range(blocks):
                    at = r * HALVES + h
                    start = starts[at]
                    if start is None:
                        start = pl.multiple_of(roles[1] * height, height)
                    part = feats[at].at[pl.ds(start, height), cols]
                    rows = pl.ds(r * height, height)
                    pltpu.make_async_copy(part, held.at[k, rows, :], in_sems.at[k]).start()

    def arrive(target, sem):
        pltpu.make_async_copy(target, target, sem).wait()

    ahead = min(AHEAD, steps)
    for k in range(ahead):
        begin(jnp.int32(k))
    for tower, target in enumerate((k_own, k_other)):
        for r in range(blocks):
            core, x, y = r // 4, r // 2 % 2, r % 2
            source, col = cots[2 * tower + x], cot_cols[2 * tower + x]
            rows = pl.ds((2 * core + (y ^ tower)) * height, height)
            source = source.at[rows, pl.ds(col, total.shape[1])]
            target_rows = target.at[pl.ds(r * height, height), :]
            pltpu.make_async_copy(source, target_rows, cot_sems.at[tower]).start()
    total[...] = jnp.zeros_like(total)

    def forward_step(k, carry):
        pl.when(k + ahead < steps)(lambda: begin(k + ahead))
        arrive(held.at[k], in_sems.at[k])
        arrive(weight.at[k], w_sems.at[k])
        total[...] += jnp.dot(held[k], weight[k], preferred_element_type=F32)
        return carry

    lax.fori_loop(0, steps, forward_step, 0)
    arrive(k_own, cot_sems.at[0])
    arrive(k_other, cot_sems.at[1])

    bias, own_coef, other_coef = (vectors[i : i + 1, :] for i in range(3))
    c = 0.7978845608028654
    block = 32

    def rows_of(i, sums):
        rows = pl.ds(pl.multiple_of(i * block, block), block)
        x = total[rows, :] + bias
        x2 = x * x
        t = jnp.tanh(c * (x + 0.044715 * (x2 * x)))
        half = 0.5 * (1.0 + t)
        act = (x * half).astype(BF16)
        slope = half + (0.5 * c) * x * (1.0 - t * t) * (1.0 + (3.0 * 0.044715) * x2)
        k0 = k_own[rows, :].astype(F32)
        k1 = k_other[rows, :].astype(F32)
        dpre = ((own_coef * k0 + other_coef * k1) * slope).astype(BF16)
        act_out[rows, :] = act
        dpre_out[rows, :] = dpre
        actf = act.astype(F32)

        def fold(v):
            return jnp.sum(v.reshape(block // 8, 8, v.shape[1]), axis=0)

        return (
            sums[0] + fold(dpre.astype(F32)),
            sums[1] + fold(k0 * actf),
            sums[2] + fold(k1 * actf),
        )

    zero = jnp.zeros((8, total.shape[1]), F32)
    sums = lax.fori_loop(0, images // block, rows_of, (zero, zero, zero))
    for i in range(3):
        sums_out[i : i + 1, :] = jnp.sum(sums[i], axis=0, keepdims=True)
    keep_out[...] = dpre_out[: images // 2]
    send_out[...] = dpre_out[images // 2 :]

    def product(k):
        return lax.dot_general(
            held[k], dpre_out[...], (((0,), (0,)), ((), ())), preferred_element_type=F32
        )

    def last_steps(k, carry):
        made = product(k).astype(BF16)
        for i in range(chunks):
            low[k - per, i] = made[:, columns(i)]
        for s in range(1, count):

            @pl.when(k // per == s)
            def _(s=s):
                rows = pl.ds(pl.multiple_of((k - s * per) * tile, tile), tile)
                for i in range(chunks):
                    pltpu.make_async_copy(low.at[k - per, i], outs[i][s].at[rows, :], out_sems.at[k]).start()

        return carry

    def first_steps(k, carry):
        made = product(k)
        rows = pl.ds(pl.multiple_of(k * tile, tile), tile)
        for i in range(chunks):
            high[k, i] = made[:, columns(i)]
            pltpu.make_async_copy(high.at[k, i], outs[i][0].at[rows, :], out_sems.at[k]).start()
        return carry

    if count > 1:
        lax.fori_loop(per, steps, last_steps, 0)
    lax.fori_loop(0, per, first_steps, 0)
    for k in range(steps):
        arrive(high.at[k] if k < per else low.at[k - per], out_sems.at[k])


def chunk(roles, feats, pieces, vectors, cots):
    images = len(feats) * feats[-1][-1][0].shape[0]
    units = pieces[0][0][0].shape[1]
    width = units * len(pieces)
    depth = sum(part.shape[1] for part, _ in feats[0])
    starts = [start for block in feats for _, start in block]
    count = len(pieces[0])
    height = pieces[0][0][0].shape[0]
    tile = tile_of(height)
    steps, per = depth // tile, height // tile
    terms = [term for chunk in pieces for piece in chunk for term in piece]
    anywhere = pl.BlockSpec(memory_space=pl.ANY)
    vmem = pl.BlockSpec(memory_space=pltpu.VMEM)
    kinds = ([F32] + [BF16] * (count - 1)) * len(pieces)
    return pl.pallas_call(
        functools.partial(chunk_kernel, [[len(p) for p in chunk] for chunk in pieces], starts, [c for _, c in cots]),
        in_specs=[pl.BlockSpec(memory_space=pltpu.SMEM), vmem]
        + [anywhere] * (len(cots) + len(feats) * HALVES + len(terms)),
        out_specs=[vmem] * 4 + [anywhere] * len(kinds),
        out_shape=[
            jax.ShapeDtypeStruct((images, width), BF16),
            jax.ShapeDtypeStruct((images // 2, width), BF16),
            jax.ShapeDtypeStruct((images // 2, width), BF16),
            jax.ShapeDtypeStruct((8, width), F32),
        ]
        + [jax.ShapeDtypeStruct((height, units), kind) for kind in kinds],
        scratch_shapes=[
            pltpu.VMEM((steps, images, tile), BF16),
            pltpu.VMEM((steps, tile, width), BF16),
            pltpu.VMEM((images, width), F32),
            pltpu.VMEM((images, width), BF16),
            pltpu.VMEM((images, width), BF16),
            pltpu.VMEM((images, width), BF16),
            pltpu.VMEM((per, len(pieces), tile, units), F32),
            pltpu.VMEM((max(steps - per, 1), len(pieces), tile, units), BF16),
            pltpu.SemaphoreType.DMA((steps,)),
            pltpu.SemaphoreType.DMA((steps,)),
            pltpu.SemaphoreType.DMA((2,)),
            pltpu.SemaphoreType.DMA((steps,)),
        ],
        compiler_params=params(),
        cost_estimate=SMALL,
        name="chunk",
    )(roles, vectors, *[cot for cot, _ in cots], *[part for block in feats for part, _ in block], *terms)


def back_kernel(layout, firsts, blocks, roles, *refs):
    outs = refs[-10:-6]
    grad, weight, made, grad_sems, w_sems, out_sems = refs[-6:]
    sources, count = len(layout), len(layout[0])
    grads = refs[:sources]
    at = sources
    pieces = []
    for counts in layout:
        pieces.append([])
        for many in counts:
            pieces[-1].append(refs[at : at + many])
            at += many
    slots, tile, total = weight.shape
    units = total // sources
    steps = made.shape[0]
    per = steps // count
    share = made.shape[1] // len(outs)

    def columns(j):
        return slice(j * units, (j + 1) * units)

    def begin(k):
        slot = lax.rem(k, slots)
        for s in range(count):

            @pl.when(k // per == s)
            def _(s=s):
                rows = pl.ds(pl.multiple_of((k - s * per) * tile, tile), tile)
                for j in range(sources):
                    fetch(roles[0], pieces[j][s], rows, weight.at[slot, :, columns(j)], w_sems.at[slot])

    def arrive(target, sem):
        pltpu.make_async_copy(target, target, sem).wait()

    copies = []
    for j in range(sources):
        for i, block in enumerate(blocks):
            rows = grad.shape[0] // len(blocks)
            source = grads[j].at[pl.ds(firsts[j] + block * rows, rows), :]
            target = grad.at[pl.ds(i * rows, rows), columns(j)]
            copies.append(pltpu.make_async_copy(source, target, grad_sems.at[j, i]))
            copies[-1].start()
    ahead = min(slots - 1, steps)
    for k in range(ahead):
        begin(jnp.int32(k))
    for copy in copies:
        copy.wait()

    def step(k, carry):
        pl.when(k + ahead < steps)(lambda: begin(k + ahead))
        slot = lax.rem(k, slots)
        arrive(weight.at[slot], w_sems.at[slot])
        made[k] = lax.dot_general(
            grad[...], weight[slot], (((1,), (1,)), ((), ())), preferred_element_type=F32
        ).astype(BF16)
        cols = pl.ds(pl.multiple_of(k * tile, tile), tile)
        for i, out in enumerate(outs):
            source = made.at[k, pl.ds(i * share, share), :]
            pltpu.make_async_copy(source, out.at[:, cols], out_sems.at[k]).start()
        return carry

    lax.fori_loop(0, steps, step, 0)
    for k in range(steps):
        arrive(made.at[k], out_sems.at[k])


def back(roles, grads, pieces, blocks):
    units = grads[0][0].shape[1]
    images = min(grad.shape[0] for grad, _ in grads) // 4 * len(blocks)
    count = len(pieces[0])
    height = pieces[0][0][0].shape[0]
    depth = height * count
    tile = next(t for t in (768, 512, 384, 256, 128) if height % t == 0)
    steps = depth // tile
    total = units * len(grads)
    terms = [term for chunk in pieces for piece in chunk for term in piece]
    layout = [[len(piece) for piece in chunk] for chunk in pieces]
    anywhere = pl.BlockSpec(memory_space=pl.ANY)
    return pl.pallas_call(
        functools.partial(back_kernel, layout, [row for _, row in grads], blocks),
        in_specs=[pl.BlockSpec(memory_space=pltpu.SMEM)] + [anywhere] * (len(grads) + len(terms)),
        out_specs=[anywhere] * 4,
        out_shape=[jax.ShapeDtypeStruct((images // 4, depth), BF16)] * 4,
        scratch_shapes=[
            pltpu.VMEM((images, total), BF16),
            pltpu.VMEM((AHEAD + 1, tile, total), BF16),
            pltpu.VMEM((steps, images, tile), BF16),
            pltpu.SemaphoreType.DMA((len(grads), len(blocks))),
            pltpu.SemaphoreType.DMA((AHEAD + 1,)),
            pltpu.SemaphoreType.DMA((steps,)),
        ],
        compiler_params=params(),
        cost_estimate=SMALL,
        name="back",
    )(roles, *[grad for grad, _ in grads], *terms)


def either(flag, value, axis):
    return jnp.where(flag, jnp.flip(value, axis), value)


class Program:
    def __init__(self, convmaps, group, alpha1, weight, bias, alpha2, cotangent):
        self.order = Order()
        self.convmaps, self.group, self.weight = convmaps, group, weight
        self.count, _, self.places, self.channels = convmaps.shape
        batch_id = lax.axis_index("batch")
        tower_id = lax.axis_index("tower")
        self.x, self.z = batch_id % 2, batch_id // 2
        self.y, self.core = tower_id // 2, tower_id % 2
        self.depth, self.width = weight.shape
        self.units = self.width // 2
        self.n = self.units // (4 if is_line() else 2)
        self.chunks = self.units // self.n
        self.images = 8 * self.count
        self.mine, self.theirs = self.x * self.units, (1 - self.x) * self.units
        units = self.units
        second = lax.dynamic_slice_in_dim(alpha2, self.mine, units, 1)
        self.own_coef = lax.dynamic_index_in_dim(second, self.y, 0, keepdims=True).astype(F32)
        self.cross = lax.dynamic_index_in_dim(second, 1 - self.y, 0, keepdims=True)
        own_bias = lax.dynamic_slice_in_dim(bias, self.mine, units, 0)[None, :].astype(F32)
        self.own_bias = own_bias
        self.cotangent = cotangent
        places = jnp.arange(POOLED)
        if is_line():
            places = places.reshape(4, -1)[line_order(self.z)].reshape(-1)
        self.table = spread_table(places)
        inside, small = windows(places)
        self.pool_table = inside.astype(BF16)
        keep = jnp.stack([jnp.ones_like(small), small]).astype(F32) * (1.0 / 9.0)
        self.keep = jnp.broadcast_to(keep, (2, POOLED, self.channels))
        self.first = either(self.y == 1, alpha1.astype(F32), 0).reshape(4, self.channels)
        self.is_outer = (self.z == 0) | (self.z == 3)
        self.roles = jnp.stack([self.is_outer.astype(jnp.int32), 1 - self.core])
        self.cots = {}
        self.places_of = jnp.stack([self.x, self.y, self.core]).astype(jnp.int32)
        self.weight_grad = ()
        self.acts, self.grads, self.far_grads, self.sums = {}, {}, {}, {}
        self.stitched, self.crossed = {}, {}

    def then(self, value):
        return self.order.then(value)

    def did(self, value):
        return self.order.did(value)

    def keep_cross(self, came):
        cross_back = self.did(self.then(came)).astype(F32)
        zeros = jnp.zeros((5, self.units), F32)
        self.vectors = jnp.concatenate([self.own_bias, self.own_coef, cross_back, zeros])
        self.cross = self.cross.astype(F32)

    def load_cotangents(self):
        cot = self.then(self.cotangent).reshape(2, 2, self.count, self.width)
        cot = either(self.core == 1, either(self.y == 1, cot, 0), 1).swapaxes(0, 1).reshape(-1, self.width)
        self.cot_mine = self.did(lax.dynamic_slice_in_dim(cot, self.mine, self.units, 1))
        self.cot_theirs = lax.dynamic_slice_in_dim(cot, self.theirs, self.units, 1)

    def pool(self):
        return jnp.einsum("pq,nsqc->nspc", self.pool_table, self.convmaps, preferred_element_type=F32)

    def mix(self, summed):
        return mix(summed, self.group, self.keep, self.first)

    def cols(self, j):
        return slice(j * self.n, (j + 1) * self.n)

    def span(self, js):
        return slice(js[0] * self.n, (js[-1] + 1) * self.n)

    def weight_part(self, start, j, many=1):
        return lax.dynamic_slice(self.then(self.weight), (0, start + j * self.n), (self.depth, many * self.n))

    def swap_weight(self, j, many=1):
        return self.send(x_swap, self.weight_part(self.theirs, j, many))

    def slab_weight(self, j, came):
        a, b = self.weight_part(self.mine, j), self.then(came)
        return self.did(jnp.where(self.x == 0, jnp.concatenate([a, b]), jnp.concatenate([b, a])))

    def swap_cotangents(self, js):
        return self.send(x_swap, self.cot_theirs[:, self.span(js)])

    def cots_of(self, j):
        here, there = self.cots[j]
        first = (j - min(i for i in self.cots if self.cots[i][0] is here)) * self.n
        return [(self.cot_mine, j * self.n), (here, first), (self.cot_across, j * self.n), (there, first)]

    def send(self, move, value, *args):
        return move(self.did(self.then(value)), *args)

    def chunk(self, j, feats, pieces):
        act, keep, send, sums, *products = chunk(
            self.roles,
            feats,
            [pieces],
            self.then(self.vectors[:, self.cols(j)]),
            self.cots_of(j),
        )
        self.did(act)
        self.acts[j], self.grads[j], self.far_grads[j], self.sums[j] = act, keep, send, sums
        return products

    def stitch(self, j, came):
        cols = self.cols(j)
        other_act = jnp.flip(self.then(came).reshape(4, 2, self.count, self.n), 1).reshape(self.images, self.n)
        mix = self.own_coef[:, cols] * self.acts[j].astype(F32) + self.cross[:, cols] * other_act.astype(F32)
        mix = self.did(mix.astype(BF16)).reshape(2, 2, 2 * self.count, self.n)
        self.stitched[j] = mix[:, 0].reshape(-1, self.n)
        return mix[:, 1].reshape(-1, self.n)

    def leaving(self, slab):
        return lax.dynamic_slice_in_dim(slab, (1 - self.x) * self.depth, self.depth, 0).astype(BF16)

    def store(self, j, rows, came):
        shape = (self.depth, self.width)
        made = store(self.then(rows), came, self.places_of, j, self.chunks, shape, self.weight_grad)
        self.weight_grad = (self.did(made),)

    def activations(self):
        own, other = ([parts[j] for j in range(self.chunks)] for parts in (self.stitched, self.crossed))
        return place_rows(self.places_of, [self.then(own[0])] + own[1:], other)

    def unit_sums(self, *parts):
        return jnp.concatenate([part[:3] for part in parts or self.sums.values()], axis=1)

    def small_grads(self, sums):
        mine, far = sums[:3], sums[3:6]
        wide = jnp.where(
            self.x == 0, jnp.concatenate([mine, far], -1), jnp.concatenate([far, mine], -1)
        )
        return wide[0], either(self.y == 1, wide[1:3], 0)

    def back(self, y, came_grads, pieces, came_pieces):
        chunks = range(self.chunks)
        grads = [(self.grads[j], 0) for j in chunks] + list(came_grads)
        grads[0] = (self.then(grads[0][0]), 0)
        parts = back(
            self.roles,
            grads,
            [pieces[j] for j in chunks] + [came_pieces[j] for j in chunks],
            [y, 2 + y],
        )
        self.did(parts[0])
        return parts[:2], parts[2:]

    def add(self, keep, came):
        return self.did((keep.astype(F32) + self.then(came).astype(F32)).astype(BF16))

    def by_tower(self, partial):
        return either(self.y == 1, partial.reshape(2, 2, self.channels), 0)

    def unpool(self, i, keep, came, other, pooled, before=(), part=0, parts=1):
        images = keep.shape[0] // parts
        grad, sums = unpool(
            self.then(keep),
            came,
            other,
            pooled,
            part * images,
            images,
            self.group,
            self.table,
            self.first,
            self.places,
            i * keep.shape[0] + part * images,
            self.count,
            before,
        )
        return (self.did(grad),), sums


def line_program(p):
    then, did = p.then, p.did
    came, blocks, near, inner, outer, first_out, last_out = {}, {}, {}, {}, {}, {}, {}
    total, into, crossed, middle, final, slab_came = {}, {}, {}, {}, {}, {}
    from_own, swapped = {}, {}

    def send(kind, value):
        return p.send(line, value, kind)

    def arrive(value):
        return did(then(value))

    def block(j):
        blocks[j] = p.slab_weight(j, came[j])

    def pieces(j):
        beside = (near[j],) if j < 2 else (from_own[j], swapped[j])
        return [(blocks[j],), beside, (first_out[j], inner[j]), (last_out[j], outer[j])]

    def part(j, s):
        return total[j][s]

    def payload(inward, outward):
        return did(jnp.where(p.is_outer, then(inward), outward))

    def ends(value):
        return send("near", value)

    def inward(j, s):
        return send("inward", then(part(j, s)))

    def plus(j, s, value):
        return (part(j, s).astype(F32) + then(value).astype(F32)).astype(BF16)

    def edge(j):
        return jnp.where(
            p.is_outer, then(final[j]).astype(F32), into[j, 1].astype(F32) + middle[j].astype(F32)
        )

    def blended(*groups):
        (first, *rest), *others = groups
        made = blend(p.roles, [(then(first), *rest)] + others)
        did(made[0])
        return made

    def pick(a, b):
        return did(jnp.where(p.is_outer, then(a), b))

    def core_swap(j, s):
        came_pieces[j, s] = p.send(c_swap, picked[j, s])

    def core_came(j, s):
        came_pieces[j, s] = arrive(came_pieces[j, s])

    picked, came_pieces = {}, {}

    def far_end(j):
        return plus(j, 3, into[j, 3])

    came[0] = p.swap_weight(0)
    came[1] = p.swap_weight(1)
    cross_came = p.send(y_swap, p.cross)
    p.load_cotangents()
    p.keep_cross(cross_came)
    p.table = did(then(p.table))
    came[0] = arrive(came[0])
    block(0)
    near[0] = ends(blocks[0])
    inner[0] = send("middle", blocks[0])
    came_pair = p.swap_weight(2, 2)
    p.cot_across = p.send(y_swap, p.cot_mine)
    p.pool_table = then(p.pool_table)
    summed = did(p.pool())
    came[1] = arrive(came[1])
    cot_came = p.swap_cotangents([0, 1])
    block(1)
    near[0] = arrive(near[0])
    near[1] = ends(blocks[1])
    inner[0] = arrive(inner[0])
    inner[1] = send("middle", blocks[1])
    kept_a, kept_b, sent_a, sent_b, pooled = p.mix(then(summed))
    did(kept_a)
    came_pair = arrive(came_pair)
    p.cot_across = arrive(p.cot_across)
    cot_came = arrive(cot_came)
    x_a = p.send(x_swap, kept_a)
    y_a = p.send(y_swap, sent_a)
    c_kept_a = p.send(c_swap, kept_a)
    came[2], came[3] = came_pair[:, : p.n], came_pair[:, p.n :]
    block(2)
    near[1] = arrive(near[1])
    first_out[0] = send("outward", inner[0])
    inner[1] = arrive(inner[1])
    outer[0] = send("middle", near[0])
    x_a = arrive(x_a)
    x_b = p.send(x_swap, kept_b)
    y_a = arrive(y_a)
    y_b = p.send(y_swap, sent_b)
    c_kept_a = arrive(c_kept_a)
    c_kept_b = p.send(c_swap, kept_b)
    block(3)
    first_out[0] = arrive(first_out[0])
    first_out[1] = send("outward", inner[1])
    outer[0] = arrive(outer[0])
    outer[1] = send("middle", near[1])
    x_b = arrive(x_b)
    x_y_a = p.send(x_swap, y_a)
    y_b = arrive(y_b)
    cot_crossed = p.send(y_swap, cot_came)
    c_kept_b = arrive(c_kept_b)
    c_x_a = p.send(c_swap, x_a)
    value = payload(blocks[2], outer[0])
    first_out[1] = arrive(first_out[1])
    swapped[2] = last_out[0] = ends(value)
    outer[1] = arrive(outer[1])
    inner[2] = send("middle", blocks[2])
    x_y_a = arrive(x_y_a)
    x_y_b = p.send(x_swap, y_b)
    p.cots[0] = p.cots[1] = (cot_came, arrive(cot_crossed))
    c_x_a = arrive(c_x_a)
    c_y_a = p.send(c_swap, y_a)
    c_x_b = p.send(c_swap, x_b)
    value = payload(blocks[3], outer[1])
    for j in range(4):
        picked[j, 0] = blocks[j]
    picked[0, 1], picked[1, 1] = near[0], near[1]
    swapped[2] = last_out[0] = arrive(swapped[2])
    swapped[3] = last_out[1] = ends(value)
    inner[2] = arrive(inner[2])
    outer[2] = send("middle", swapped[2])
    x_y_b = arrive(x_y_b)
    c_y_a = arrive(c_y_a)
    c_x_b = arrive(c_x_b)
    c_y_b = p.send(c_swap, y_b)
    c_x_y_a = p.send(c_swap, x_y_a)
    c_x_y_b = p.send(c_swap, x_y_b)
    swapped[3] = last_out[1] = arrive(swapped[3])
    from_own[2] = send("outward", blocks[2])
    p.vectors = did(then(p.vectors))
    c_y_b = arrive(c_y_b)
    c_x_y_a = arrive(c_x_y_a)
    c_x_y_b = arrive(c_x_y_b)
    core_swap(0, 0)
    core_swap(0, 1)
    cot_came = p.swap_cotangents([2, 3])
    feats = [
        [(kept_a, 0), (kept_b, 0)],
        [(y_a, 0), (y_b, 0)],
        [(x_a, 0), (x_b, 0)],
        [(x_y_a, 0), (x_y_b, 0)],
        [(c_kept_a, 0), (c_kept_b, 0)],
        [(c_y_a, 0), (c_y_b, 0)],
        [(c_x_a, 0), (c_x_b, 0)],
        [(c_x_y_a, 0), (c_x_y_b, 0)],
    ]
    total[0] = p.chunk(0, feats, pieces(0))
    outer[2] = arrive(outer[2])
    value = payload(part(0, 3), inner[2])
    from_own[2] = arrive(from_own[2])
    into[0, 3] = first_out[2] = ends(value)
    core_came(0, 0)
    core_came(0, 1)
    cot_came = arrive(cot_came)
    inner[3] = send("middle", blocks[3])
    act_came = p.send(y_swap, p.acts[0])
    core_swap(1, 0)
    core_swap(1, 1)
    total[1] = p.chunk(1, feats, pieces(1))
    value = payload(part(0, 2), outer[2])
    into[0, 3] = first_out[2] = arrive(into[0, 3])
    into[0, 2] = last_out[2] = ends(value)
    far0 = did(far_end(0))
    inner[3] = arrive(inner[3])
    outer[3] = send("middle", swapped[3])
    cot_crossed = p.send(y_swap, cot_came)
    act_came = arrive(act_came)
    core_came(1, 0)
    core_came(1, 1)
    core_swap(2, 0)
    core_swap(3, 0)
    picked[0, 2], picked[1, 2], picked[0, 3], picked[1, 3], picked[2, 1], picked[2, 2], value = blended(
        (first_out[0], inner[0]),
        (first_out[1], inner[1]),
        (last_out[0], outer[0]),
        (last_out[1], outer[1]),
        (from_own[2], swapped[2]),
        (first_out[2], inner[2]),
        (part(0, 1), blocks[3]),
    )
    act_mixes = [p.stitch(0, act_came)]
    cot_crossed = arrive(cot_crossed)
    into[0, 2] = last_out[2] = arrive(into[0, 2])
    into[0, 1] = from_own[3] = ends(value)
    p.cots[2] = p.cots[3] = (cot_came, cot_crossed)
    core_came(2, 0)
    core_came(3, 0)
    core_swap(0, 2)
    core_swap(1, 2)
    core_swap(2, 1)
    total[2] = p.chunk(2, feats, pieces(2))
    outer[3] = arrive(outer[3])
    [value] = blended((part(1, 3), inner[3]))
    into[0, 1] = from_own[3] = arrive(into[0, 1])
    into[1, 3] = first_out[3] = ends(value)
    rest = did(plus(0, 2, into[0, 2]))
    crossed[0] = send("middle", far0)
    core_came(0, 2)
    core_came(1, 2)
    core_came(2, 1)
    acts_came = p.send(y_swap, jnp.concatenate([then(p.acts[1]), p.acts[2]], axis=1))
    core_swap(0, 3)
    core_swap(1, 3)
    value, picked[3, 1], picked[2, 3] = blended(
        (part(1, 2), outer[3]), (from_own[3], swapped[3]), (last_out[2], outer[2])
    )
    into[1, 3] = first_out[3] = arrive(into[1, 3])
    into[1, 2] = last_out[3] = ends(value)
    far1 = did(far_end(1))
    crossed[0] = arrive(crossed[0])
    middle[0] = send("middle", rest)
    acts_came = arrive(acts_came)
    core_came(0, 3)
    core_came(1, 3)
    core_swap(2, 2)
    core_swap(3, 1)
    core_swap(2, 3)
    value, picked[3, 2] = blended((part(1, 1), part(0, 1), crossed[0]), (first_out[3], inner[3]))
    far = did(jnp.concatenate([then(p.far_grads[0]), p.far_grads[1], p.far_grads[2]]))
    for j in (1, 2):
        act_mixes.append(p.stitch(j, acts_came[:, (j - 1) * p.n : j * p.n]))
    act_mixes = did(jnp.concatenate([then(act_mixes[0]), *act_mixes[1:]]))
    into[1, 2] = last_out[3] = arrive(into[1, 2])
    into[1, 1] = final[0] = ends(value)
    sums = did(p.unit_sums(then(p.sums[0]), p.sums[1], p.sums[2]))
    core_came(2, 2)
    core_came(3, 1)
    core_came(2, 3)
    core_swap(3, 2)
    came_outer = p.send(c_swap, outer[3])
    mixes_came = p.send(x_swap, act_mixes)
    total[3] = p.chunk(3, feats, pieces(3))
    middle[0] = arrive(middle[0])
    into[1, 1] = final[0] = arrive(into[1, 1])
    into[2, 3] = inward(2, 3)
    core_came(3, 2)
    came_outer = arrive(came_outer)
    mixes_came = arrive(mixes_came)
    far = p.send(c_swap, far)
    came_last = p.send(c_swap, last_out[3])
    far3 = p.send(c_swap, p.far_grads[3])
    crossed[1] = send("middle", far1)
    rows = {0: did(then(part(0, 0)) + edge(0))}
    far = arrive(far)
    slab_came[0] = p.send(x_swap, p.leaving(rows[0]))
    came_last = arrive(came_last)
    far3 = arrive(far3)
    act_came = p.send(y_swap, p.acts[3])
    third = far.shape[0] // 3
    came_grads = [(far, 0), (far, third), (far, 2 * third), (far3, 0)]
    picked[3, 3], came_pieces[3, 3] = (last_out[3], outer[3]), (came_last, came_outer)
    own_pieces, far_pieces = (
        [[terms if isinstance(terms := kind[j, s], tuple) else (terms,) for s in range(4)] for j in range(4)]
        for kind in (picked, came_pieces)
    )
    keep_far, leave_far = p.back(1, came_grads, own_pieces, far_pieces)
    came_far, came_x, own_y = {}, {}, {}
    into[2, 3] = arrive(into[2, 3])
    into[2, 2] = inward(2, 2)
    [rest] = blended((part(1, 2), part(1, 2), into[1, 2]))
    crossed[1] = arrive(crossed[1])
    slab_came[0] = arrive(slab_came[0])
    act_came = arrive(act_came)
    middle[1] = send("middle", rest)
    came_far[0] = p.send(x_swap, leave_far[0])
    keep, leave = p.back(0, came_grads, own_pieces, far_pieces)
    into[2, 2] = arrive(into[2, 2])
    into[3, 3] = inward(3, 3)
    [far2] = blended((part(2, 3), part(2, 3), into[2, 3]))
    middle[1] = arrive(middle[1])
    crossed[2] = send("middle", far2)
    came_far[0] = arrive(came_far[0])
    came_x[0] = p.send(x_swap, leave[0])
    own_y[0] = p.send(y_swap, p.add(keep_far[0], came_far[0]))
    value, own2 = blended((part(3, 2), part(1, 1), crossed[1]), (part(2, 2), part(2, 2), into[2, 2]))
    sums = jnp.concatenate([sums, p.unit_sums(p.sums[3])], axis=1)
    act_mix = p.stitch(3, act_came)
    for j in range(3):
        p.crossed[j] = did(then(mixes_came)[j * p.n * 2 : (j + 1) * p.n * 2])
    p.store(0, rows[0], slab_came[0])
    into[3, 3] = arrive(into[3, 3])
    into[3, 2] = final[1] = ends(value)
    rest = did(far_end(3))
    came_x[0] = arrive(came_x[0])
    came_far[1] = p.send(x_swap, leave_far[1])
    crossed[2] = arrive(crossed[2])
    crossed[3] = send("middle", rest)
    own_y[0] = arrive(own_y[0])
    [value] = blended((part(2, 1), part(2, 1), crossed[2]))
    grad, partial_a = p.unpool(0, keep[0], came_x[0], own_y[0], pooled, (), 0, 2)
    into[3, 2] = final[1] = arrive(into[3, 2])
    into[2, 1] = final[2] = ends(value)
    last = did(plus(3, 2, into[3, 2]))
    came_far[1] = arrive(came_far[1])
    came_x[1] = p.send(x_swap, leave[1])
    crossed[3] = arrive(crossed[3])
    middle[2] = send("middle", own2)
    own_y[1] = p.send(y_swap, p.add(keep_far[1], came_far[1]))
    p.crossed[3] = p.send(x_swap, act_mix)
    [value] = blended((part(3, 1), part(3, 1), crossed[3]))
    grad, partial_b = p.unpool(0, keep[0], came_x[0], own_y[0], pooled, grad, 1, 2)
    into[2, 1] = final[2] = arrive(into[2, 1])
    into[3, 1] = final[3] = ends(value)
    came_x[1] = arrive(came_x[1])
    middle[2] = arrive(middle[2])
    middle[3] = send("middle", last)
    rows[1] = did(then(part(1, 0)) + edge(1))
    slab_came[1] = p.send(x_swap, p.leaving(rows[1]))
    own_y[1] = arrive(own_y[1])
    p.crossed[3] = arrive(p.crossed[3])
    rows[2] = did(part(2, 0) + edge(2))
    slab_came[2] = p.send(x_swap, p.leaving(rows[2]))
    [grad], partial = p.unpool(1, keep[1], came_x[1], own_y[1], pooled, grad)
    into[3, 1] = final[3] = arrive(into[3, 1])
    middle[3] = arrive(middle[3])
    partial = jnp.sum(then(partial_a) + partial_b + partial, axis=1)
    partial = did(p.by_tower(partial).reshape(1, -1))
    partial_came = p.send(c_swap, partial)
    slab_came[1] = arrive(slab_came[1])
    rows[3] = did(part(3, 0) + edge(3))
    slab_came[3] = p.send(x_swap, p.leaving(rows[3]))
    partial = did(partial + then(partial_came))
    second_came = p.send(y_swap, jnp.concatenate([sums[2:], partial]))
    p.store(1, rows[1], slab_came[1])
    second_came = arrive(second_came)
    sums = did(jnp.concatenate([sums[:2], second_came[:1], partial + second_came[1:]]))
    sums_came = p.send(flipped, sums, "batch", 2)
    slab_came[2] = arrive(slab_came[2])
    p.store(2, rows[2], slab_came[2])
    sums = did(sums + then(sums_came))
    sums_came = p.send(flipped, sums, "batch", 4)
    activations = did(p.activations())
    sums = did(sums + then(sums_came))
    sums_came = p.send(x_swap, sums)
    slab_came[3] = arrive(slab_came[3])
    p.store(3, rows[3], slab_came[3])
    sums_came = then(sums_came)
    bias_grad, alpha2_grad = p.small_grads(jnp.concatenate([sums[:3], sums_came[:3]]))
    alpha1_grad = (sums[3] + sums_came[3]).reshape(2, 2, p.channels)
    input_grad = jnp.swapaxes(grad, 1, 2)
    return (activations, input_grad, p.weight_grad[0], bias_grad, alpha1_grad, alpha2_grad)


def plain_program(p):
    groups = slab_groups()
    p.keep_cross(p.send(y_swap, p.cross))
    p.load_cotangents()
    p.cot_across = p.send(y_swap, p.cot_mine)
    *features, pooled = p.mix(p.pool())
    feats = [features[:HALVES], [y_swap(part) for part in features[HALVES:]]]
    feats += [[x_swap(part) for part in block] for block in feats]
    feats += [[c_swap(part) for part in block] for block in feats]
    feats = [[(part, 0) for part in block] for block in feats]
    chunks = []
    for j in range(p.chunks):
        came = p.swap_cotangents([j])
        p.cots[j] = (came, p.send(y_swap, came))
        block = p.slab_weight(j, p.swap_weight(j))
        rows = lax.all_gather(block, "batch", axis=0, tiled=True, axis_index_groups=groups)
        chunks.append([(rows,)])
        [total] = p.chunk(j, feats, chunks[j])
        slab = lax.psum_scatter(total, "batch", scatter_dimension=0, tiled=True, axis_index_groups=groups)
        p.store(j, slab, p.send(x_swap, p.leaving(slab)))
        p.crossed[j] = p.send(x_swap, p.stitch(j, p.send(y_swap, p.acts[j])))
    sums = lax.psum(p.unit_sums(), "batch", axis_index_groups=groups)
    far = x_swap(sums)
    second = y_swap(jnp.concatenate([sums[2:], far[2:]]))
    bias_grad, alpha2_grad = p.small_grads(
        jnp.concatenate([sums[:2], second[:1], far[:2], second[1:]])
    )
    own_pieces = chunks
    far = [(c_swap(p.far_grads[j]), 0) for j in range(p.chunks)]
    far_pieces = [[(c_swap(term),) for [term] in chunk] for chunk in own_pieces]
    keep, leave = p.back(0, far, own_pieces, far_pieces)
    keep_far, leave_far = p.back(1, far, own_pieces, far_pieces)
    partial, grad = 0.0, ()
    for i in range(2):
        other = y_swap(p.add(keep_far[i], x_swap(leave_far[i])))
        came = x_swap(leave[i])
        grad, sums = p.unpool(i, keep[i], came, other, pooled, grad)
        partial = partial + jnp.sum(sums, axis=1)
    alpha1_grad = lax.psum(p.by_tower(partial), ("batch", "tower"))
    input_grad = jnp.swapaxes(grad[0], 1, 2)
    return (p.activations(), input_grad, p.weight_grad[0], bias_grad, alpha1_grad, alpha2_grad)


def shards(*args):
    return (line_program if is_line() else plain_program)(Program(*args))


def solution(mesh):
    in_specs = (
        P(("batch", "tower"), None, None, None),
        P(("batch", "tower")),
        P(),
        P("batch", "tower"),
        P("tower"),
        P(None, "tower"),
        P("batch", "tower"),
    )
    out_specs = (
        P("batch", "tower"),
        P(("batch", "tower"), None, None, None),
        P("batch", "tower"),
        P("tower"),
        P(),
        P(None, "tower"),
    )
    return jax.shard_map(shards, mesh=mesh, in_specs=in_specs, out_specs=out_specs, check_vma=False)
```

```python
import functools

import jax
import jax.numpy as jnp
from jax import lax
from jax.experimental import pallas as pl
from jax.experimental.pallas import tpu as pltpu
from jax.sharding import PartitionSpec as P

F32 = jnp.float32
BF16 = jnp.bfloat16
POOLED = 36
PITCH = 48
LANES = 128
VMEM_LIMIT = 56 * 1024 * 1024
SMALL = pl.CostEstimate(flops=1000, bytes_accessed=1000, transcendentals=0)
AHEAD = 2
IMAGE_BLOCK = 16
BLEND_STEPS = 4
HALVES = 2


def params():
    return pltpu.CompilerParams(vmem_limit_bytes=VMEM_LIMIT)


def flipped(value, axis, bit):
    pairs = [(source, source ^ bit) for source in range(lax.axis_size(axis))]
    return lax.ppermute(value, axis, pairs)


def x_swap(value):
    return flipped(value, "batch", 1)


def y_swap(value):
    return flipped(value, "tower", 2)


def c_swap(value):
    return flipped(value, "tower", 1)


def line(value, kind):
    steps = {
        "near": ((0, 1), (1, 0), (2, 3), (3, 2)),
        "middle": ((1, 2), (2, 1)),
        "outward": ((1, 0), (2, 3)),
        "inward": ((0, 1), (3, 2)),
    }[kind]
    pairs = [(2 * a + x, 2 * b + x) for a, b in steps for x in range(2)]
    return lax.ppermute(value, "batch", pairs)


def slab_groups():
    size = lax.axis_size("batch")
    return [list(range(x, size, 2)) for x in range(2)]


def after(value, *others):
    return lax.optimization_barrier((value, *others))[0]


class Order:
    def __init__(self):
        self.last = None

    def then(self, value):
        return value if self.last is None else after(value, self.last)

    def did(self, value):
        self.last = value
        return value


def is_line():
    return lax.axis_size("batch") == 8


def line_order(z):
    rows = jnp.array([[0, 1, 2, 3], [1, 0, 2, 3], [2, 3, 1, 0], [3, 2, 1, 0]])
    return rows[z]


def core_groups():
    return [[t, t + 1] for t in range(0, lax.axis_size("tower"), 2)]


def both_cores(value):
    return lax.all_gather(value, "tower", axis=0, tiled=True, axis_index_groups=core_groups())


def windows(order):
    map_pos = jnp.arange(169)[None, :]
    prow = (order // 6)[:, None]
    pcol = (order % 6)[:, None]
    qrow = map_pos // 13
    qcol = map_pos % 13
    inside = (
        (qrow >= 2 * prow) & (qrow <= 2 * prow + 2) & (qcol >= 2 * pcol) & (qcol <= 2 * pcol + 2)
    )
    return inside, (prow < 5) & (pcol < 5)


def spread_table(order):
    inside, small = windows(order)
    table = jnp.stack([inside, inside & small]).astype(BF16)
    table = jnp.pad(table, ((0, 0), (0, PITCH - POOLED), (0, 0)))
    both = table[:, None, :, :, None] * jnp.eye(2, dtype=BF16)[None, :, None, None, :]
    spread = jnp.swapaxes(both.reshape(2, 2 * PITCH, 338), 1, 2)
    return jnp.pad(jnp.concatenate([spread, spread], axis=2), ((0, 0), (0, 352 - 338), (0, 0)))


def mix_kernel(group, keep, first, summed, *refs):
    *feature_outs, pooled_out, own, other, pool0, pool1 = refs
    count, _, places, ch = summed.shape
    base = pl.program_id(0) * count

    def image(n, carry):
        scale = keep[group[base + n]]
        p0 = summed[n, 0] * scale
        p1 = summed[n, 1] * scale
        rows = pl.ds(pl.multiple_of(n * PITCH, PITCH), places)
        mixed0 = first[0:1, :] * p0 + first[1:2, :] * p1
        mixed1 = first[2:3, :] * p0 + first[3:4, :] * p1
        for hold, value in ((pool0, p0), (pool1, p1), (own, mixed0), (other, mixed1)):
            for h in range(ch // LANES):
                hold[h, rows, :] = value[:, h * LANES : (h + 1) * LANES]
        return carry

    lax.fori_loop(0, count, image, 0, unroll=2)
    per = POOLED // HALVES
    for p in range(POOLED):
        rows = pl.ds(p, count, stride=PITCH)
        for h in range(ch // LANES):
            lanes = slice(p * ch + h * LANES, p * ch + (h + 1) * LANES)
            part = slice((p % per) * ch + h * LANES, (p % per) * ch + (h + 1) * LANES)
            feature_outs[p // per][:, part] = own[h, rows, :].astype(BF16)
            feature_outs[HALVES + p // per][:, part] = other[h, rows, :].astype(BF16)
            pooled_out[0, :, lanes] = pool0[h, rows, :]
            pooled_out[1, :, lanes] = pool1[h, rows, :]


def mix(summed, group, keep, first):
    count, _, places, ch = summed.shape
    nb = IMAGE_BLOCK
    feats = places * ch
    features = [((count, feats // HALVES), BF16)] * (2 * HALVES)
    return pl.pallas_call(
        mix_kernel,
        grid_spec=pltpu.PrefetchScalarGridSpec(
            num_scalar_prefetch=1,
            grid=(count // nb,),
            in_specs=[
                pl.BlockSpec(keep.shape, lambda i, g: (0, 0, 0)),
                pl.BlockSpec((4, ch), lambda i, g: (0, 0)),
                pl.BlockSpec((nb, 2, places, ch), lambda i, g: (i, 0, 0, 0)),
            ],
            out_specs=[pl.BlockSpec((nb, feats // HALVES), lambda i, g: (i, 0))] * (2 * HALVES)
            + [pl.BlockSpec((2, nb, feats), lambda i, g: (0, i, 0))],
            scratch_shapes=[pltpu.VMEM((ch // LANES, nb * PITCH, LANES), F32)] * 4,
        ),
        out_shape=[jax.ShapeDtypeStruct(*f) for f in features]
        + [jax.ShapeDtypeStruct((2, count, feats), F32)],
        compiler_params=params(),
        cost_estimate=SMALL,
        name="mix",
    )(group, keep, first, summed)


def unpool_kernel(start, group, table, first, keep_in, came_in, other_in, pooled, *refs):
    out, sums, own, other = refs[-4:]
    count = out.shape[0]
    base = start + pl.program_id(0) * count
    ch = out.shape[3]
    places = out.shape[1]

    @pl.when(pl.program_id(0) == 0)
    def _():
        own[...] = jnp.zeros_like(own)
        other[...] = jnp.zeros_like(other)
        sums[...] = jnp.zeros_like(sums)

    for h in range(ch // LANES):
        totals = [0.0] * 4
        for p in range(POOLED):
            lanes = slice(p * ch + h * LANES, p * ch + (h + 1) * LANES)
            rows = pl.ds(p, count, stride=PITCH)
            g0 = keep_in[:, lanes].astype(F32) + came_in[:, lanes].astype(F32)
            g1 = other_in[:, lanes].astype(F32)
            own[h, rows, :] = g0
            other[h, rows, :] = g1
            for s in range(2):
                value = pooled[s, :, lanes]
                totals[s] = totals[s] + g0 * value
                totals[2 + s] = totals[2 + s] + g1 * value
        for k in range(4):
            sums[k, :, h * LANES : (h + 1) * LANES] += totals[k]

    def image(n, carry):
        window = table[group[base + n]]
        rows = pl.ds(pl.multiple_of(n * PITCH, PITCH), PITCH)
        g0, g1 = (
            jnp.concatenate([hold[h, rows, :] for h in range(ch // LANES)], axis=1) for hold in (own, other)
        )
        highs, lows = [], []
        for s in range(2):
            grad = (first[s : s + 1, :] * g0 + first[2 + s : 3 + s, :] * g1) * (1.0 / 9.0)
            highs.append(grad.astype(BF16))
            lows.append((grad - highs[s].astype(F32)).astype(BF16))
        parts = jnp.concatenate(highs + lows, axis=0)
        spread = jnp.dot(window, parts, preferred_element_type=F32).astype(BF16)
        out[n] = spread[: 2 * places].reshape(places, 2, ch)
        return carry

    lax.fori_loop(0, count, image, 0, unroll=2)


def unpool(keep, came, other, pooled, row, images, group, table, first, places, at, count, before=()):
    feats = keep.shape[1]
    ch = first.shape[1]
    nb = IMAGE_BLOCK
    rows = pl.BlockSpec((nb, feats), lambda i, g: (row // nb + i, 0))
    grad, sums = pl.pallas_call(
        functools.partial(unpool_kernel, at),
        grid_spec=pltpu.PrefetchScalarGridSpec(
            num_scalar_prefetch=1,
            grid=(images // nb,),
            in_specs=[
                pl.BlockSpec(table.shape, lambda i, g: (0, 0, 0)),
                pl.BlockSpec((4, ch), lambda i, g: (0, 0)),
                rows,
                rows,
                rows,
                pl.BlockSpec((2, nb, feats), lambda i, g: (0, at // nb + i, 0)),
            ]
            + [pl.BlockSpec(memory_space=pl.ANY)] * len(before),
            out_specs=[
                pl.BlockSpec((nb, places, 2, ch), lambda i, g: (at // nb + i, 0, 0, 0)),
                pl.BlockSpec((4, nb, ch), lambda i, g: (0, 0, 0)),
            ],
            scratch_shapes=[pltpu.VMEM((ch // LANES, nb * PITCH, LANES), F32)] * 2,
        ),
        out_shape=[jax.ShapeDtypeStruct((count, places, 2, ch), BF16), jax.ShapeDtypeStruct((4, nb, ch), F32)],
        input_output_aliases={7: 0} if before else {},
        compiler_params=params(),
        cost_estimate=SMALL,
        name="unpool",
    )(group, table, first, keep, came, other, pooled, *before)
    return grad, sums


def store_kernel(chunk, chunks, x, own, came, *refs):
    out, stay, go, sems = refs[-4:]
    rows, width = came.shape

    def columns(at):
        return out.at[:, pl.ds(pl.multiple_of(at * width, width), width)]

    source = own.at[pl.ds(pl.multiple_of(x[0] * rows, rows), rows), :]
    read = pltpu.make_async_copy(source, stay, sems.at[0])
    read.start()
    go[...] = came[...].astype(F32)
    write = pltpu.make_async_copy(go, columns((1 - x[0]) * chunks + chunk), sems.at[1])
    write.start()
    read.wait()
    write_own = pltpu.make_async_copy(stay, columns(x[0] * chunks + chunk), sems.at[2])
    write_own.start()
    write.wait()
    write_own.wait()


def store(own, came, x, chunk, chunks, shape, before=()):
    anywhere = pl.BlockSpec(memory_space=pl.ANY)
    return pl.pallas_call(
        functools.partial(store_kernel, chunk, chunks),
        in_specs=[pl.BlockSpec(memory_space=pltpu.SMEM), anywhere, pl.BlockSpec(memory_space=pltpu.VMEM)]
        + [anywhere] * len(before),
        out_specs=anywhere,
        out_shape=jax.ShapeDtypeStruct(shape, F32),
        scratch_shapes=[pltpu.VMEM(came.shape, F32)] * 2 + [pltpu.SemaphoreType.DMA((3,))],
        input_output_aliases={3: 0} if before else {},
        compiler_params=params(),
        cost_estimate=SMALL,
        name="store",
    )(x, own, came, *before)


def place_rows_kernel(places, *refs):
    *parts, out, sem = refs
    height, width = parts[0].shape[0] // 4, parts[0].shape[1]
    chunks = len(parts) // 2
    x, y, core = places[0], places[1], places[2]
    copies = []
    for i, part in enumerate(parts):
        side, j = i // chunks, i % chunks
        col = (jnp.where(x == side, 0, chunks) + j) * width
        cols = pl.ds(pl.multiple_of(col, width), width)
        for b in range(4):
            row = (2 * ((b % 2) ^ y) + ((b // 2) ^ core)) * height
            target = out.at[pl.ds(pl.multiple_of(row, height), height), cols]
            copies.append(pltpu.make_async_copy(part.at[pl.ds(b * height, height), :], target, sem.at[i, b]))
            copies[-1].start()
    for copy in copies:
        copy.wait()


def place_rows(places, own, other):
    parts = own + other
    rows, width = parts[0].shape
    return pl.pallas_call(
        place_rows_kernel,
        in_specs=[pl.BlockSpec(memory_space=pltpu.SMEM)] + [pl.BlockSpec(memory_space=pltpu.VMEM)] * len(parts),
        out_specs=pl.BlockSpec(memory_space=pl.ANY),
        out_shape=jax.ShapeDtypeStruct((rows, width * len(parts)), BF16),
        scratch_shapes=[pltpu.SemaphoreType.DMA((len(parts), 4))],
        compiler_params=params(),
        cost_estimate=SMALL,
        name="place_rows",
    )(places, *parts)


def blend_kernel(counts, roles, *refs):
    hold, in_sems, out_sems = refs[-3:]
    blocks, outs = refs[: sum(counts)], refs[sum(counts) : -3]
    rows = hold.shape[1] // BLEND_STEPS
    outer = roles[0] == 1

    def span(i):
        return pl.ds(i * rows, rows)

    def bring(block, k, i):
        return pltpu.make_async_copy(block.at[span(i), :], hold.at[k, span(i), :], in_sems.at[k, i])

    def leave(k, out, i):
        return pltpu.make_async_copy(hold.at[k, span(i), :], out.at[span(i), :], out_sems.at[k, i])

    groups, at = [], 0
    for count in counts:
        groups.append(blocks[at : at + count])
        at += count
    slots = [sum(max(count - 1, 1) for count in counts[:g]) for g in range(len(counts))]
    for g, (first, *rest) in enumerate(groups):
        for i in range(BLEND_STEPS):

            @pl.when(outer)
            def _(first=first, g=g, i=i):
                bring(first, slots[g], i).start()

            @pl.when(jnp.logical_not(outer))
            def _(rest=rest, g=g, i=i):
                for k, block in enumerate(rest):
                    bring(block, slots[g] + k, i).start()

    for g, (first, *rest) in enumerate(groups):
        for i in range(BLEND_STEPS):
            bring(first, slots[g], i).wait()
            if len(rest) > 1:

                @pl.when(jnp.logical_not(outer))
                def _(rest=rest, g=g, i=i):
                    for k in range(1, len(rest)):
                        bring(rest[k], slots[g] + k, i).wait()
                    total = sum(hold[slots[g] + k, span(i), :].astype(F32) for k in range(len(rest)))
                    hold[slots[g], span(i), :] = total.astype(BF16)

            leave(slots[g], outs[g], i).start()
    for g in range(len(groups)):
        for i in range(BLEND_STEPS):
            leave(slots[g], outs[g], i).wait()


def blend(roles, groups):
    counts = [len(group) for group in groups]
    shape = groups[0][0].shape
    slots = sum(max(count - 1, 1) for count in counts)
    anywhere = pl.BlockSpec(memory_space=pl.ANY)
    return pl.pallas_call(
        functools.partial(blend_kernel, counts),
        in_specs=[pl.BlockSpec(memory_space=pltpu.SMEM)] + [anywhere] * sum(counts),
        out_specs=[anywhere] * len(groups),
        out_shape=[jax.ShapeDtypeStruct(shape, BF16)] * len(groups),
        scratch_shapes=[
            pltpu.VMEM((slots, *shape), BF16),
            pltpu.SemaphoreType.DMA((slots, BLEND_STEPS)),
            pltpu.SemaphoreType.DMA((slots, BLEND_STEPS)),
        ],
        compiler_params=params(),
        cost_estimate=SMALL,
        name="blend",
    )(roles, *[block for group in groups for block in group])


def tile_of(rows):
    return next(t for t in (1152, 768, 576, 512, 384, 256, 128) if rows % t == 0)


def fetch(outer, terms, rows, target, sem):
    def copy(term):
        return pltpu.make_async_copy(term.at[rows, :], target, sem)

    if len(terms) == 1:
        copy(terms[0]).start()
    else:
        pl.when(outer == 1)(lambda: copy(terms[0]).start())
        pl.when(outer == 0)(lambda: copy(terms[1]).start())


def chunk_kernel(layout, starts, cot_cols, roles, vectors, *refs):
    chunks, count = len(layout), len(layout[0])
    cots, refs = refs[:4], refs[4:]
    blocks = len(starts) // HALVES
    feats, refs = refs[: blocks * HALVES], refs[blocks * HALVES :]
    at = 0
    pieces = []
    for counts in layout:
        pieces.append([])
        for many in counts:
            pieces[-1].append(refs[at : at + many])
            at += many
    act_out, keep_out, send_out, sums_out = refs[at : at + 4]
    outs = [refs[at + 4 + i * count : at + 4 + (i + 1) * count] for i in range(chunks)]
    held, weight, total, dpre_out, k_own, k_other, high, low, in_sems, w_sems, cot_sems, out_sems = refs[-12:]
    steps, images, tile = held.shape
    per = steps // count
    units = total.shape[1] // chunks
    half, height = steps // HALVES, images // blocks

    def columns(i):
        return slice(i * units, (i + 1) * units)

    def begin(k):
        for s in range(count):

            @pl.when(k // per == s)
            def _(s=s):
                rows = pl.ds(pl.multiple_of((k - s * per) * tile, tile), tile)
                for i in range(chunks):
                    fetch(roles[0], pieces[i][s], rows, weight.at[k, :, columns(i)], w_sems.at[k])

        for h in range(HALVES):

            @pl.when(k // half == h)
            def _(h=h):
                cols = pl.ds(pl.multiple_of((k - h * half) * tile, tile), tile)
                for r in range(blocks):
                    at = r * HALVES + h
                    start = starts[at]
                    if start is None:
                        start = pl.multiple_of(roles[1] * height, height)
                    part = feats[at].at[pl.ds(start, height), cols]
                    rows = pl.ds(r * height, height)
                    pltpu.make_async_copy(part, held.at[k, rows, :], in_sems.at[k]).start()

    def arrive(target, sem):
        pltpu.make_async_copy(target, target, sem).wait()

    ahead = min(AHEAD, steps)
    for k in range(ahead):
        begin(jnp.int32(k))
    for tower, target in enumerate((k_own, k_other)):
        for r in range(blocks):
            core, x, y = r // 4, r // 2 % 2, r % 2
            source, col = cots[2 * tower + x], cot_cols[2 * tower + x]
            rows = pl.ds((2 * core + (y ^ tower)) * height, height)
            source = source.at[rows, pl.ds(col, total.shape[1])]
            target_rows = target.at[pl.ds(r * height, height), :]
            pltpu.make_async_copy(source, target_rows, cot_sems.at[tower]).start()
    total[...] = jnp.zeros_like(total)

    def forward_step(k, carry):
        pl.when(k + ahead < steps)(lambda: begin(k + ahead))
        arrive(held.at[k], in_sems.at[k])
        arrive(weight.at[k], w_sems.at[k])
        total[...] += jnp.dot(held[k], weight[k], preferred_element_type=F32)
        return carry

    lax.fori_loop(0, steps, forward_step, 0)
    arrive(k_own, cot_sems.at[0])
    arrive(k_other, cot_sems.at[1])

    bias, own_coef, other_coef = (vectors[i : i + 1, :] for i in range(3))
    c = 0.7978845608028654
    block = 32

    def rows_of(i, sums):
        rows = pl.ds(pl.multiple_of(i * block, block), block)
        x = total[rows, :] + bias
        x2 = x * x
        t = jnp.tanh(c * (x + 0.044715 * (x2 * x)))
        half = 0.5 * (1.0 + t)
        act = (x * half).astype(BF16)
        slope = half + (0.5 * c) * x * (1.0 - t * t) * (1.0 + (3.0 * 0.044715) * x2)
        k0 = k_own[rows, :].astype(F32)
        k1 = k_other[rows, :].astype(F32)
        dpre = ((own_coef * k0 + other_coef * k1) * slope).astype(BF16)
        act_out[rows, :] = act
        dpre_out[rows, :] = dpre
        actf = act.astype(F32)

        def fold(v):
            return jnp.sum(v.reshape(block // 8, 8, v.shape[1]), axis=0)

        return (
            sums[0] + fold(dpre.astype(F32)),
            sums[1] + fold(k0 * actf),
            sums[2] + fold(k1 * actf),
        )

    zero = jnp.zeros((8, total.shape[1]), F32)
    sums = lax.fori_loop(0, images // block, rows_of, (zero, zero, zero))
    for i in range(3):
        sums_out[i : i + 1, :] = jnp.sum(sums[i], axis=0, keepdims=True)
    keep_out[...] = dpre_out[: images // 2]
    send_out[...] = dpre_out[images // 2 :]

    def product(k):
        return lax.dot_general(
            held[k], dpre_out[...], (((0,), (0,)), ((), ())), preferred_element_type=F32
        )

    def last_steps(k, carry):
        made = product(k).astype(BF16)
        for i in range(chunks):
            low[k - per, i] = made[:, columns(i)]
        for s in range(1, count):

            @pl.when(k // per == s)
            def _(s=s):
                rows = pl.ds(pl.multiple_of((k - s * per) * tile, tile), tile)
                for i in range(chunks):
                    pltpu.make_async_copy(low.at[k - per, i], outs[i][s].at[rows, :], out_sems.at[k]).start()

        return carry

    def first_steps(k, carry):
        made = product(k)
        rows = pl.ds(pl.multiple_of(k * tile, tile), tile)
        for i in range(chunks):
            high[k, i] = made[:, columns(i)]
            pltpu.make_async_copy(high.at[k, i], outs[i][0].at[rows, :], out_sems.at[k]).start()
        return carry

    if count > 1:
        lax.fori_loop(per, steps, last_steps, 0)
    lax.fori_loop(0, per, first_steps, 0)
    for k in range(steps):
        arrive(high.at[k] if k < per else low.at[k - per], out_sems.at[k])


def chunk(roles, feats, pieces, vectors, cots):
    images = len(feats) * feats[-1][-1][0].shape[0]
    units = pieces[0][0][0].shape[1]
    width = units * len(pieces)
    depth = sum(part.shape[1] for part, _ in feats[0])
    starts = [start for block in feats for _, start in block]
    count = len(pieces[0])
    height = pieces[0][0][0].shape[0]
    tile = tile_of(height)
    steps, per = depth // tile, height // tile
    terms = [term for chunk in pieces for piece in chunk for term in piece]
    anywhere = pl.BlockSpec(memory_space=pl.ANY)
    vmem = pl.BlockSpec(memory_space=pltpu.VMEM)
    kinds = ([F32] + [BF16] * (count - 1)) * len(pieces)
    return pl.pallas_call(
        functools.partial(chunk_kernel, [[len(p) for p in chunk] for chunk in pieces], starts, [c for _, c in cots]),
        in_specs=[pl.BlockSpec(memory_space=pltpu.SMEM), vmem]
        + [anywhere] * (len(cots) + len(feats) * HALVES + len(terms)),
        out_specs=[vmem] * 4 + [anywhere] * len(kinds),
        out_shape=[
            jax.ShapeDtypeStruct((images, width), BF16),
            jax.ShapeDtypeStruct((images // 2, width), BF16),
            jax.ShapeDtypeStruct((images // 2, width), BF16),
            jax.ShapeDtypeStruct((8, width), F32),
        ]
        + [jax.ShapeDtypeStruct((height, units), kind) for kind in kinds],
        scratch_shapes=[
            pltpu.VMEM((steps, images, tile), BF16),
            pltpu.VMEM((steps, tile, width), BF16),
            pltpu.VMEM((images, width), F32),
            pltpu.VMEM((images, width), BF16),
            pltpu.VMEM((images, width), BF16),
            pltpu.VMEM((images, width), BF16),
            pltpu.VMEM((per, len(pieces), tile, units), F32),
            pltpu.VMEM((max(steps - per, 1), len(pieces), tile, units), BF16),
            pltpu.SemaphoreType.DMA((steps,)),
            pltpu.SemaphoreType.DMA((steps,)),
            pltpu.SemaphoreType.DMA((2,)),
            pltpu.SemaphoreType.DMA((steps,)),
        ],
        compiler_params=params(),
        cost_estimate=SMALL,
        name="chunk",
    )(roles, vectors, *[cot for cot, _ in cots], *[part for block in feats for part, _ in block], *terms)


def back_kernel(layout, firsts, blocks, roles, *refs):
    outs = refs[-10:-6]
    grad, weight, made, grad_sems, w_sems, out_sems = refs[-6:]
    sources, count = len(layout), len(layout[0])
    grads = refs[:sources]
    at = sources
    pieces = []
    for counts in layout:
        pieces.append([])
        for many in counts:
            pieces[-1].append(refs[at : at + many])
            at += many
    slots, tile, total = weight.shape
    units = total // sources
    steps = made.shape[0]
    per = steps // count
    share = made.shape[1] // len(outs)

    def columns(j):
        return slice(j * units, (j + 1) * units)

    def begin(k):
        slot = lax.rem(k, slots)
        for s in range(count):

            @pl.when(k // per == s)
            def _(s=s):
                rows = pl.ds(pl.multiple_of((k - s * per) * tile, tile), tile)
                for j in range(sources):
                    fetch(roles[0], pieces[j][s], rows, weight.at[slot, :, columns(j)], w_sems.at[slot])

    def arrive(target, sem):
        pltpu.make_async_copy(target, target, sem).wait()

    copies = []
    for j in range(sources):
        for i, block in enumerate(blocks):
            rows = grad.shape[0] // len(blocks)
            source = grads[j].at[pl.ds(firsts[j] + block * rows, rows), :]
            target = grad.at[pl.ds(i * rows, rows), columns(j)]
            copies.append(pltpu.make_async_copy(source, target, grad_sems.at[j, i]))
            copies[-1].start()
    ahead = min(slots - 1, steps)
    for k in range(ahead):
        begin(jnp.int32(k))
    for copy in copies:
        copy.wait()

    def step(k, carry):
        pl.when(k + ahead < steps)(lambda: begin(k + ahead))
        slot = lax.rem(k, slots)
        arrive(weight.at[slot], w_sems.at[slot])
        made[k] = lax.dot_general(
            grad[...], weight[slot], (((1,), (1,)), ((), ())), preferred_element_type=F32
        ).astype(BF16)
        cols = pl.ds(pl.multiple_of(k * tile, tile), tile)
        for i, out in enumerate(outs):
            source = made.at[k, pl.ds(i * share, share), :]
            pltpu.make_async_copy(source, out.at[:, cols], out_sems.at[k]).start()
        return carry

    lax.fori_loop(0, steps, step, 0)
    for k in range(steps):
        arrive(made.at[k], out_sems.at[k])


def back(roles, grads, pieces, blocks):
    units = grads[0][0].shape[1]
    images = min(grad.shape[0] for grad, _ in grads) // 4 * len(blocks)
    count = len(pieces[0])
    height = pieces[0][0][0].shape[0]
    depth = height * count
    tile = next(t for t in (768, 512, 384, 256, 128) if height % t == 0)
    steps = depth // tile
    total = units * len(grads)
    terms = [term for chunk in pieces for piece in chunk for term in piece]
    layout = [[len(piece) for piece in chunk] for chunk in pieces]
    anywhere = pl.BlockSpec(memory_space=pl.ANY)
    return pl.pallas_call(
        functools.partial(back_kernel, layout, [row for _, row in grads], blocks),
        in_specs=[pl.BlockSpec(memory_space=pltpu.SMEM)] + [anywhere] * (len(grads) + len(terms)),
        out_specs=[anywhere] * 4,
        out_shape=[jax.ShapeDtypeStruct((images // 4, depth), BF16)] * 4,
        scratch_shapes=[
            pltpu.VMEM((images, total), BF16),
            pltpu.VMEM((AHEAD + 1, tile, total), BF16),
            pltpu.VMEM((steps, images, tile), BF16),
            pltpu.SemaphoreType.DMA((len(grads), len(blocks))),
            pltpu.SemaphoreType.DMA((AHEAD + 1,)),
            pltpu.SemaphoreType.DMA((steps,)),
        ],
        compiler_params=params(),
        cost_estimate=SMALL,
        name="back",
    )(roles, *[grad for grad, _ in grads], *terms)


def either(flag, value, axis):
    return jnp.where(flag, jnp.flip(value, axis), value)


class Program:
    def __init__(self, convmaps, group, alpha1, weight, bias, alpha2, cotangent):
        self.order = Order()
        self.convmaps, self.group, self.weight = convmaps, group, weight
        self.count, _, self.places, self.channels = convmaps.shape
        batch_id = lax.axis_index("batch")
        tower_id = lax.axis_index("tower")
        self.x, self.z = batch_id % 2, batch_id // 2
        self.y, self.core = tower_id // 2, tower_id % 2
        self.depth, self.width = weight.shape
        self.units = self.width // 2
        self.n = self.units // (4 if is_line() else 2)
        self.chunks = self.units // self.n
        self.images = 8 * self.count
        self.mine, self.theirs = self.x * self.units, (1 - self.x) * self.units
        units = self.units
        second = lax.dynamic_slice_in_dim(alpha2, self.mine, units, 1)
        self.own_coef = lax.dynamic_index_in_dim(second, self.y, 0, keepdims=True).astype(F32)
        self.cross = lax.dynamic_index_in_dim(second, 1 - self.y, 0, keepdims=True)
        own_bias = lax.dynamic_slice_in_dim(bias, self.mine, units, 0)[None, :].astype(F32)
        self.own_bias = own_bias
        self.cotangent = cotangent
        places = jnp.arange(POOLED)
        if is_line():
            places = places.reshape(4, -1)[line_order(self.z)].reshape(-1)
        self.table = spread_table(places)
        inside, small = windows(places)
        self.pool_table = inside.astype(BF16)
        keep = jnp.stack([jnp.ones_like(small), small]).astype(F32) * (1.0 / 9.0)
        self.keep = jnp.broadcast_to(keep, (2, POOLED, self.channels))
        self.first = either(self.y == 1, alpha1.astype(F32), 0).reshape(4, self.channels)
        self.is_outer = (self.z == 0) | (self.z == 3)
        self.roles = jnp.stack([self.is_outer.astype(jnp.int32), 1 - self.core])
        self.cots = {}
        self.places_of = jnp.stack([self.x, self.y, self.core]).astype(jnp.int32)
        self.weight_grad = ()
        self.acts, self.grads, self.far_grads, self.sums = {}, {}, {}, {}
        self.stitched, self.crossed = {}, {}

    def then(self, value):
        return self.order.then(value)

    def did(self, value):
        return self.order.did(value)

    def keep_cross(self, came):
        cross_back = self.did(self.then(came)).astype(F32)
        zeros = jnp.zeros((5, self.units), F32)
        self.vectors = jnp.concatenate([self.own_bias, self.own_coef, cross_back, zeros])
        self.cross = self.cross.astype(F32)

    def load_cotangents(self):
        cot = self.then(self.cotangent).reshape(2, 2, self.count, self.width)
        cot = either(self.core == 1, either(self.y == 1, cot, 0), 1).swapaxes(0, 1).reshape(-1, self.width)
        self.cot_mine = self.did(lax.dynamic_slice_in_dim(cot, self.mine, self.units, 1))
        self.cot_theirs = lax.dynamic_slice_in_dim(cot, self.theirs, self.units, 1)

    def pool(self):
        return jnp.einsum("pq,nsqc->nspc", self.pool_table, self.convmaps, preferred_element_type=F32)

    def mix(self, summed):
        return mix(summed, self.group, self.keep, self.first)

    def cols(self, j):
        return slice(j * self.n, (j + 1) * self.n)

    def span(self, js):
        return slice(js[0] * self.n, (js[-1] + 1) * self.n)

    def weight_part(self, start, j, many=1):
        return lax.dynamic_slice(self.then(self.weight), (0, start + j * self.n), (self.depth, many * self.n))

    def swap_weight(self, j, many=1):
        return self.send(x_swap, self.weight_part(self.theirs, j, many))

    def slab_weight(self, j, came):
        a, b = self.weight_part(self.mine, j), self.then(came)
        return self.did(jnp.where(self.x == 0, jnp.concatenate([a, b]), jnp.concatenate([b, a])))

    def swap_cotangents(self, js):
        return self.send(x_swap, self.cot_theirs[:, self.span(js)])

    def cots_of(self, j):
        here, there = self.cots[j]
        first = (j - min(i for i in self.cots if self.cots[i][0] is here)) * self.n
        return [(self.cot_mine, j * self.n), (here, first), (self.cot_across, j * self.n), (there, first)]

    def send(self, move, value, *args):
        return move(self.did(self.then(value)), *args)

    def chunk(self, j, feats, pieces):
        act, keep, send, sums, *products = chunk(
            self.roles,
            feats,
            [pieces],
            self.then(self.vectors[:, self.cols(j)]),
            self.cots_of(j),
        )
        self.did(act)
        self.acts[j], self.grads[j], self.far_grads[j], self.sums[j] = act, keep, send, sums
        return products

    def stitch(self, j, came):
        cols = self.cols(j)
        other_act = jnp.flip(self.then(came).reshape(4, 2, self.count, self.n), 1).reshape(self.images, self.n)
        mix = self.own_coef[:, cols] * self.acts[j].astype(F32) + self.cross[:, cols] * other_act.astype(F32)
        mix = self.did(mix.astype(BF16)).reshape(2, 2, 2 * self.count, self.n)
        self.stitched[j] = mix[:, 0].reshape(-1, self.n)
        return mix[:, 1].reshape(-1, self.n)

    def leaving(self, slab):
        return lax.dynamic_slice_in_dim(slab, (1 - self.x) * self.depth, self.depth, 0).astype(BF16)

    def store(self, j, rows, came):
        shape = (self.depth, self.width)
        made = store(self.then(rows), came, self.places_of, j, self.chunks, shape, self.weight_grad)
        self.weight_grad = (self.did(made),)

    def activations(self):
        own, other = ([parts[j] for j in range(self.chunks)] for parts in (self.stitched, self.crossed))
        return place_rows(self.places_of, [self.then(own[0])] + own[1:], other)

    def unit_sums(self, *parts):
        return jnp.concatenate([part[:3] for part in parts or self.sums.values()], axis=1)

    def small_grads(self, sums):
        mine, far = sums[:3], sums[3:6]
        wide = jnp.where(
            self.x == 0, jnp.concatenate([mine, far], -1), jnp.concatenate([far, mine], -1)
        )
        return wide[0], either(self.y == 1, wide[1:3], 0)

    def back(self, y, came_grads, pieces, came_pieces):
        chunks = range(self.chunks)
        grads = [(self.grads[j], 0) for j in chunks] + list(came_grads)
        grads[0] = (self.then(grads[0][0]), 0)
        parts = back(
            self.roles,
            grads,
            [pieces[j] for j in chunks] + [came_pieces[j] for j in chunks],
            [y, 2 + y],
        )
        self.did(parts[0])
        return parts[:2], parts[2:]

    def add(self, keep, came):
        return self.did((keep.astype(F32) + self.then(came).astype(F32)).astype(BF16))

    def by_tower(self, partial):
        return either(self.y == 1, partial.reshape(2, 2, self.channels), 0)

    def unpool(self, i, keep, came, other, pooled, before=(), part=0, parts=1):
        images = keep.shape[0] // parts
        grad, sums = unpool(
            self.then(keep),
            came,
            other,
            pooled,
            part * images,
            images,
            self.group,
            self.table,
            self.first,
            self.places,
            i * keep.shape[0] + part * images,
            self.count,
            before,
        )
        return (self.did(grad),), sums


def line_program(p):
    then, did = p.then, p.did
    came, blocks, near, inner, outer, first_out, last_out = {}, {}, {}, {}, {}, {}, {}
    total, into, crossed, middle, final, slab_came = {}, {}, {}, {}, {}, {}
    from_own, swapped = {}, {}

    def send(kind, value):
        return p.send(line, value, kind)

    def arrive(value):
        return did(then(value))

    def block(j):
        blocks[j] = p.slab_weight(j, came[j])

    def pieces(j):
        beside = (near[j],) if j < 2 else (from_own[j], swapped[j])
        return [(blocks[j],), beside, (first_out[j], inner[j]), (last_out[j], outer[j])]

    def part(j, s):
        return total[j][s]

    def payload(inward, outward):
        return did(jnp.where(p.is_outer, then(inward), outward))

    def ends(value):
        return send("near", value)

    def inward(j, s):
        return send("inward", then(part(j, s)))

    def plus(j, s, value):
        return (part(j, s).astype(F32) + then(value).astype(F32)).astype(BF16)

    def edge(j):
        return jnp.where(
            p.is_outer, then(final[j]).astype(F32), into[j, 1].astype(F32) + middle[j].astype(F32)
        )

    def blended(*groups):
        (first, *rest), *others = groups
        made = blend(p.roles, [(then(first), *rest)] + others)
        did(made[0])
        return made

    def pick(a, b):
        return did(jnp.where(p.is_outer, then(a), b))

    def core_swap(j, s):
        came_pieces[j, s] = p.send(c_swap, picked[j, s])

    def core_came(j, s):
        came_pieces[j, s] = arrive(came_pieces[j, s])

    picked, came_pieces = {}, {}

    def far_end(j):
        return plus(j, 3, into[j, 3])

    came[0] = p.swap_weight(0)
    came[1] = p.swap_weight(1)
    cross_came = p.send(y_swap, p.cross)
    p.load_cotangents()
    p.keep_cross(cross_came)
    p.table = did(then(p.table))
    came[0] = arrive(came[0])
    block(0)
    near[0] = ends(blocks[0])
    inner[0] = send("middle", blocks[0])
    came_pair = p.swap_weight(2, 2)
    p.cot_across = p.send(y_swap, p.cot_mine)
    p.pool_table = then(p.pool_table)
    summed = did(p.pool())
    came[1] = arrive(came[1])
    cot_came = p.swap_cotangents([0, 1])
    block(1)
    near[0] = arrive(near[0])
    near[1] = ends(blocks[1])
    inner[0] = arrive(inner[0])
    inner[1] = send("middle", blocks[1])
    kept_a, kept_b, sent_a, sent_b, pooled = p.mix(then(summed))
    did(kept_a)
    came_pair = arrive(came_pair)
    p.cot_across = arrive(p.cot_across)
    cot_came = arrive(cot_came)
    x_a = p.send(x_swap, kept_a)
    y_a = p.send(y_swap, sent_a)
    c_kept_a = p.send(c_swap, kept_a)
    came[2], came[3] = came_pair[:, : p.n], came_pair[:, p.n :]
    block(2)
    near[1] = arrive(near[1])
    first_out[0] = send("outward", inner[0])
    inner[1] = arrive(inner[1])
    outer[0] = send("middle", near[0])
    x_a = arrive(x_a)
    x_b = p.send(x_swap, kept_b)
    y_a = arrive(y_a)
    y_b = p.send(y_swap, sent_b)
    c_kept_a = arrive(c_kept_a)
    c_kept_b = p.send(c_swap, kept_b)
    block(3)
    first_out[0] = arrive(first_out[0])
    first_out[1] = send("outward", inner[1])
    outer[0] = arrive(outer[0])
    outer[1] = send("middle", near[1])
    x_b = arrive(x_b)
    x_y_a = p.send(x_swap, y_a)
    y_b = arrive(y_b)
    cot_crossed = p.send(y_swap, cot_came)
    c_kept_b = arrive(c_kept_b)
    c_x_a = p.send(c_swap, x_a)
    value = payload(blocks[2], outer[0])
    first_out[1] = arrive(first_out[1])
    swapped[2] = last_out[0] = ends(value)
    outer[1] = arrive(outer[1])
    inner[2] = send("middle", blocks[2])
    x_y_a = arrive(x_y_a)
    x_y_b = p.send(x_swap, y_b)
    p.cots[0] = p.cots[1] = (cot_came, arrive(cot_crossed))
    c_x_a = arrive(c_x_a)
    c_y_a = p.send(c_swap, y_a)
    c_x_b = p.send(c_swap, x_b)
    value = payload(blocks[3], outer[1])
    for j in range(4):
        picked[j, 0] = blocks[j]
    picked[0, 1], picked[1, 1] = near[0], near[1]
    swapped[2] = last_out[0] = arrive(swapped[2])
    swapped[3] = last_out[1] = ends(value)
    inner[2] = arrive(inner[2])
    outer[2] = send("middle", swapped[2])
    x_y_b = arrive(x_y_b)
    c_y_a = arrive(c_y_a)
    c_x_b = arrive(c_x_b)
    c_y_b = p.send(c_swap, y_b)
    c_x_y_a = p.send(c_swap, x_y_a)
    c_x_y_b = p.send(c_swap, x_y_b)
    swapped[3] = last_out[1] = arrive(swapped[3])
    from_own[2] = send("outward", blocks[2])
    p.vectors = did(then(p.vectors))
    c_y_b = arrive(c_y_b)
    c_x_y_a = arrive(c_x_y_a)
    c_x_y_b = arrive(c_x_y_b)
    core_swap(0, 0)
    core_swap(0, 1)
    cot_came = p.swap_cotangents([2, 3])
    feats = [
        [(kept_a, 0), (kept_b, 0)],
        [(y_a, 0), (y_b, 0)],
        [(x_a, 0), (x_b, 0)],
        [(x_y_a, 0), (x_y_b, 0)],
        [(c_kept_a, 0), (c_kept_b, 0)],
        [(c_y_a, 0), (c_y_b, 0)],
        [(c_x_a, 0), (c_x_b, 0)],
        [(c_x_y_a, 0), (c_x_y_b, 0)],
    ]
    total[0] = p.chunk(0, feats, pieces(0))
    outer[2] = arrive(outer[2])
    value = payload(part(0, 3), inner[2])
    from_own[2] = arrive(from_own[2])
    into[0, 3] = first_out[2] = ends(value)
    core_came(0, 0)
    core_came(0, 1)
    cot_came = arrive(cot_came)
    inner[3] = send("middle", blocks[3])
    act_came = p.send(y_swap, p.acts[0])
    core_swap(1, 0)
    core_swap(1, 1)
    total[1] = p.chunk(1, feats, pieces(1))
    value = payload(part(0, 2), outer[2])
    into[0, 3] = first_out[2] = arrive(into[0, 3])
    into[0, 2] = last_out[2] = ends(value)
    far0 = did(far_end(0))
    inner[3] = arrive(inner[3])
    outer[3] = send("middle", swapped[3])
    cot_crossed = p.send(y_swap, cot_came)
    act_came = arrive(act_came)
    core_came(1, 0)
    core_came(1, 1)
    core_swap(2, 0)
    core_swap(3, 0)
    picked[0, 2], picked[1, 2], picked[0, 3], picked[1, 3], picked[2, 1], picked[2, 2], value = blended(
        (first_out[0], inner[0]),
        (first_out[1], inner[1]),
        (last_out[0], outer[0]),
        (last_out[1], outer[1]),
        (from_own[2], swapped[2]),
        (first_out[2], inner[2]),
        (part(0, 1), blocks[3]),
    )
    act_mixes = [p.stitch(0, act_came)]
    cot_crossed = arrive(cot_crossed)
    into[0, 2] = last_out[2] = arrive(into[0, 2])
    into[0, 1] = from_own[3] = ends(value)
    p.cots[2] = p.cots[3] = (cot_came, cot_crossed)
    core_came(2, 0)
    core_came(3, 0)
    core_swap(0, 2)
    core_swap(1, 2)
    core_swap(2, 1)
    total[2] = p.chunk(2, feats, pieces(2))
    outer[3] = arrive(outer[3])
    [value] = blended((part(1, 3), inner[3]))
    into[0, 1] = from_own[3] = arrive(into[0, 1])
    into[1, 3] = first_out[3] = ends(value)
    rest = did(plus(0, 2, into[0, 2]))
    crossed[0] = send("middle", far0)
    core_came(0, 2)
    core_came(1, 2)
    core_came(2, 1)
    acts_came = p.send(y_swap, jnp.concatenate([then(p.acts[1]), p.acts[2]], axis=1))
    core_swap(0, 3)
    core_swap(1, 3)
    value, picked[3, 1], picked[2, 3] = blended(
        (part(1, 2), outer[3]), (from_own[3], swapped[3]), (last_out[2], outer[2])
    )
    into[1, 3] = first_out[3] = arrive(into[1, 3])
    into[1, 2] = last_out[3] = ends(value)
    far1 = did(far_end(1))
    crossed[0] = arrive(crossed[0])
    middle[0] = send("middle", rest)
    acts_came = arrive(acts_came)
    core_came(0, 3)
    core_came(1, 3)
    core_swap(2, 2)
    core_swap(3, 1)
    core_swap(2, 3)
    value, picked[3, 2] = blended((part(1, 1), part(0, 1), crossed[0]), (first_out[3], inner[3]))
    far = did(jnp.concatenate([then(p.far_grads[0]), p.far_grads[1], p.far_grads[2]]))
    for j in (1, 2):
        act_mixes.append(p.stitch(j, acts_came[:, (j - 1) * p.n : j * p.n]))
    act_mixes = did(jnp.concatenate([then(act_mixes[0]), *act_mixes[1:]]))
    into[1, 2] = last_out[3] = arrive(into[1, 2])
    into[1, 1] = final[0] = ends(value)
    sums = did(p.unit_sums(then(p.sums[0]), p.sums[1], p.sums[2]))
    core_came(2, 2)
    core_came(3, 1)
    core_came(2, 3)
    core_swap(3, 2)
    came_outer = p.send(c_swap, outer[3])
    mixes_came = p.send(x_swap, act_mixes)
    total[3] = p.chunk(3, feats, pieces(3))
    middle[0] = arrive(middle[0])
    into[1, 1] = final[0] = arrive(into[1, 1])
    into[2, 3] = inward(2, 3)
    core_came(3, 2)
    came_outer = arrive(came_outer)
    mixes_came = arrive(mixes_came)
    far = p.send(c_swap, far)
    came_last = p.send(c_swap, last_out[3])
    far3 = p.send(c_swap, p.far_grads[3])
    crossed[1] = send("middle", far1)
    rows = {0: did(then(part(0, 0)) + edge(0))}
    far = arrive(far)
    slab_came[0] = p.send(x_swap, p.leaving(rows[0]))
    came_last = arrive(came_last)
    far3 = arrive(far3)
    act_came = p.send(y_swap, p.acts[3])
    third = far.shape[0] // 3
    came_grads = [(far, 0), (far, third), (far, 2 * third), (far3, 0)]
    picked[3, 3], came_pieces[3, 3] = (last_out[3], outer[3]), (came_last, came_outer)
    own_pieces, far_pieces = (
        [[terms if isinstance(terms := kind[j, s], tuple) else (terms,) for s in range(4)] for j in range(4)]
        for kind in (picked, came_pieces)
    )
    keep_far, leave_far = p.back(1, came_grads, own_pieces, far_pieces)
    came_far, came_x, own_y = {}, {}, {}
    into[2, 3] = arrive(into[2, 3])
    into[2, 2] = inward(2, 2)
    crossed[1] = arrive(crossed[1])
    slab_came[0] = arrive(slab_came[0])
    act_came = arrive(act_came)
    came_far[0] = p.send(x_swap, leave_far[0])
    [rest] = blended((part(1, 2), part(1, 2), into[1, 2]))
    middle[1] = send("middle", rest)
    keep, leave = p.back(0, came_grads, own_pieces, far_pieces)
    into[2, 2] = arrive(into[2, 2])
    into[3, 3] = inward(3, 3)
    [far2] = blended((part(2, 3), part(2, 3), into[2, 3]))
    middle[1] = arrive(middle[1])
    crossed[2] = send("middle", far2)
    came_far[0] = arrive(came_far[0])
    came_x[0] = p.send(x_swap, leave[0])
    own_y[0] = p.send(y_swap, p.add(keep_far[0], came_far[0]))
    value, own2 = blended((part(3, 2), part(1, 1), crossed[1]), (part(2, 2), part(2, 2), into[2, 2]))
    sums = jnp.concatenate([sums, p.unit_sums(p.sums[3])], axis=1)
    act_mix = p.stitch(3, act_came)
    for j in range(3):
        p.crossed[j] = did(then(mixes_came)[j * p.n * 2 : (j + 1) * p.n * 2])
    p.store(0, rows[0], slab_came[0])
    into[3, 3] = arrive(into[3, 3])
    into[3, 2] = final[1] = ends(value)
    rest = did(far_end(3))
    came_x[0] = arrive(came_x[0])
    came_far[1] = p.send(x_swap, leave_far[1])
    crossed[2] = arrive(crossed[2])
    crossed[3] = send("middle", rest)
    own_y[0] = arrive(own_y[0])
    [value] = blended((part(2, 1), part(2, 1), crossed[2]))
    grad, partial_a = p.unpool(0, keep[0], came_x[0], own_y[0], pooled, (), 0, 2)
    into[3, 2] = final[1] = arrive(into[3, 2])
    into[2, 1] = final[2] = ends(value)
    last = did(plus(3, 2, into[3, 2]))
    came_far[1] = arrive(came_far[1])
    came_x[1] = p.send(x_swap, leave[1])
    crossed[3] = arrive(crossed[3])
    middle[2] = send("middle", own2)
    own_y[1] = p.send(y_swap, p.add(keep_far[1], came_far[1]))
    p.crossed[3] = p.send(x_swap, act_mix)
    [value] = blended((part(3, 1), part(3, 1), crossed[3]))
    grad, partial_b = p.unpool(0, keep[0], came_x[0], own_y[0], pooled, grad, 1, 2)
    into[2, 1] = final[2] = arrive(into[2, 1])
    into[3, 1] = final[3] = ends(value)
    came_x[1] = arrive(came_x[1])
    middle[2] = arrive(middle[2])
    middle[3] = send("middle", last)
    rows[1] = did(then(part(1, 0)) + edge(1))
    slab_came[1] = p.send(x_swap, p.leaving(rows[1]))
    own_y[1] = arrive(own_y[1])
    p.crossed[3] = arrive(p.crossed[3])
    rows[2] = did(part(2, 0) + edge(2))
    slab_came[2] = p.send(x_swap, p.leaving(rows[2]))
    [grad], partial = p.unpool(1, keep[1], came_x[1], own_y[1], pooled, grad)
    into[3, 1] = final[3] = arrive(into[3, 1])
    middle[3] = arrive(middle[3])
    partial = jnp.sum(then(partial_a) + partial_b + partial, axis=1)
    partial = did(p.by_tower(partial).reshape(1, -1))
    partial_came = p.send(c_swap, partial)
    slab_came[1] = arrive(slab_came[1])
    rows[3] = did(part(3, 0) + edge(3))
    slab_came[3] = p.send(x_swap, p.leaving(rows[3]))
    partial = did(partial + then(partial_came))
    second_came = p.send(y_swap, jnp.concatenate([sums[2:], partial]))
    p.store(1, rows[1], slab_came[1])
    second_came = arrive(second_came)
    sums = did(jnp.concatenate([sums[:2], second_came[:1], partial + second_came[1:]]))
    sums_came = p.send(flipped, sums, "batch", 2)
    slab_came[2] = arrive(slab_came[2])
    p.store(2, rows[2], slab_came[2])
    sums = did(sums + then(sums_came))
    sums_came = p.send(flipped, sums, "batch", 4)
    activations = did(p.activations())
    sums = did(sums + then(sums_came))
    sums_came = p.send(x_swap, sums)
    slab_came[3] = arrive(slab_came[3])
    p.store(3, rows[3], slab_came[3])
    sums_came = then(sums_came)
    bias_grad, alpha2_grad = p.small_grads(jnp.concatenate([sums[:3], sums_came[:3]]))
    alpha1_grad = (sums[3] + sums_came[3]).reshape(2, 2, p.channels)
    input_grad = jnp.swapaxes(grad, 1, 2)
    return (activations, input_grad, p.weight_grad[0], bias_grad, alpha1_grad, alpha2_grad)


def plain_program(p):
    groups = slab_groups()
    p.keep_cross(p.send(y_swap, p.cross))
    p.load_cotangents()
    p.cot_across = p.send(y_swap, p.cot_mine)
    *features, pooled = p.mix(p.pool())
    feats = [features[:HALVES], [y_swap(part) for part in features[HALVES:]]]
    feats += [[x_swap(part) for part in block] for block in feats]
    feats += [[c_swap(part) for part in block] for block in feats]
    feats = [[(part, 0) for part in block] for block in feats]
    chunks = []
    for j in range(p.chunks):
        came = p.swap_cotangents([j])
        p.cots[j] = (came, p.send(y_swap, came))
        block = p.slab_weight(j, p.swap_weight(j))
        rows = lax.all_gather(block, "batch", axis=0, tiled=True, axis_index_groups=groups)
        chunks.append([(rows,)])
        [total] = p.chunk(j, feats, chunks[j])
        slab = lax.psum_scatter(total, "batch", scatter_dimension=0, tiled=True, axis_index_groups=groups)
        p.store(j, slab, p.send(x_swap, p.leaving(slab)))
        p.crossed[j] = p.send(x_swap, p.stitch(j, p.send(y_swap, p.acts[j])))
    sums = lax.psum(p.unit_sums(), "batch", axis_index_groups=groups)
    far = x_swap(sums)
    second = y_swap(jnp.concatenate([sums[2:], far[2:]]))
    bias_grad, alpha2_grad = p.small_grads(
        jnp.concatenate([sums[:2], second[:1], far[:2], second[1:]])
    )
    own_pieces = chunks
    far = [(c_swap(p.far_grads[j]), 0) for j in range(p.chunks)]
    far_pieces = [[(c_swap(term),) for [term] in chunk] for chunk in own_pieces]
    keep, leave = p.back(0, far, own_pieces, far_pieces)
    keep_far, leave_far = p.back(1, far, own_pieces, far_pieces)
    partial, grad = 0.0, ()
    for i in range(2):
        other = y_swap(p.add(keep_far[i], x_swap(leave_far[i])))
        came = x_swap(leave[i])
        grad, sums = p.unpool(i, keep[i], came, other, pooled, grad)
        partial = partial + jnp.sum(sums, axis=1)
    alpha1_grad = lax.psum(p.by_tower(partial), ("batch", "tower"))
    input_grad = jnp.swapaxes(grad[0], 1, 2)
    return (p.activations(), input_grad, p.weight_grad[0], bias_grad, alpha1_grad, alpha2_grad)


def shards(*args):
    return (line_program if is_line() else plain_program)(Program(*args))


def solution(mesh):
    in_specs = (
        P(("batch", "tower"), None, None, None),
        P(("batch", "tower")),
        P(),
        P("batch", "tower"),
        P("tower"),
        P(None, "tower"),
        P("batch", "tower"),
    )
    out_specs = (
        P("batch", "tower"),
        P(("batch", "tower"), None, None, None),
        P("batch", "tower"),
        P("tower"),
        P(),
        P(None, "tower"),
    )
    return jax.shard_map(shards, mesh=mesh, in_specs=in_specs, out_specs=out_specs, check_vma=False)
```
